32 devices in a mesh: row: 8 (over y, x, core), col: 4 (over z).
Axes of the slice: x: 2, y: 2, z: 4, core: 2. Of those that a mesh axis runs over, the one named last changes fastest.
Arguments:
- features: bfloat16 [8192, 1024], P(('row', 'col')), may hold values from -6 to 6
- weight: bfloat16 [1024, 512], replicated, may hold values from -0.1875 to 0.1875
- source_norm: float32 [8192], P(('row', 'col')), may hold values from 0.01 to 0.1
- target_norm: float32 [8192], P(('row', 'col')), may hold values from 0.3 to 3
- tile_weights: bfloat16 [32, 64, 128, 128], P(('row', 'col')), may hold values from 0 to 1
- tile_source: int32 [32, 64], P(('row', 'col')), may hold values from 0 to 7
- tile_target: int32 [32, 64], P(('row', 'col')), may hold values from 0 to 15, as said below
- tile_count: int32 [32], P(('row', 'col')), may hold values from 1 to 64, as said below
- mirror_tile: int32 [32, 16], P(('row', 'col')), may hold values from 0 to 2, as said below
Outputs:
- activated: bfloat16 [8192, 512], P(('row', 'col'))
The draws below stay inside these ranges and needn't reach their ends.
Inputs may be any that keep to these rules, and one draw needn't show every extreme that they name: `mirror_tile`: the value 2 marks an empty slot; slots k * 2 to k * 2 + 1 hold node tiles of grid row k. In every draw the slots of some grid row are filled on every device. `tile_target`: every slot named holds a node tile of the same device's mirror_tile row, not 2. `tile_count`: some device uses all 64 slots in every draw; counts are uneven.
All inputs are finite; a program needn't handle non-finite values.
Results may differ from the reference program's by a relative error of at most 0.015.
Values may be sent and summed in bfloat16 or wider, within the bound.
No kernel may reach another device: no remote copies, remote signals or barrier semaphores. Data moves between devices by JAX's collectives and lax.ppermute only.
A program may use at most 128 MiB of HBM per device.

```python
import math
import jax
import jax.numpy as jnp
from jax import lax

F = 1024
H = 512
TILE = 128
VB = 2
TMAX = 64
CAP = 2
BLOCKS = 32
NODES = 8192
SLOTS = 16
SRC_TILES = 8
N_COL = 4


def mirror_layout(key):
    key_fill = jax.random.fold_in(key, 101)
    key_full = jax.random.fold_in(key, 102)
    key_label = jax.random.fold_in(key, 103)
    owners = SLOTS // CAP
    filled = jax.random.randint(key_fill, (BLOCKS, owners), 0, CAP + 1)
    chosen = jax.random.randint(key_full, (), 0, owners)
    filled = jnp.where(jnp.arange(owners)[None, :] == chosen, CAP, filled)
    valid = jnp.arange(CAP)[None, None, :] < filled[:, :, None]
    labels = jax.random.randint(key_label, (BLOCKS, owners, CAP), 0, VB)
    labels = jnp.where(valid, labels, VB)
    return labels.reshape(BLOCKS, SLOTS).astype(jnp.int32)


def draw_mirror_tile(key, part):
    labels = mirror_layout(key)
    return labels


def draw_tile_target(key, part):
    labels = mirror_layout(key)
    key = jax.random.fold_in(key, 2)
    key_score = jax.random.fold_in(key, 21)
    key_pick = jax.random.fold_in(key, 22)
    valid = labels < VB
    scores = jax.random.randint(key_score, (BLOCKS, SLOTS), 0, 2 ** 20) + jnp.where(valid, 0, 2 ** 21)
    ordered = jnp.argsort(scores, axis=1, stable=True).astype(jnp.int32)
    live = jnp.sum(valid.astype(jnp.int32), axis=1)
    picks = jax.random.randint(key_pick, (BLOCKS, TMAX), 0, live[:, None])
    return jnp.take_along_axis(ordered, picks, axis=1).astype(jnp.int32)


def draw_tile_count(key, part):
    key = jax.random.fold_in(key, 3)
    key_base = jax.random.fold_in(key, 31)
    key_heavy = jax.random.fold_in(key, 32)
    base = jax.random.randint(key_base, (BLOCKS,), 0, TMAX + 1)
    counts = jnp.maximum(1, base * base // TMAX)
    heavy = jax.random.randint(key_heavy, (), 0, BLOCKS)
    counts = jnp.where(jnp.arange(BLOCKS) == heavy, TMAX, counts)
    return counts.astype(jnp.int32)


def set_ends(array, rng, smallest, top_value):
    dims = array.shape
    spot = [jax.random.randint(jax.random.fold_in(rng, axis), (), 0, dims[axis]) for axis in range(len(dims))]
    array = array.at[tuple(spot)].set(smallest)
    longest = dims.index(max(dims))
    spot[longest] = (spot[longest] + 1) % dims[longest]
    return array.at[tuple(spot)].set(top_value)


def block_scale(rng, shape, split, low, high):
    loudness, own = 1.0, jax.random.fold_in(rng, 6)
    for position, parts in split:
        steps = jnp.exp(jax.random.uniform(jax.random.fold_in(own, position), (parts,), jnp.float32, low / len(split), high / len(split)))
        loudness = loudness * jnp.repeat(steps, shape[position] // parts).reshape([-1 if axis == position else 1 for axis in range(len(shape))])
    return loudness


def noise(rng, dims, deviation, reach, cuts=(), kind=jnp.bfloat16):
    array = deviation * jax.random.normal(rng, dims, jnp.float32)
    if cuts:
        array = array * block_scale(rng, dims, cuts, -0.22, 0.18)
    return jnp.clip(array, -reach, reach).astype(kind)


def setup_inputs(seed: int = 0) -> dict:
    seeds = jax.random.split(jax.random.key(seed), 10)
    return {
        "features": noise(seeds[0], (NODES, F), 1.0, 6.0, ((0, 32),)),
        "weight": noise(seeds[1], (F, H), F ** -0.5, 0.1875),
        "source_norm": jnp.clip(jnp.exp(math.log(0.1) - 2.3025851 * jax.random.uniform(seeds[2], (NODES,), jnp.float32) ** block_scale(seeds[2], (NODES,), ((0, 32),), -0.2, 0.2)), 0.01, 0.1),
        "target_norm": jnp.clip(jnp.exp(math.log(3.0) - 2.3025851 * jax.random.uniform(seeds[3], (NODES,), jnp.float32) ** block_scale(seeds[3], (NODES,), ((0, 32),), -0.2, 0.2)), 0.3, 3.0),
        "tile_weights": jnp.clip(1.0 * jax.random.uniform(seeds[4], (BLOCKS, TMAX, TILE, TILE), jnp.float32) ** block_scale(seeds[4], (BLOCKS, TMAX, TILE, TILE), ((0, 32),), -0.2, 0.2), 0.0, 1.0).astype(jnp.bfloat16),
        "tile_source": set_ends(jax.random.randint(seeds[5], (BLOCKS, TMAX), 0, SRC_TILES), jax.random.fold_in(seeds[5], 1), 0, SRC_TILES - 1).astype(jnp.int32),
        "tile_target": draw_tile_target(jax.random.fold_in(seeds[9], 71), 0),
        "tile_count": draw_tile_count(jax.random.fold_in(seeds[9], 71), 0),
        "mirror_tile": draw_mirror_tile(jax.random.fold_in(seeds[9], 71), 0),
    }


def reference(features, weight, source_norm, target_norm, tile_weights, tile_source, tile_target, tile_count, mirror_tile):
    projected = jnp.dot(features, weight, preferred_element_type=jnp.float32)
    scaled = (source_norm[:, None] * projected).astype(jnp.bfloat16)
    scaled_tiles = scaled.reshape(NODES // TILE, TILE, H)
    slot_range = jnp.arange(TMAX, dtype=jnp.int32)
    owner_row = jnp.arange(SLOTS, dtype=jnp.int32) // CAP

    def one_device(carry, device):
        grid_row = device // N_COL
        grid_col = device % N_COL
        tiles = tile_weights[device].astype(jnp.float32)
        blocks = scaled_tiles[grid_row * SRC_TILES + tile_source[device]].astype(jnp.float32)
        live = (slot_range < tile_count[device]).astype(jnp.float32)
        product = jnp.einsum("tij,tjk->tik", tiles, blocks) * live[:, None, None]
        partial_value = jax.ops.segment_sum(product, tile_target[device], num_segments=SLOTS)
        partial_value = lax.optimization_barrier(partial_value.astype(jnp.bfloat16)).astype(jnp.float32)
        labels = mirror_tile[device]
        valid = (labels < VB).astype(jnp.float32)
        target = (owner_row * N_COL + grid_col) * VB + jnp.minimum(labels, VB - 1)
        carry = carry.at[target].add(partial_value * valid[:, None, None])
        return carry, None

    start = jnp.zeros((NODES // TILE, TILE, H), jnp.float32)
    summed, _ = lax.scan(one_device, start, jnp.arange(BLOCKS, dtype=jnp.int32))
    gathered = summed.reshape(NODES, H) + projected
    return jnp.maximum(target_norm[:, None] * gathered, 0.0).astype(jnp.bfloat16)
```

```python
import functools

import jax
import jax.numpy as jnp
from jax import lax
from jax.experimental import pallas as pl
from jax.experimental.pallas import tpu as pltpu
from jax.sharding import PartitionSpec as P

DENSE_ELEMENTS = 4 * 1024 * 1024
CHUNKS = 2
WEIGHTS = ((20, 20), (0, 20))
MIB = 1024 * 1024
SMEM = pl.BlockSpec(memory_space=pltpu.SMEM)
VMEM = pl.BlockSpec(memory_space=pltpu.VMEM)
HBM = pl.BlockSpec(memory_space=pltpu.HBM)


def params(mib):
    return pltpu.CompilerParams(vmem_limit_bytes=int(mib * MIB))


def cost(flops, moved):
    return pl.CostEstimate(flops=flops, bytes_accessed=moved, transcendentals=0)


def in_hbm(*values):
    return [pltpu.with_memory_space_constraint(value, pltpu.HBM) for value in values]


def rows_to_lanes(row, lanes):
    return jnp.broadcast_to(row, (lanes, row.shape[1])).T


def project_kernel(features_hbm, weight_hbm, norm_hbm, projected, *refs):
    *scaled, features, weight, norm, sems = refs
    copies = [
        pltpu.make_async_copy(source, target, sems.at[k])
        for k, (source, target) in enumerate(
            [(weight_hbm, weight), (features_hbm, features), (norm_hbm, norm)]
        )
    ]
    for copy in copies:
        copy.start()
    for copy in copies:
        copy.wait()
    lanes = norm.shape[1]
    value = jnp.dot(features[...], weight[...], preferred_element_type=jnp.float32)
    projected[...] = value
    width = scaled[0].shape[1]
    for part in range(norm.shape[0]):
        factor = rows_to_lanes(norm[part : part + 1, :], lanes)
        for column in range(0, value.shape[1], lanes):
            piece = value[part * lanes : (part + 1) * lanes, column : column + lanes]
            target = scaled[column // width]
            start = column % width
            target[part * lanes : (part + 1) * lanes, start : start + lanes] = (
                factor * piece
            ).astype(target.dtype)


def project(features, weight, source_norm, chunks):
    rows, depth = features.shape
    hidden = weight.shape[1]
    norm = source_norm.reshape(-1, 128)
    return pl.pallas_call(
        project_kernel,
        out_shape=[jax.ShapeDtypeStruct((rows, hidden), jnp.float32)]
        + [jax.ShapeDtypeStruct((rows, hidden // chunks), jnp.bfloat16)] * chunks,
        in_specs=[HBM] * 3,
        out_specs=[VMEM] * (1 + chunks),
        scratch_shapes=[
            pltpu.VMEM(features.shape, features.dtype),
            pltpu.VMEM(weight.shape, weight.dtype),
            pltpu.VMEM(norm.shape, norm.dtype),
            pltpu.SemaphoreType.DMA((3,)),
        ],
        compiler_params=params(12),
        cost_estimate=cost(2 * rows * depth * hidden, 2 * depth * (rows + hidden)),
    )(*in_hbm(features, weight, norm))


def merge_kernel(
    own_tiles, per_owner, row, column, count, sources_hbm, targets_hbm, labels_hbm, tiles_hbm, out,
    total, tiles, sources, targets, labels, sems, tile_sems,
):
    small = [
        pltpu.make_async_copy(source, target, sems.at[k])
        for k, (source, target) in enumerate(
            [(sources_hbm, sources), (targets_hbm, targets), (labels_hbm, labels)]
        )
    ]
    parts = tile_sems.shape[0]
    each = tiles.shape[0] // parts
    large = [
        pltpu.make_async_copy(
            tiles_hbm.at[0, pl.ds(k * each, each)],
            tiles.at[pl.ds(k * each, each)],
            tile_sems.at[k],
        )
        for k in range(parts)
    ]
    for copy in small + large:
        copy.start()
    spare, span = total.shape[0] - 1, total.shape[1]
    owners = spare // own_tiles
    total[...] = jnp.zeros_like(total)
    my_row, my_column, used = row[0], column[0], count[0]
    for copy in small:
        copy.wait()

    def add(slot):
        target, source = targets[0, slot], sources[0, slot]
        label = labels[0, target]
        apart = lax.bitwise_xor(target // per_owner, my_row)
        position = (1 - apart % 2) * (owners // 2) + apart // 2
        place = jnp.where(label < own_tiles, position * own_tiles + label, spare)
        block = lax.bitwise_xor(source // own_tiles, my_column)
        total[place, block * own_tiles + source % own_tiles] += tiles[slot].astype(jnp.float32)

    for k, copy in enumerate(large):
        copy.wait()
        pl.loop(k * each, jnp.minimum(used, (k + 1) * each))(add)

    rows = total.shape[2]
    for source in range(span):
        for place in range(spare):
            out[place * rows : (place + 1) * rows, source * rows : (source + 1) * rows] = total[
                place, source
            ].astype(out.dtype)


def merge_tiles(own_tiles, owners, span, index_args, tile_weights):
    sources, targets, count, labels = index_args
    _, capacity, rows, _ = tile_weights.shape
    places = owners * own_tiles
    row = lax.axis_index("row").astype(jnp.int32).reshape(1)
    column = lax.axis_index("col").astype(jnp.int32).reshape(1)
    return pl.pallas_call(
        functools.partial(merge_kernel, own_tiles, labels.shape[1] // owners),
        out_shape=jax.ShapeDtypeStruct((places * rows, span * rows), jnp.bfloat16),
        in_specs=[SMEM] * 3 + [HBM] * 4,
        out_specs=VMEM,
        scratch_shapes=[
            pltpu.VMEM((places + 1, span, rows, rows), jnp.float32),
            pltpu.VMEM(tile_weights.shape[1:], tile_weights.dtype),
            pltpu.SMEM(sources.shape, jnp.int32),
            pltpu.SMEM(targets.shape, jnp.int32),
            pltpu.SMEM(labels.shape, jnp.int32),
            pltpu.SemaphoreType.DMA((3,)),
            pltpu.SemaphoreType.DMA((4 if capacity % 4 == 0 else 1,)),
        ],
        compiler_params=params(24),
        cost_estimate=cost(8 * MIB, 12 * MIB),
    )(row, column, count, *in_hbm(sources, targets, labels, tile_weights))


def product_kernel(first, matrix, *refs):
    *blocks, out = refs
    rows = blocks[0].shape[0]

    @pl.loop(0, out.shape[0] // rows)
    def _(place):
        from_row = pl.multiple_of((first + place) * rows, rows)
        value = None
        for k, block in enumerate(blocks):
            term = jnp.dot(
                matrix[pl.ds(from_row, rows), k * rows : (k + 1) * rows],
                block[...],
                preferred_element_type=jnp.float32,
            )
            value = term if value is None else value + term
        out[pl.ds(pl.multiple_of(place * rows, rows), rows), :] = value.astype(out.dtype)


def product(matrix, blocks, half, dtype, weight):
    rows, width = blocks[0].shape
    total, depth = matrix.shape
    return pl.pallas_call(
        functools.partial(product_kernel, half * (total // rows // 2)),
        out_shape=jax.ShapeDtypeStruct((total // 2, width), dtype),
        in_specs=[VMEM] * (1 + len(blocks)),
        out_specs=VMEM,
        compiler_params=params(16),
        cost_estimate=cost(weight * total * depth * width, 1),
    )(matrix, *blocks)


def join_kernel(stay, came, kept, *sent):
    rows = kept.shape[0]
    value = stay[...].astype(jnp.float32) + came[...].astype(jnp.float32)
    kept[...] = value[:rows]
    for place, out in enumerate(sent):
        out[...] = value[(place + 1) * rows : (place + 2) * rows].astype(out.dtype)


def join(stay, came, rows):
    total, width = stay.shape
    parts = total // rows
    return pl.pallas_call(
        join_kernel,
        out_shape=[jax.ShapeDtypeStruct((rows, width), jnp.float32)]
        + [jax.ShapeDtypeStruct((rows, width), jnp.bfloat16)] * (parts - 1),
        in_specs=[VMEM] * 2,
        out_specs=[VMEM] * parts,
        compiler_params=params(12),
        cost_estimate=cost(1, 1),
    )(stay, came)


def finish_kernel(chunks, projected, norm, *refs):
    out = refs[-1]
    per_chunk = (len(refs) - 1) // chunks
    lanes = norm.shape[1]
    width = refs[0].shape[1]
    for part in range(norm.shape[0]):
        factor = rows_to_lanes(norm[part : part + 1, :], lanes)
        here = slice(part * lanes, (part + 1) * lanes)
        for column in range(0, out.shape[1], lanes):
            pieces = refs[column // width * per_chunk : (column // width + 1) * per_chunk]
            start = column % width
            value = projected[here, column : column + lanes]
            for piece in pieces:
                value += piece[here, start : start + lanes].astype(jnp.float32)
            out[here, column : column + lanes] = jnp.maximum(factor * value, 0.0).astype(out.dtype)


def finish(projected, target_norm, pieces):
    rows, hidden = projected.shape
    flat = [piece for chunk in pieces for piece in chunk]
    return pl.pallas_call(
        functools.partial(finish_kernel, len(pieces)),
        out_shape=jax.ShapeDtypeStruct((rows, hidden), jnp.bfloat16),
        in_specs=[VMEM] * (2 + len(flat)),
        out_specs=VMEM,
        compiler_params=params(12),
        cost_estimate=cost(6 * rows * hidden, 16 * rows * hidden),
    )(projected, target_norm.reshape(-1, 128), *flat)


def visit_kernel(own_tiles, per_owner, sources, targets, count, labels, tiles, blocks, out, total):
    spare, rows = total.shape[0] - 1, total.shape[1]
    total[...] = jnp.zeros_like(total)

    @pl.loop(0, count[0])
    def _(slot):
        target = targets[0, slot]
        label = labels[0, target]
        place = jnp.where(label < own_tiles, target // per_owner * own_tiles + label, spare)
        start = pl.multiple_of(sources[0, slot] * rows, rows)
        total[place] += jnp.dot(
            tiles[0, slot], blocks[pl.ds(start, rows), :], preferred_element_type=jnp.float32
        )

    @pl.loop(0, spare)
    def _(place):
        out[pl.ds(pl.multiple_of(place * rows, rows), rows), :] = total[place].astype(out.dtype)


def visit_tiles(own_tiles, owners, index_args, tile_weights, blocks):
    slots = index_args[-1].shape[1]
    rows = tile_weights.shape[-1]
    places = owners * own_tiles
    hidden = blocks.shape[1]
    return pl.pallas_call(
        functools.partial(visit_kernel, own_tiles, slots // owners),
        out_shape=jax.ShapeDtypeStruct((places * rows, hidden), jnp.bfloat16),
        in_specs=[SMEM] * 4 + [VMEM] * 2,
        out_specs=VMEM,
        scratch_shapes=[pltpu.VMEM((places + 1, rows, hidden), jnp.float32)],
        compiler_params=params(56),
    )(*index_args, tile_weights, blocks)


def swap(value, axis, apart):
    pairs = [(i, i ^ apart) for i in range(lax.axis_size(axis))]
    return lax.ppermute(value, axis, pairs)


def exchange(sent):
    return [swap(value, "row", 2 * (k + 1)) for k, value in enumerate(sent)]


def per_device(
    features,
    weight,
    source_norm,
    target_norm,
    tile_weights,
    tile_source,
    tile_target,
    tile_count,
    mirror_tile,
):
    tile_rows = tile_weights.shape[-1]
    own_rows = features.shape[0]
    own_tiles = own_rows // tile_rows
    owners, columns = lax.axis_size("row"), lax.axis_size("col")
    span = own_tiles * columns
    index_args = (tile_source, tile_target, tile_count, mirror_tile)

    cells = owners * own_tiles * span * tile_rows * tile_rows
    if columns != 4 or owners & (owners - 1) or cells > DENSE_ELEMENTS:
        projected = jnp.dot(features, weight, preferred_element_type=jnp.float32)
        scaled = (source_norm[:, None] * projected).astype(jnp.bfloat16)
        blocks = lax.all_gather(scaled, "col", axis=0, tiled=True)
        partial_value = visit_tiles(own_tiles, owners, index_args, tile_weights, blocks)
        outgoing = partial_value.reshape(owners, own_rows, -1)
        arrived = lax.all_to_all(outgoing, "row", split_axis=0, concat_axis=0, tiled=True)
        gathered = jnp.sum(arrived.astype(jnp.float32), axis=0) + projected
        return jnp.maximum(target_norm[:, None] * gathered, 0.0).astype(jnp.bfloat16)

    projected, *scaled = project(features, weight, source_norm, CHUNKS)
    matrix = merge_tiles(own_tiles, owners, span, index_args, tile_weights)
    across = [swap(own, "col", 3) for own in scaled]
    beside = [swap(own, "col", 1) for own in scaled]
    across[0], matrix = lax.optimization_barrier((across[0], matrix))
    passed = [swap(value, "col", 1) for value in across]
    pieces, sent = [], None
    for blocks, wait in zip(zip(scaled, beside, passed, across), WEIGHTS):
        late = blocks
        if sent is not None:
            moved = exchange(sent)
            blocks, _ = lax.optimization_barrier((blocks, sent))
            late, moved = lax.optimization_barrier((blocks, moved))
            pieces[-1] += moved
        away = product(matrix, blocks, 0, jnp.bfloat16, wait[0])
        stay = product(matrix, late, 1, jnp.float32, wait[1])
        kept, *sent = join(stay, swap(away, "row", 1), own_rows)
        pieces.append([kept])
    pieces[-1] += exchange(sent)
    return finish(projected, target_norm, pieces)


def solution(mesh):
    in_specs = (
        P(("row", "col"), None),
        P(),
        P(("row", "col")),
        P(("row", "col")),
        P(("row", "col"), None, None, None),
        P(("row", "col"), None),
        P(("row", "col"), None),
        P(("row", "col")),
        P(("row", "col"), None),
    )
    out_specs = P(("row", "col"), None)
    return jax.shard_map(
        per_device, mesh=mesh, in_specs=in_specs, out_specs=out_specs, check_vma=False
    )
```

```python
import functools

import jax
import jax.numpy as jnp
from jax import lax
from jax.experimental import pallas as pl
from jax.experimental.pallas import tpu as pltpu
from jax.sharding import PartitionSpec as P

DENSE_ELEMENTS = 4 * 1024 * 1024
CHUNKS = 2
WEIGHTS = ((20, 20), (0, 20))
MIB = 1024 * 1024
SMEM = pl.BlockSpec(memory_space=pltpu.SMEM)
VMEM = pl.BlockSpec(memory_space=pltpu.VMEM)
HBM = pl.BlockSpec(memory_space=pltpu.HBM)


def params(mib):
    return pltpu.CompilerParams(vmem_limit_bytes=int(mib * MIB))


def cost(flops, moved):
    return pl.CostEstimate(flops=flops, bytes_accessed=moved, transcendentals=0)


def in_hbm(*values):
    return [pltpu.with_memory_space_constraint(value, pltpu.HBM) for value in values]


def rows_to_lanes(row, lanes):
    return jnp.broadcast_to(row, (lanes, row.shape[1])).T


def project_kernel(features_hbm, weight_hbm, norm_hbm, projected, *refs):
    *scaled, features, weight, norm, sems = refs
    copies = [
        pltpu.make_async_copy(source, target, sems.at[k])
        for k, (source, target) in enumerate(
            [(weight_hbm, weight), (features_hbm, features), (norm_hbm, norm)]
        )
    ]
    for copy in copies:
        copy.start()
    for copy in copies:
        copy.wait()
    lanes = norm.shape[1]
    value = jnp.dot(features[...], weight[...], preferred_element_type=jnp.float32)
    projected[...] = value
    width = scaled[0].shape[1]
    for part in range(norm.shape[0]):
        factor = rows_to_lanes(norm[part : part + 1, :], lanes)
        for column in range(0, value.shape[1], lanes):
            piece = value[part * lanes : (part + 1) * lanes, column : column + lanes]
            target = scaled[column // width]
            start = column % width
            target[part * lanes : (part + 1) * lanes, start : start + lanes] = (
                factor * piece
            ).astype(target.dtype)


def project(features, weight, source_norm, chunks):
    rows, depth = features.shape
    hidden = weight.shape[1]
    norm = source_norm.reshape(-1, 128)
    return pl.pallas_call(
        project_kernel,
        out_shape=[jax.ShapeDtypeStruct((rows, hidden), jnp.float32)]
        + [jax.ShapeDtypeStruct((rows, hidden // chunks), jnp.bfloat16)] * chunks,
        in_specs=[HBM] * 3,
        out_specs=[VMEM] * (1 + chunks),
        scratch_shapes=[
            pltpu.VMEM(features.shape, features.dtype),
            pltpu.VMEM(weight.shape, weight.dtype),
            pltpu.VMEM(norm.shape, norm.dtype),
            pltpu.SemaphoreType.DMA((3,)),
        ],
        compiler_params=params(12),
        cost_estimate=cost(2 * rows * depth * hidden, 2 * depth * (rows + hidden)),
    )(*in_hbm(features, weight, norm))


def merge_kernel(
    own_tiles, per_owner, row, column, count, sources_hbm, targets_hbm, labels_hbm, tiles_hbm, out,
    total, tiles, sources, targets, labels, sems, tile_sems,
):
    small = [
        pltpu.make_async_copy(source, target, sems.at[k])
        for k, (source, target) in enumerate(
            [(sources_hbm, sources), (targets_hbm, targets), (labels_hbm, labels)]
        )
    ]
    parts = tile_sems.shape[0]
    each = tiles.shape[0] // parts
    large = [
        pltpu.make_async_copy(
            tiles_hbm.at[0, pl.ds(k * each, each)],
            tiles.at[pl.ds(k * each, each)],
            tile_sems.at[k],
        )
        for k in range(parts)
    ]
    for copy in small + large:
        copy.start()
    spare, span = total.shape[0] - 1, total.shape[1]
    owners = spare // own_tiles
    total[...] = jnp.zeros_like(total)
    my_row, my_column, used = row[0], column[0], count[0]
    for copy in small:
        copy.wait()

    def add(slot):
        target, source = targets[0, slot], sources[0, slot]
        label = labels[0, target]
        owner = target // per_owner
        position = owner // 2 + jnp.where(owner % 2 == my_row % 2, owners // 2, 0)
        place = jnp.where(label < own_tiles, position * own_tiles + label, spare)
        block = lax.bitwise_xor(source // own_tiles, my_column)
        total[place, block * own_tiles + source % own_tiles] += tiles[slot].astype(jnp.float32)

    for k, copy in enumerate(large):
        copy.wait()
        pl.loop(k * each, jnp.minimum(used, (k + 1) * each))(add)

    rows = total.shape[2]
    for source in range(span):
        for place in range(spare):
            out[place * rows : (place + 1) * rows, source * rows : (source + 1) * rows] = total[
                place, source
            ].astype(out.dtype)


def merge_tiles(own_tiles, owners, span, index_args, tile_weights):
    sources, targets, count, labels = index_args
    _, capacity, rows, _ = tile_weights.shape
    places = owners * own_tiles
    row = lax.axis_index("row").astype(jnp.int32).reshape(1)
    column = lax.axis_index("col").astype(jnp.int32).reshape(1)
    return pl.pallas_call(
        functools.partial(merge_kernel, own_tiles, labels.shape[1] // owners),
        out_shape=jax.ShapeDtypeStruct((places * rows, span * rows), jnp.bfloat16),
        in_specs=[SMEM] * 3 + [HBM] * 4,
        out_specs=VMEM,
        scratch_shapes=[
            pltpu.VMEM((places + 1, span, rows, rows), jnp.float32),
            pltpu.VMEM(tile_weights.shape[1:], tile_weights.dtype),
            pltpu.SMEM(sources.shape, jnp.int32),
            pltpu.SMEM(targets.shape, jnp.int32),
            pltpu.SMEM(labels.shape, jnp.int32),
            pltpu.SemaphoreType.DMA((3,)),
            pltpu.SemaphoreType.DMA((4 if capacity % 4 == 0 else 1,)),
        ],
        compiler_params=params(24),
        cost_estimate=cost(8 * MIB, 12 * MIB),
    )(row, column, count, *in_hbm(sources, targets, labels, tile_weights))


def product_kernel(first, matrix, *refs):
    *blocks, out = refs
    rows = blocks[0].shape[0]

    @pl.loop(0, out.shape[0] // rows)
    def _(place):
        from_row = pl.multiple_of((first + place) * rows, rows)
        value = None
        for k, block in enumerate(blocks):
            term = jnp.dot(
                matrix[pl.ds(from_row, rows), k * rows : (k + 1) * rows],
                block[...],
                preferred_element_type=jnp.float32,
            )
            value = term if value is None else value + term
        out[pl.ds(pl.multiple_of(place * rows, rows), rows), :] = value.astype(out.dtype)


def product(matrix, blocks, half, dtype, weight):
    rows, width = blocks[0].shape
    total, depth = matrix.shape
    return pl.pallas_call(
        functools.partial(product_kernel, half * (total // rows // 2)),
        out_shape=jax.ShapeDtypeStruct((total // 2, width), dtype),
        in_specs=[VMEM] * (1 + len(blocks)),
        out_specs=VMEM,
        compiler_params=params(16),
        cost_estimate=cost(weight * total * depth * width, 1),
    )(matrix, *blocks)


def join_kernel(stay, came, out):
    out[...] = (stay[...] + came[...].astype(jnp.float32)).astype(out.dtype)


def join(stay, came):
    return pl.pallas_call(
        join_kernel,
        out_shape=jax.ShapeDtypeStruct(came.shape, came.dtype),
        in_specs=[VMEM] * 2,
        out_specs=VMEM,
        compiler_params=params(12),
        cost_estimate=cost(1, 1),
    )(stay, came)


def finish_kernel(projected, norm, *refs):
    *chunks, out = refs
    lanes = norm.shape[1]
    width = chunks[0].shape[1]
    for part in range(norm.shape[0]):
        factor = rows_to_lanes(norm[part : part + 1, :], lanes)
        here = slice(part * lanes, (part + 1) * lanes)
        for column in range(0, out.shape[1], lanes):
            chunk = chunks[column // width]
            start = column % width
            value = projected[here, column : column + lanes]
            for block in range(0, chunk.shape[0], out.shape[0]):
                rows = slice(block + here.start, block + here.stop)
                value += chunk[rows, start : start + lanes].astype(jnp.float32)
            out[here, column : column + lanes] = jnp.maximum(factor * value, 0.0).astype(out.dtype)


def finish(projected, target_norm, chunks):
    rows, hidden = projected.shape
    return pl.pallas_call(
        finish_kernel,
        out_shape=jax.ShapeDtypeStruct((rows, hidden), jnp.bfloat16),
        in_specs=[VMEM] * (2 + len(chunks)),
        out_specs=VMEM,
        compiler_params=params(12),
        cost_estimate=cost(6 * rows * hidden, 16 * rows * hidden),
    )(projected, target_norm.reshape(-1, 128), *chunks)


def visit_kernel(own_tiles, per_owner, sources, targets, count, labels, tiles, blocks, out, total):
    spare, rows = total.shape[0] - 1, total.shape[1]
    total[...] = jnp.zeros_like(total)

    @pl.loop(0, count[0])
    def _(slot):
        target = targets[0, slot]
        label = labels[0, target]
        place = jnp.where(label < own_tiles, target // per_owner * own_tiles + label, spare)
        start = pl.multiple_of(sources[0, slot] * rows, rows)
        total[place] += jnp.dot(
            tiles[0, slot], blocks[pl.ds(start, rows), :], preferred_element_type=jnp.float32
        )

    @pl.loop(0, spare)
    def _(place):
        out[pl.ds(pl.multiple_of(place * rows, rows), rows), :] = total[place].astype(out.dtype)


def visit_tiles(own_tiles, owners, index_args, tile_weights, blocks):
    slots = index_args[-1].shape[1]
    rows = tile_weights.shape[-1]
    places = owners * own_tiles
    hidden = blocks.shape[1]
    return pl.pallas_call(
        functools.partial(visit_kernel, own_tiles, slots // owners),
        out_shape=jax.ShapeDtypeStruct((places * rows, hidden), jnp.bfloat16),
        in_specs=[SMEM] * 4 + [VMEM] * 2,
        out_specs=VMEM,
        scratch_shapes=[pltpu.VMEM((places + 1, rows, hidden), jnp.float32)],
        compiler_params=params(56),
    )(*index_args, tile_weights, blocks)


def swap(value, axis, apart):
    pairs = [(i, i ^ apart) for i in range(lax.axis_size(axis))]
    return lax.ppermute(value, axis, pairs)


def exchange(value):
    owners = lax.axis_size("row")
    groups = [list(range(core, owners, 2)) for core in range(2)]
    return lax.all_to_all(
        value, "row", split_axis=0, concat_axis=0, axis_index_groups=groups, tiled=True
    )


def per_device(
    features,
    weight,
    source_norm,
    target_norm,
    tile_weights,
    tile_source,
    tile_target,
    tile_count,
    mirror_tile,
):
    tile_rows = tile_weights.shape[-1]
    own_rows = features.shape[0]
    own_tiles = own_rows // tile_rows
    owners, columns = lax.axis_size("row"), lax.axis_size("col")
    span = own_tiles * columns
    index_args = (tile_source, tile_target, tile_count, mirror_tile)

    cells = owners * own_tiles * span * tile_rows * tile_rows
    if columns != 4 or owners & (owners - 1) or cells > DENSE_ELEMENTS:
        projected = jnp.dot(features, weight, preferred_element_type=jnp.float32)
        scaled = (source_norm[:, None] * projected).astype(jnp.bfloat16)
        blocks = lax.all_gather(scaled, "col", axis=0, tiled=True)
        partial_value = visit_tiles(own_tiles, owners, index_args, tile_weights, blocks)
        outgoing = partial_value.reshape(owners, own_rows, -1)
        arrived = lax.all_to_all(outgoing, "row", split_axis=0, concat_axis=0, tiled=True)
        gathered = jnp.sum(arrived.astype(jnp.float32), axis=0) + projected
        return jnp.maximum(target_norm[:, None] * gathered, 0.0).astype(jnp.bfloat16)

    projected, *scaled = project(features, weight, source_norm, CHUNKS)
    matrix = merge_tiles(own_tiles, owners, span, index_args, tile_weights)
    across = [swap(own, "col", 3) for own in scaled]
    beside = [swap(own, "col", 1) for own in scaled]
    across[0], matrix = lax.optimization_barrier((across[0], matrix))
    passed = [swap(value, "col", 1) for value in across]
    arrived, sent = [], None
    for blocks, wait in zip(zip(scaled, beside, passed, across), WEIGHTS):
        late = blocks
        if sent is not None:
            blocks, _ = lax.optimization_barrier((blocks, sent))
            late, arrived[-1] = lax.optimization_barrier((blocks, arrived[-1]))
        away = product(matrix, blocks, 0, jnp.bfloat16, wait[0])
        stay = product(matrix, late, 1, jnp.float32, wait[1])
        sent = join(stay, swap(away, "row", 1))
        arrived.append(exchange(sent))
    return finish(projected, target_norm, arrived)


def solution(mesh):
    in_specs = (
        P(("row", "col"), None),
        P(),
        P(("row", "col")),
        P(("row", "col")),
        P(("row", "col"), None, None, None),
        P(("row", "col"), None),
        P(("row", "col"), None),
        P(("row", "col")),
        P(("row", "col"), None),
    )
    out_specs = P(("row", "col"), None)
    return jax.shard_map(
        per_device, mesh=mesh, in_specs=in_specs, out_specs=out_specs, check_vma=False
    )
```

```python
import functools

import jax
import jax.numpy as jnp
from jax import lax
from jax.experimental import pallas as pl
from jax.experimental.pallas import tpu as pltpu
from jax.sharding import PartitionSpec as P

DENSE_ELEMENTS = 4 * 1024 * 1024
CHUNKS = 2
WEIGHTS = ((20, 20), (0, 20))
MIB = 1024 * 1024
SMEM = pl.BlockSpec(memory_space=pltpu.SMEM)
VMEM = pl.BlockSpec(memory_space=pltpu.VMEM)
HBM = pl.BlockSpec(memory_space=pltpu.HBM)


def params(mib):
    return pltpu.CompilerParams(vmem_limit_bytes=int(mib * MIB))


def cost(flops, moved):
    return pl.CostEstimate(flops=flops, bytes_accessed=moved, transcendentals=0)


def in_hbm(*values):
    return [pltpu.with_memory_space_constraint(value, pltpu.HBM) for value in values]


def rows_to_lanes(row, lanes):
    return jnp.broadcast_to(row, (lanes, row.shape[1])).T


def project_kernel(features_hbm, weight_hbm, norm_hbm, projected, *refs):
    *scaled, features, weight, norm, sems = refs
    copies = [
        pltpu.make_async_copy(source, target, sems.at[k])
        for k, (source, target) in enumerate(
            [(weight_hbm, weight), (features_hbm, features), (norm_hbm, norm)]
        )
    ]
    for copy in copies:
        copy.start()
    for copy in copies:
        copy.wait()
    lanes = norm.shape[1]
    value = jnp.dot(features[...], weight[...], preferred_element_type=jnp.float32)
    projected[...] = value
    width = scaled[0].shape[1]
    for part in range(norm.shape[0]):
        factor = rows_to_lanes(norm[part : part + 1, :], lanes)
        for column in range(0, value.shape[1], lanes):
            piece = value[part * lanes : (part + 1) * lanes, column : column + lanes]
            target = scaled[column // width]
            start = column % width
            target[part * lanes : (part + 1) * lanes, start : start + lanes] = (
                factor * piece
            ).astype(target.dtype)


def project(features, weight, source_norm, chunks):
    rows, depth = features.shape
    hidden = weight.shape[1]
    norm = source_norm.reshape(-1, 128)
    return pl.pallas_call(
        project_kernel,
        out_shape=[jax.ShapeDtypeStruct((rows, hidden), jnp.float32)]
        + [jax.ShapeDtypeStruct((rows, hidden // chunks), jnp.bfloat16)] * chunks,
        in_specs=[HBM] * 3,
        out_specs=[VMEM] * (1 + chunks),
        scratch_shapes=[
            pltpu.VMEM(features.shape, features.dtype),
            pltpu.VMEM(weight.shape, weight.dtype),
            pltpu.VMEM(norm.shape, norm.dtype),
            pltpu.SemaphoreType.DMA((3,)),
        ],
        compiler_params=params(12),
        cost_estimate=cost(2 * rows * depth * hidden, 2 * depth * (rows + hidden)),
    )(*in_hbm(features, weight, norm))


def merge_kernel(
    own_tiles, per_owner, row, column, count, sources_hbm, targets_hbm, labels_hbm, tiles_hbm, out,
    total, tiles, sources, targets, labels, sems, tile_sems,
):
    small = [
        pltpu.make_async_copy(source, target, sems.at[k])
        for k, (source, target) in enumerate(
            [(sources_hbm, sources), (targets_hbm, targets), (labels_hbm, labels)]
        )
    ]
    parts = tile_sems.shape[0]
    each = tiles.shape[0] // parts
    large = [
        pltpu.make_async_copy(
            tiles_hbm.at[0, pl.ds(k * each, each)],
            tiles.at[pl.ds(k * each, each)],
            tile_sems.at[k],
        )
        for k in range(parts)
    ]
    for copy in small + large:
        copy.start()
    spare, span = total.shape[0] - 1, total.shape[1]
    owners = spare // own_tiles
    total[...] = jnp.zeros_like(total)
    my_row, my_column, used = row[0], column[0], count[0]
    for copy in small:
        copy.wait()

    def add(slot):
        target, source = targets[0, slot], sources[0, slot]
        label = labels[0, target]
        apart = lax.bitwise_xor(target // per_owner, my_row)
        position = (1 - apart % 2) * (owners // 2) + apart // 2
        place = jnp.where(label < own_tiles, position * own_tiles + label, spare)
        block = lax.bitwise_xor(source // own_tiles, my_column)
        total[place, block * own_tiles + source % own_tiles] += tiles[slot].astype(jnp.float32)

    for k, copy in enumerate(large):
        copy.wait()
        pl.loop(k * each, jnp.minimum(used, (k + 1) * each))(add)

    rows = total.shape[2]
    for source in range(span):
        for place in range(spare):
            out[place * rows : (place + 1) * rows, source * rows : (source + 1) * rows] = total[
                place, source
            ].astype(out.dtype)


def merge_tiles(own_tiles, owners, span, index_args, tile_weights):
    sources, targets, count, labels = index_args
    _, capacity, rows, _ = tile_weights.shape
    places = owners * own_tiles
    row = lax.axis_index("row").astype(jnp.int32).reshape(1)
    column = lax.axis_index("col").astype(jnp.int32).reshape(1)
    return pl.pallas_call(
        functools.partial(merge_kernel, own_tiles, labels.shape[1] // owners),
        out_shape=jax.ShapeDtypeStruct((places * rows, span * rows), jnp.bfloat16),
        in_specs=[SMEM] * 3 + [HBM] * 4,
        out_specs=VMEM,
        scratch_shapes=[
            pltpu.VMEM((places + 1, span, rows, rows), jnp.float32),
            pltpu.VMEM(tile_weights.shape[1:], tile_weights.dtype),
            pltpu.SMEM(sources.shape, jnp.int32),
            pltpu.SMEM(targets.shape, jnp.int32),
            pltpu.SMEM(labels.shape, jnp.int32),
            pltpu.SemaphoreType.DMA((3,)),
            pltpu.SemaphoreType.DMA((4 if capacity % 4 == 0 else 1,)),
        ],
        compiler_params=params(24),
        cost_estimate=cost(8 * MIB, 12 * MIB),
    )(row, column, count, *in_hbm(sources, targets, labels, tile_weights))


def product_kernel(first, matrix, *refs):
    *blocks, out, gathered = refs
    rows = blocks[0].shape[0]
    for k, block in enumerate(blocks):
        gathered[k * rows : (k + 1) * rows, :] = block[...]
    value = jnp.dot(
        matrix[first : first + out.shape[0], :],
        gathered[...],
        preferred_element_type=jnp.float32,
    )
    out[...] = value.astype(out.dtype)


def product(matrix, blocks, half, dtype, weight):
    rows, width = blocks[0].shape
    total, depth = matrix.shape
    return pl.pallas_call(
        functools.partial(product_kernel, half * (total // 2)),
        out_shape=jax.ShapeDtypeStruct((total // 2, width), dtype),
        in_specs=[VMEM] * (1 + len(blocks)),
        out_specs=VMEM,
        scratch_shapes=[pltpu.VMEM((depth, width), blocks[0].dtype)],
        compiler_params=params(16),
        cost_estimate=cost(weight * total * depth * width, 1),
    )(matrix, *blocks)


def join_kernel(stay, came, kept, *sent):
    rows = kept.shape[0]
    value = stay[...].astype(jnp.float32) + came[...].astype(jnp.float32)
    kept[...] = value[:rows]
    for place, out in enumerate(sent):
        out[...] = value[(place + 1) * rows : (place + 2) * rows].astype(out.dtype)


def join(stay, came, rows):
    total, width = stay.shape
    parts = total // rows
    return pl.pallas_call(
        join_kernel,
        out_shape=[jax.ShapeDtypeStruct((rows, width), jnp.float32)]
        + [jax.ShapeDtypeStruct((rows, width), jnp.bfloat16)] * (parts - 1),
        in_specs=[VMEM] * 2,
        out_specs=[VMEM] * parts,
        compiler_params=params(12),
        cost_estimate=cost(1, 1),
    )(stay, came)


def finish_kernel(chunks, projected, norm, *refs):
    out = refs[-1]
    per_chunk = (len(refs) - 1) // chunks
    lanes = norm.shape[1]
    width = refs[0].shape[1]
    for part in range(norm.shape[0]):
        factor = rows_to_lanes(norm[part : part + 1, :], lanes)
        here = slice(part * lanes, (part + 1) * lanes)
        for column in range(0, out.shape[1], lanes):
            pieces = refs[column // width * per_chunk : (column // width + 1) * per_chunk]
            start = column % width
            value = projected[here, column : column + lanes]
            for piece in pieces:
                value += piece[here, start : start + lanes].astype(jnp.float32)
            out[here, column : column + lanes] = jnp.maximum(factor * value, 0.0).astype(out.dtype)


def finish(projected, target_norm, pieces):
    rows, hidden = projected.shape
    flat = [piece for chunk in pieces for piece in chunk]
    return pl.pallas_call(
        functools.partial(finish_kernel, len(pieces)),
        out_shape=jax.ShapeDtypeStruct((rows, hidden), jnp.bfloat16),
        in_specs=[VMEM] * (2 + len(flat)),
        out_specs=VMEM,
        compiler_params=params(12),
        cost_estimate=cost(6 * rows * hidden, 16 * rows * hidden),
    )(projected, target_norm.reshape(-1, 128), *flat)


def visit_kernel(own_tiles, per_owner, sources, targets, count, labels, tiles, blocks, out, total):
    spare, rows = total.shape[0] - 1, total.shape[1]
    total[...] = jnp.zeros_like(total)

    @pl.loop(0, count[0])
    def _(slot):
        target = targets[0, slot]
        label = labels[0, target]
        place = jnp.where(label < own_tiles, target // per_owner * own_tiles + label, spare)
        start = pl.multiple_of(sources[0, slot] * rows, rows)
        total[place] += jnp.dot(
            tiles[0, slot], blocks[pl.ds(start, rows), :], preferred_element_type=jnp.float32
        )

    @pl.loop(0, spare)
    def _(place):
        out[pl.ds(pl.multiple_of(place * rows, rows), rows), :] = total[place].astype(out.dtype)


def visit_tiles(own_tiles, owners, index_args, tile_weights, blocks):
    slots = index_args[-1].shape[1]
    rows = tile_weights.shape[-1]
    places = owners * own_tiles
    hidden = blocks.shape[1]
    return pl.pallas_call(
        functools.partial(visit_kernel, own_tiles, slots // owners),
        out_shape=jax.ShapeDtypeStruct((places * rows, hidden), jnp.bfloat16),
        in_specs=[SMEM] * 4 + [VMEM] * 2,
        out_specs=VMEM,
        scratch_shapes=[pltpu.VMEM((places + 1, rows, hidden), jnp.float32)],
        compiler_params=params(56),
    )(*index_args, tile_weights, blocks)


def swap(value, axis, apart):
    pairs = [(i, i ^ apart) for i in range(lax.axis_size(axis))]
    return lax.ppermute(value, axis, pairs)


def exchange(sent):
    return [swap(sent[k], "row", 2 * (k + 1)) for k in reversed(range(len(sent)))]


def per_device(
    features,
    weight,
    source_norm,
    target_norm,
    tile_weights,
    tile_source,
    tile_target,
    tile_count,
    mirror_tile,
):
    tile_rows = tile_weights.shape[-1]
    own_rows = features.shape[0]
    own_tiles = own_rows // tile_rows
    owners, columns = lax.axis_size("row"), lax.axis_size("col")
    span = own_tiles * columns
    index_args = (tile_source, tile_target, tile_count, mirror_tile)

    cells = owners * own_tiles * span * tile_rows * tile_rows
    if columns != 4 or owners & (owners - 1) or cells > DENSE_ELEMENTS:
        projected = jnp.dot(features, weight, preferred_element_type=jnp.float32)
        scaled = (source_norm[:, None] * projected).astype(jnp.bfloat16)
        blocks = lax.all_gather(scaled, "col", axis=0, tiled=True)
        partial_value = visit_tiles(own_tiles, owners, index_args, tile_weights, blocks)
        outgoing = partial_value.reshape(owners, own_rows, -1)
        arrived = lax.all_to_all(outgoing, "row", split_axis=0, concat_axis=0, tiled=True)
        gathered = jnp.sum(arrived.astype(jnp.float32), axis=0) + projected
        return jnp.maximum(target_norm[:, None] * gathered, 0.0).astype(jnp.bfloat16)

    projected, *scaled = project(features, weight, source_norm, CHUNKS)
    matrix = merge_tiles(own_tiles, owners, span, index_args, tile_weights)
    across = [swap(own, "col", 3) for own in scaled]
    beside = [swap(own, "col", 1) for own in scaled]
    across[0], matrix = lax.optimization_barrier((across[0], matrix))
    passed = [swap(value, "col", 1) for value in across]
    pieces, sent = [], None
    for blocks, wait in zip(zip(scaled, beside, passed, across), WEIGHTS):
        if sent is not None:
            pieces[-1] += exchange(sent)
            blocks, _ = lax.optimization_barrier((blocks, sent))
        away = product(matrix, blocks, 0, jnp.bfloat16, wait[0])
        stay = product(matrix, blocks, 1, jnp.float32, wait[1])
        kept, *sent = join(stay, swap(away, "row", 1), own_rows)
        pieces.append([kept])
    pieces[-1] += exchange(sent)
    return finish(projected, target_norm, pieces)


def solution(mesh):
    in_specs = (
        P(("row", "col"), None),
        P(),
        P(("row", "col")),
        P(("row", "col")),
        P(("row", "col"), None, None, None),
        P(("row", "col"), None),
        P(("row", "col"), None),
        P(("row", "col")),
        P(("row", "col"), None),
    )
    out_specs = P(("row", "col"), None)
    return jax.shard_map(
        per_device, mesh=mesh, in_specs=in_specs, out_specs=out_specs, check_vma=False
    )
```

```python
import functools

import jax
import jax.numpy as jnp
from jax import lax
from jax.experimental import pallas as pl
from jax.experimental.pallas import tpu as pltpu
from jax.sharding import PartitionSpec as P

DENSE_ELEMENTS = 4 * 1024 * 1024
CHUNKS = 2
WEIGHTS = ((20, 20), (0, 20))
MIB = 1024 * 1024
SMEM = pl.BlockSpec(memory_space=pltpu.SMEM)
VMEM = pl.BlockSpec(memory_space=pltpu.VMEM)
HBM = pl.BlockSpec(memory_space=pltpu.HBM)


def params(mib):
    return pltpu.CompilerParams(vmem_limit_bytes=int(mib * MIB))


def cost(flops, moved):
    return pl.CostEstimate(flops=flops, bytes_accessed=moved, transcendentals=0)


def in_hbm(*values):
    return [pltpu.with_memory_space_constraint(value, pltpu.HBM) for value in values]


def rows_to_lanes(row, lanes):
    return jnp.broadcast_to(row, (lanes, row.shape[1])).T


def project_kernel(features_hbm, weight_hbm, norm_hbm, projected, *refs):
    *scaled, features, weight, norm, sems = refs
    copies = [
        pltpu.make_async_copy(source, target, sems.at[k])
        for k, (source, target) in enumerate(
            [(weight_hbm, weight), (features_hbm, features), (norm_hbm, norm)]
        )
    ]
    for copy in copies:
        copy.start()
    for copy in copies:
        copy.wait()
    lanes = norm.shape[1]
    value = jnp.dot(features[...], weight[...], preferred_element_type=jnp.float32)
    projected[...] = value
    width = scaled[0].shape[1]
    for part in range(norm.shape[0]):
        factor = rows_to_lanes(norm[part : part + 1, :], lanes)
        for column in range(0, value.shape[1], lanes):
            piece = value[part * lanes : (part + 1) * lanes, column : column + lanes]
            target = scaled[column // width]
            start = column % width
            target[part * lanes : (part + 1) * lanes, start : start + lanes] = (
                factor * piece
            ).astype(target.dtype)


def project(features, weight, source_norm, chunks):
    rows, depth = features.shape
    hidden = weight.shape[1]
    norm = source_norm.reshape(-1, 128)
    return pl.pallas_call(
        project_kernel,
        out_shape=[jax.ShapeDtypeStruct((rows, hidden), jnp.float32)]
        + [jax.ShapeDtypeStruct((rows, hidden // chunks), jnp.bfloat16)] * chunks,
        in_specs=[HBM] * 3,
        out_specs=[VMEM] * (1 + chunks),
        scratch_shapes=[
            pltpu.VMEM(features.shape, features.dtype),
            pltpu.VMEM(weight.shape, weight.dtype),
            pltpu.VMEM(norm.shape, norm.dtype),
            pltpu.SemaphoreType.DMA((3,)),
        ],
        compiler_params=params(12),
        cost_estimate=cost(2 * rows * depth * hidden, 2 * depth * (rows + hidden)),
    )(*in_hbm(features, weight, norm))


def merge_kernel(
    own_tiles, per_owner, row, column, count, sources_hbm, targets_hbm, labels_hbm, tiles_hbm, out,
    total, tiles, sources, targets, labels, sems, tile_sems,
):
    small = [
        pltpu.make_async_copy(source, target, sems.at[k])
        for k, (source, target) in enumerate(
            [(sources_hbm, sources), (targets_hbm, targets), (labels_hbm, labels)]
        )
    ]
    parts = tile_sems.shape[0]
    each = tiles.shape[0] // parts
    large = [
        pltpu.make_async_copy(
            tiles_hbm.at[0, pl.ds(k * each, each)],
            tiles.at[pl.ds(k * each, each)],
            tile_sems.at[k],
        )
        for k in range(parts)
    ]
    for copy in small + large:
        copy.start()
    spare, span = total.shape[0] - 1, total.shape[1]
    owners = spare // own_tiles
    total[...] = jnp.zeros_like(total)
    my_row, my_column, used = row[0], column[0], count[0]
    for copy in small:
        copy.wait()

    def add(slot):
        target, source = targets[0, slot], sources[0, slot]
        label = labels[0, target]
        apart = lax.bitwise_xor(target // per_owner, my_row)
        position = (1 - apart % 2) * (owners // 2) + apart // 2
        place = jnp.where(label < own_tiles, position * own_tiles + label, spare)
        block = lax.bitwise_xor(source // own_tiles, my_column)
        total[place, block * own_tiles + source % own_tiles] += tiles[slot].astype(jnp.float32)

    for k, copy in enumerate(large):
        copy.wait()
        pl.loop(k * each, jnp.minimum(used, (k + 1) * each))(add)

    rows = total.shape[2]
    for source in range(span):
        for place in range(spare):
            out[place * rows : (place + 1) * rows, source * rows : (source + 1) * rows] = total[
                place, source
            ].astype(out.dtype)


def merge_tiles(own_tiles, owners, span, index_args, tile_weights):
    sources, targets, count, labels = index_args
    _, capacity, rows, _ = tile_weights.shape
    places = owners * own_tiles
    row = lax.axis_index("row").astype(jnp.int32).reshape(1)
    column = lax.axis_index("col").astype(jnp.int32).reshape(1)
    return pl.pallas_call(
        functools.partial(merge_kernel, own_tiles, labels.shape[1] // owners),
        out_shape=jax.ShapeDtypeStruct((places * rows, span * rows), jnp.bfloat16),
        in_specs=[SMEM] * 3 + [HBM] * 4,
        out_specs=VMEM,
        scratch_shapes=[
            pltpu.VMEM((places + 1, span, rows, rows), jnp.float32),
            pltpu.VMEM(tile_weights.shape[1:], tile_weights.dtype),
            pltpu.SMEM(sources.shape, jnp.int32),
            pltpu.SMEM(targets.shape, jnp.int32),
            pltpu.SMEM(labels.shape, jnp.int32),
            pltpu.SemaphoreType.DMA((3,)),
            pltpu.SemaphoreType.DMA((4 if capacity % 4 == 0 else 1,)),
        ],
        compiler_params=params(24),
        cost_estimate=cost(8 * MIB, 12 * MIB),
    )(row, column, count, *in_hbm(sources, targets, labels, tile_weights))


def product_kernel(first, matrix, *refs):
    *blocks, out, gathered = refs
    rows = blocks[0].shape[0]
    for k, block in enumerate(blocks):
        gathered[k * rows : (k + 1) * rows, :] = block[...]
    value = jnp.dot(
        matrix[first : first + out.shape[0], :],
        gathered[...],
        preferred_element_type=jnp.float32,
    )
    out[...] = value.astype(out.dtype)


def product(matrix, blocks, half, dtype, weight):
    rows, width = blocks[0].shape
    total, depth = matrix.shape
    return pl.pallas_call(
        functools.partial(product_kernel, half * (total // 2)),
        out_shape=jax.ShapeDtypeStruct((total // 2, width), dtype),
        in_specs=[VMEM] * (1 + len(blocks)),
        out_specs=VMEM,
        scratch_shapes=[pltpu.VMEM((depth, width), blocks[0].dtype)],
        compiler_params=params(16),
        cost_estimate=cost(weight * total * depth * width, 1),
    )(matrix, *blocks)


def join_kernel(stay, came, kept, *sent):
    rows = kept.shape[0]
    value = stay[...].astype(jnp.float32) + came[...].astype(jnp.float32)
    kept[...] = value[:rows]
    for place, out in enumerate(sent):
        out[...] = value[(place + 1) * rows : (place + 2) * rows].astype(out.dtype)


def join(stay, came, rows):
    total, width = stay.shape
    parts = total // rows
    return pl.pallas_call(
        join_kernel,
        out_shape=[jax.ShapeDtypeStruct((rows, width), jnp.float32)]
        + [jax.ShapeDtypeStruct((rows, width), jnp.bfloat16)] * (parts - 1),
        in_specs=[VMEM] * 2,
        out_specs=[VMEM] * parts,
        compiler_params=params(12),
        cost_estimate=cost(1, 1),
    )(stay, came)


def finish_kernel(chunks, projected, norm, *refs):
    out = refs[-1]
    per_chunk = (len(refs) - 1) // chunks
    lanes = norm.shape[1]
    width = refs[0].shape[1]
    for part in range(norm.shape[0]):
        factor = rows_to_lanes(norm[part : part + 1, :], lanes)
        here = slice(part * lanes, (part + 1) * lanes)
        for column in range(0, out.shape[1], lanes):
            pieces = refs[column // width * per_chunk : (column // width + 1) * per_chunk]
            start = column % width
            value = projected[here, column : column + lanes]
            for piece in pieces:
                value += piece[here, start : start + lanes].astype(jnp.float32)
            out[here, column : column + lanes] = jnp.maximum(factor * value, 0.0).astype(out.dtype)


def finish(projected, target_norm, pieces):
    rows, hidden = projected.shape
    flat = [piece for chunk in pieces for piece in chunk]
    return pl.pallas_call(
        functools.partial(finish_kernel, len(pieces)),
        out_shape=jax.ShapeDtypeStruct((rows, hidden), jnp.bfloat16),
        in_specs=[VMEM] * (2 + len(flat)),
        out_specs=VMEM,
        compiler_params=params(12),
        cost_estimate=cost(6 * rows * hidden, 16 * rows * hidden),
    )(projected, target_norm.reshape(-1, 128), *flat)


def visit_kernel(own_tiles, per_owner, sources, targets, count, labels, tiles, blocks, out, total):
    spare, rows = total.shape[0] - 1, total.shape[1]
    total[...] = jnp.zeros_like(total)

    @pl.loop(0, count[0])
    def _(slot):
        target = targets[0, slot]
        label = labels[0, target]
        place = jnp.where(label < own_tiles, target // per_owner * own_tiles + label, spare)
        start = pl.multiple_of(sources[0, slot] * rows, rows)
        total[place] += jnp.dot(
            tiles[0, slot], blocks[pl.ds(start, rows), :], preferred_element_type=jnp.float32
        )

    @pl.loop(0, spare)
    def _(place):
        out[pl.ds(pl.multiple_of(place * rows, rows), rows), :] = total[place].astype(out.dtype)


def visit_tiles(own_tiles, owners, index_args, tile_weights, blocks):
    slots = index_args[-1].shape[1]
    rows = tile_weights.shape[-1]
    places = owners * own_tiles
    hidden = blocks.shape[1]
    return pl.pallas_call(
        functools.partial(visit_kernel, own_tiles, slots // owners),
        out_shape=jax.ShapeDtypeStruct((places * rows, hidden), jnp.bfloat16),
        in_specs=[SMEM] * 4 + [VMEM] * 2,
        out_specs=VMEM,
        scratch_shapes=[pltpu.VMEM((places + 1, rows, hidden), jnp.float32)],
        compiler_params=params(56),
    )(*index_args, tile_weights, blocks)


def swap(value, axis, apart):
    pairs = [(i, i ^ apart) for i in range(lax.axis_size(axis))]
    return lax.ppermute(value, axis, pairs)


def exchange(sent):
    return [swap(value, "row", 2 * (k + 1)) for k, value in enumerate(sent)]


def per_device(
    features,
    weight,
    source_norm,
    target_norm,
    tile_weights,
    tile_source,
    tile_target,
    tile_count,
    mirror_tile,
):
    tile_rows = tile_weights.shape[-1]
    own_rows = features.shape[0]
    own_tiles = own_rows // tile_rows
    owners, columns = lax.axis_size("row"), lax.axis_size("col")
    span = own_tiles * columns
    index_args = (tile_source, tile_target, tile_count, mirror_tile)

    cells = owners * own_tiles * span * tile_rows * tile_rows
    if columns != 4 or owners & (owners - 1) or cells > DENSE_ELEMENTS:
        projected = jnp.dot(features, weight, preferred_element_type=jnp.float32)
        scaled = (source_norm[:, None] * projected).astype(jnp.bfloat16)
        blocks = lax.all_gather(scaled, "col", axis=0, tiled=True)
        partial_value = visit_tiles(own_tiles, owners, index_args, tile_weights, blocks)
        outgoing = partial_value.reshape(owners, own_rows, -1)
        arrived = lax.all_to_all(outgoing, "row", split_axis=0, concat_axis=0, tiled=True)
        gathered = jnp.sum(arrived.astype(jnp.float32), axis=0) + projected
        return jnp.maximum(target_norm[:, None] * gathered, 0.0).astype(jnp.bfloat16)

    projected, *scaled = project(features, weight, source_norm, CHUNKS)
    matrix = merge_tiles(own_tiles, owners, span, index_args, tile_weights)
    pieces, sent = [], None
    for chunk, (own, wait) in enumerate(zip(scaled, WEIGHTS)):
        lead = trail = own
        if chunk:
            lead, _ = lax.optimization_barrier((own, across))
            trail, _ = lax.optimization_barrier((own, away))
        across = swap(lead, "col", 3)
        beside = swap(trail, "col", 1)
        if chunk:
            onward, _ = lax.optimization_barrier((across, sent))
        else:
            onward, beside, matrix = lax.optimization_barrier((across, beside, matrix))
        passed = swap(onward, "col", 1)
        blocks = own, beside, passed, across
        if chunk:
            pieces[-1] += exchange(sent)
            blocks, _ = lax.optimization_barrier((blocks, sent))
        away = product(matrix, blocks, 0, jnp.bfloat16, wait[0])
        stay = product(matrix, blocks, 1, jnp.float32, wait[1])
        kept, *sent = join(stay, swap(away, "row", 1), own_rows)
        pieces.append([kept])
    pieces[-1] += exchange(sent)
    return finish(projected, target_norm, pieces)


def solution(mesh):
    in_specs = (
        P(("row", "col"), None),
        P(),
        P(("row", "col")),
        P(("row", "col")),
        P(("row", "col"), None, None, None),
        P(("row", "col"), None),
        P(("row", "col"), None),
        P(("row", "col")),
        P(("row", "col"), None),
    )
    out_specs = P(("row", "col"), None)
    return jax.shard_map(
        per_device, mesh=mesh, in_specs=in_specs, out_specs=out_specs, check_vma=False
    )
```

```python
import functools

import jax
import jax.numpy as jnp
from jax import lax
from jax.experimental import pallas as pl
from jax.experimental.pallas import tpu as pltpu
from jax.sharding import PartitionSpec as P

DENSE_ELEMENTS = 4 * 1024 * 1024
CHUNKS = 2
WEIGHTS = ((20, 20), (0, 20))
MIB = 1024 * 1024
SMEM = pl.BlockSpec(memory_space=pltpu.SMEM)
VMEM = pl.BlockSpec(memory_space=pltpu.VMEM)
HBM = pl.BlockSpec(memory_space=pltpu.HBM)


def params(mib):
    return pltpu.CompilerParams(vmem_limit_bytes=int(mib * MIB))


def cost(flops, moved):
    return pl.CostEstimate(flops=flops, bytes_accessed=moved, transcendentals=0)


def in_hbm(*values):
    return [pltpu.with_memory_space_constraint(value, pltpu.HBM) for value in values]


def rows_to_lanes(row, lanes):
    return jnp.broadcast_to(row, (lanes, row.shape[1])).T


def project_kernel(features_hbm, weight_hbm, norm_hbm, projected, *refs):
    *scaled, features, weight, norm, sems = refs
    copies = [
        pltpu.make_async_copy(source, target, sems.at[k])
        for k, (source, target) in enumerate(
            [(weight_hbm, weight), (features_hbm, features), (norm_hbm, norm)]
        )
    ]
    for copy in copies:
        copy.start()
    for copy in copies:
        copy.wait()
    lanes = norm.shape[1]
    value = jnp.dot(features[...], weight[...], preferred_element_type=jnp.float32)
    projected[...] = value
    width = scaled[0].shape[1]
    for part in range(norm.shape[0]):
        factor = rows_to_lanes(norm[part : part + 1, :], lanes)
        for column in range(0, value.shape[1], lanes):
            piece = value[part * lanes : (part + 1) * lanes, column : column + lanes]
            target = scaled[column // width]
            start = column % width
            target[part * lanes : (part + 1) * lanes, start : start + lanes] = (
                factor * piece
            ).astype(target.dtype)


def project(features, weight, source_norm, chunks):
    rows, depth = features.shape
    hidden = weight.shape[1]
    norm = source_norm.reshape(-1, 128)
    return pl.pallas_call(
        project_kernel,
        out_shape=[jax.ShapeDtypeStruct((rows, hidden), jnp.float32)]
        + [jax.ShapeDtypeStruct((rows, hidden // chunks), jnp.bfloat16)] * chunks,
        in_specs=[HBM] * 3,
        out_specs=[VMEM] * (1 + chunks),
        scratch_shapes=[
            pltpu.VMEM(features.shape, features.dtype),
            pltpu.VMEM(weight.shape, weight.dtype),
            pltpu.VMEM(norm.shape, norm.dtype),
            pltpu.SemaphoreType.DMA((3,)),
        ],
        compiler_params=params(12),
        cost_estimate=cost(2 * rows * depth * hidden, 2 * depth * (rows + hidden)),
    )(*in_hbm(features, weight, norm))


def merge_kernel(
    own_tiles, per_owner, row, column, count, sources_hbm, targets_hbm, labels_hbm, tiles_hbm, out,
    total, tiles, sources, targets, labels, sems, tile_sems,
):
    small = [
        pltpu.make_async_copy(source, target, sems.at[k])
        for k, (source, target) in enumerate(
            [(sources_hbm, sources), (targets_hbm, targets), (labels_hbm, labels)]
        )
    ]
    parts = tile_sems.shape[0]
    each = tiles.shape[0] // parts
    large = [
        pltpu.make_async_copy(
            tiles_hbm.at[0, pl.ds(k * each, each)],
            tiles.at[pl.ds(k * each, each)],
            tile_sems.at[k],
        )
        for k in range(parts)
    ]
    for copy in small + large:
        copy.start()
    spare, span = total.shape[0] - 1, total.shape[1]
    owners = spare // own_tiles
    total[...] = jnp.zeros_like(total)
    my_row, my_column, used = row[0], column[0], count[0]
    for copy in small:
        copy.wait()

    def add(slot):
        target, source = targets[0, slot], sources[0, slot]
        label = labels[0, target]
        apart = lax.bitwise_xor(target // per_owner, my_row)
        position = (1 - apart % 2) * (owners // 2) + apart // 2
        place = jnp.where(label < own_tiles, position * own_tiles + label, spare)
        block = lax.bitwise_xor(source // own_tiles, my_column)
        total[place, block * own_tiles + source % own_tiles] += tiles[slot].astype(jnp.float32)

    for k, copy in enumerate(large):
        copy.wait()
        pl.loop(k * each, jnp.minimum(used, (k + 1) * each))(add)

    rows = total.shape[2]
    for source in range(span):
        for place in range(spare):
            out[place * rows : (place + 1) * rows, source * rows : (source + 1) * rows] = total[
                place, source
            ].astype(out.dtype)


def merge_tiles(own_tiles, owners, span, index_args, tile_weights):
    sources, targets, count, labels = index_args
    _, capacity, rows, _ = tile_weights.shape
    places = owners * own_tiles
    row = lax.axis_index("row").astype(jnp.int32).reshape(1)
    column = lax.axis_index("col").astype(jnp.int32).reshape(1)
    return pl.pallas_call(
        functools.partial(merge_kernel, own_tiles, labels.shape[1] // owners),
        out_shape=jax.ShapeDtypeStruct((places * rows, span * rows), jnp.bfloat16),
        in_specs=[SMEM] * 3 + [HBM] * 4,
        out_specs=VMEM,
        scratch_shapes=[
            pltpu.VMEM((places + 1, span, rows, rows), jnp.float32),
            pltpu.VMEM(tile_weights.shape[1:], tile_weights.dtype),
            pltpu.SMEM(sources.shape, jnp.int32),
            pltpu.SMEM(targets.shape, jnp.int32),
            pltpu.SMEM(labels.shape, jnp.int32),
            pltpu.SemaphoreType.DMA((3,)),
            pltpu.SemaphoreType.DMA((4 if capacity % 4 == 0 else 1,)),
        ],
        compiler_params=params(24),
        cost_estimate=cost(8 * MIB, 12 * MIB),
    )(row, column, count, *in_hbm(sources, targets, labels, tile_weights))


def product_kernel(first, matrix, *refs):
    *blocks, out, gathered = refs
    rows = blocks[0].shape[0]
    for k, block in enumerate(blocks):
        gathered[k * rows : (k + 1) * rows, :] = block[...]
    value = jnp.dot(
        matrix[first : first + out.shape[0], :],
        gathered[...],
        preferred_element_type=jnp.float32,
    )
    out[...] = value.astype(out.dtype)


def product(matrix, blocks, half, dtype, weight):
    rows, width = blocks[0].shape
    total, depth = matrix.shape
    return pl.pallas_call(
        functools.partial(product_kernel, half * (total // 2)),
        out_shape=jax.ShapeDtypeStruct((total // 2, width), dtype),
        in_specs=[VMEM] * (1 + len(blocks)),
        out_specs=VMEM,
        scratch_shapes=[pltpu.VMEM((depth, width), blocks[0].dtype)],
        compiler_params=params(16),
        cost_estimate=cost(weight * total * depth * width, 1),
    )(matrix, *blocks)


def join_kernel(stay, came, kept, *sent):
    rows = kept.shape[0]
    value = stay[...].astype(jnp.float32) + came[...].astype(jnp.float32)
    kept[...] = value[:rows]
    for place, out in enumerate(sent):
        out[...] = value[(place + 1) * rows : (place + 2) * rows].astype(out.dtype)


def join(stay, came, rows):
    total, width = stay.shape
    parts = total // rows
    return pl.pallas_call(
        join_kernel,
        out_shape=[jax.ShapeDtypeStruct((rows, width), jnp.float32)]
        + [jax.ShapeDtypeStruct((rows, width), jnp.bfloat16)] * (parts - 1),
        in_specs=[VMEM] * 2,
        out_specs=[VMEM] * parts,
        compiler_params=params(12),
        cost_estimate=cost(1, 1),
    )(stay, came)


def finish_kernel(chunks, projected, norm, *refs):
    out = refs[-1]
    per_chunk = (len(refs) - 1) // chunks
    lanes = norm.shape[1]
    width = refs[0].shape[1]
    for part in range(norm.shape[0]):
        factor = rows_to_lanes(norm[part : part + 1, :], lanes)
        here = slice(part * lanes, (part + 1) * lanes)
        for column in range(0, out.shape[1], lanes):
            pieces = refs[column // width * per_chunk : (column // width + 1) * per_chunk]
            start = column % width
            value = projected[here, column : column + lanes]
            for piece in pieces:
                value += piece[here, start : start + lanes].astype(jnp.float32)
            out[here, column : column + lanes] = jnp.maximum(factor * value, 0.0).astype(out.dtype)


def finish(projected, target_norm, pieces):
    rows, hidden = projected.shape
    flat = [piece for chunk in pieces for piece in chunk]
    return pl.pallas_call(
        functools.partial(finish_kernel, len(pieces)),
        out_shape=jax.ShapeDtypeStruct((rows, hidden), jnp.bfloat16),
        in_specs=[VMEM] * (2 + len(flat)),
        out_specs=VMEM,
        compiler_params=params(12),
        cost_estimate=cost(6 * rows * hidden, 16 * rows * hidden),
    )(projected, target_norm.reshape(-1, 128), *flat)


def visit_kernel(own_tiles, per_owner, sources, targets, count, labels, tiles, blocks, out, total):
    spare, rows = total.shape[0] - 1, total.shape[1]
    total[...] = jnp.zeros_like(total)

    @pl.loop(0, count[0])
    def _(slot):
        target = targets[0, slot]
        label = labels[0, target]
        place = jnp.where(label < own_tiles, target // per_owner * own_tiles + label, spare)
        start = pl.multiple_of(sources[0, slot] * rows, rows)
        total[place] += jnp.dot(
            tiles[0, slot], blocks[pl.ds(start, rows), :], preferred_element_type=jnp.float32
        )

    @pl.loop(0, spare)
    def _(place):
        out[pl.ds(pl.multiple_of(place * rows, rows), rows), :] = total[place].astype(out.dtype)


def visit_tiles(own_tiles, owners, index_args, tile_weights, blocks):
    slots = index_args[-1].shape[1]
    rows = tile_weights.shape[-1]
    places = owners * own_tiles
    hidden = blocks.shape[1]
    return pl.pallas_call(
        functools.partial(visit_kernel, own_tiles, slots // owners),
        out_shape=jax.ShapeDtypeStruct((places * rows, hidden), jnp.bfloat16),
        in_specs=[SMEM] * 4 + [VMEM] * 2,
        out_specs=VMEM,
        scratch_shapes=[pltpu.VMEM((places + 1, rows, hidden), jnp.float32)],
        compiler_params=params(56),
    )(*index_args, tile_weights, blocks)


def swap(value, axis, apart):
    pairs = [(i, i ^ apart) for i in range(lax.axis_size(axis))]
    return lax.ppermute(value, axis, pairs)


def exchange(sent):
    return [swap(value, "row", 2 * (k + 1)) for k, value in enumerate(sent)]


def per_device(
    features,
    weight,
    source_norm,
    target_norm,
    tile_weights,
    tile_source,
    tile_target,
    tile_count,
    mirror_tile,
):
    tile_rows = tile_weights.shape[-1]
    own_rows = features.shape[0]
    own_tiles = own_rows // tile_rows
    owners, columns = lax.axis_size("row"), lax.axis_size("col")
    span = own_tiles * columns
    index_args = (tile_source, tile_target, tile_count, mirror_tile)

    cells = owners * own_tiles * span * tile_rows * tile_rows
    if columns != 4 or owners & (owners - 1) or cells > DENSE_ELEMENTS:
        projected = jnp.dot(features, weight, preferred_element_type=jnp.float32)
        scaled = (source_norm[:, None] * projected).astype(jnp.bfloat16)
        blocks = lax.all_gather(scaled, "col", axis=0, tiled=True)
        partial_value = visit_tiles(own_tiles, owners, index_args, tile_weights, blocks)
        outgoing = partial_value.reshape(owners, own_rows, -1)
        arrived = lax.all_to_all(outgoing, "row", split_axis=0, concat_axis=0, tiled=True)
        gathered = jnp.sum(arrived.astype(jnp.float32), axis=0) + projected
        return jnp.maximum(target_norm[:, None] * gathered, 0.0).astype(jnp.bfloat16)

    projected, *scaled = project(features, weight, source_norm, CHUNKS)
    matrix = merge_tiles(own_tiles, owners, span, index_args, tile_weights)
    across = [swap(own, "col", 3) for own in scaled]
    across[0], matrix = lax.optimization_barrier((across[0], matrix))
    passed = [swap(value, "col", 1) for value in across]
    pieces, sent = [], None
    for own, far, near, wait in zip(scaled, across, passed, WEIGHTS):
        ready = own
        if sent is not None:
            ready, _ = lax.optimization_barrier((own, away))
        blocks = own, swap(ready, "col", 1), near, far
        if sent is not None:
            pieces[-1] += exchange(sent)
            blocks, _ = lax.optimization_barrier((blocks, sent))
        away = product(matrix, blocks, 0, jnp.bfloat16, wait[0])
        stay = product(matrix, blocks, 1, jnp.float32, wait[1])
        kept, *sent = join(stay, swap(away, "row", 1), own_rows)
        pieces.append([kept])
    pieces[-1] += exchange(sent)
    return finish(projected, target_norm, pieces)


def solution(mesh):
    in_specs = (
        P(("row", "col"), None),
        P(),
        P(("row", "col")),
        P(("row", "col")),
        P(("row", "col"), None, None, None),
        P(("row", "col"), None),
        P(("row", "col"), None),
        P(("row", "col")),
        P(("row", "col"), None),
    )
    out_specs = P(("row", "col"), None)
    return jax.shard_map(
        per_device, mesh=mesh, in_specs=in_specs, out_specs=out_specs, check_vma=False
    )
```

```python
import functools

import jax
import jax.numpy as jnp
from jax import lax
from jax.experimental import pallas as pl
from jax.experimental.pallas import tpu as pltpu
from jax.sharding import PartitionSpec as P

DENSE_ELEMENTS = 4 * 1024 * 1024
CHUNKS = 2
WEIGHTS = ((20, 20), (0, 20))
MIB = 1024 * 1024
SMEM = pl.BlockSpec(memory_space=pltpu.SMEM)
VMEM = pl.BlockSpec(memory_space=pltpu.VMEM)
HBM = pl.BlockSpec(memory_space=pltpu.HBM)


def params(mib):
    return pltpu.CompilerParams(vmem_limit_bytes=int(mib * MIB))


def cost(flops, moved):
    return pl.CostEstimate(flops=flops, bytes_accessed=moved, transcendentals=0)


def in_hbm(*values):
    return [pltpu.with_memory_space_constraint(value, pltpu.HBM) for value in values]


def rows_to_lanes(row, lanes):
    return jnp.broadcast_to(row, (lanes, row.shape[1])).T


def project_kernel(features_hbm, weight_hbm, norm_hbm, projected, *refs):
    *scaled, features, weight, norm, sems = refs
    copies = [
        pltpu.make_async_copy(source, target, sems.at[k])
        for k, (source, target) in enumerate(
            [(weight_hbm, weight), (features_hbm, features), (norm_hbm, norm)]
        )
    ]
    for copy in copies:
        copy.start()
    for copy in copies:
        copy.wait()
    lanes = norm.shape[1]
    value = jnp.dot(features[...], weight[...], preferred_element_type=jnp.float32)
    projected[...] = value
    width = scaled[0].shape[1]
    for part in range(norm.shape[0]):
        factor = rows_to_lanes(norm[part : part + 1, :], lanes)
        for column in range(0, value.shape[1], lanes):
            piece = value[part * lanes : (part + 1) * lanes, column : column + lanes]
            target = scaled[column // width]
            start = column % width
            target[part * lanes : (part + 1) * lanes, start : start + lanes] = (
                factor * piece
            ).astype(target.dtype)


def project(features, weight, source_norm, chunks):
    rows, depth = features.shape
    hidden = weight.shape[1]
    norm = source_norm.reshape(-1, 128)
    return pl.pallas_call(
        project_kernel,
        out_shape=[jax.ShapeDtypeStruct((rows, hidden), jnp.float32)]
        + [jax.ShapeDtypeStruct((rows, hidden // chunks), jnp.bfloat16)] * chunks,
        in_specs=[HBM] * 3,
        out_specs=[VMEM] * (1 + chunks),
        scratch_shapes=[
            pltpu.VMEM(features.shape, features.dtype),
            pltpu.VMEM(weight.shape, weight.dtype),
            pltpu.VMEM(norm.shape, norm.dtype),
            pltpu.SemaphoreType.DMA((3,)),
        ],
        compiler_params=params(12),
        cost_estimate=cost(2 * rows * depth * hidden, 2 * depth * (rows + hidden)),
    )(*in_hbm(features, weight, norm))


def merge_kernel(
    own_tiles, per_owner, row, column, count, sources_hbm, targets_hbm, labels_hbm, tiles_hbm, out,
    total, tiles, sources, targets, labels, sems, tile_sems,
):
    small = [
        pltpu.make_async_copy(source, target, sems.at[k])
        for k, (source, target) in enumerate(
            [(sources_hbm, sources), (targets_hbm, targets), (labels_hbm, labels)]
        )
    ]
    parts = tile_sems.shape[0]
    each = tiles.shape[0] // parts
    large = [
        pltpu.make_async_copy(
            tiles_hbm.at[0, pl.ds(k * each, each)],
            tiles.at[pl.ds(k * each, each)],
            tile_sems.at[k],
        )
        for k in range(parts)
    ]
    for copy in small + large:
        copy.start()
    spare, span = total.shape[0] - 1, total.shape[1]
    total[...] = jnp.zeros_like(total)
    my_row, my_column, used = row[0], column[0], count[0]
    for copy in small:
        copy.wait()

    def add(slot):
        target, source = targets[0, slot], sources[0, slot]
        label = labels[0, target]
        owner = target // per_owner
        apart = lax.bitwise_xor(owner, my_row)
        core = label // (own_tiles // 2)
        x, y = apart // 2 % 2, apart // 4
        first, second = jnp.where(core == 0, x, y), jnp.where(core == 0, y, x)
        place = jnp.where(core == my_row % 2, 8, 0) + (1 - first) * 4 + (1 - second) * 2
        place += jnp.where(owner % 2 == core, 1, 0)
        place = place * (own_tiles // 2) + label % (own_tiles // 2)
        place = jnp.where(label < own_tiles, place, spare)
        block = lax.bitwise_xor(source // own_tiles, my_column)
        total[place, block * own_tiles + source % own_tiles] += tiles[slot].astype(jnp.float32)

    for k, copy in enumerate(large):
        copy.wait()
        pl.loop(k * each, jnp.minimum(used, (k + 1) * each))(add)

    rows = total.shape[2]
    for source in range(span):
        for place in range(spare):
            out[place * rows : (place + 1) * rows, source * rows : (source + 1) * rows] = total[
                place, source
            ].astype(out.dtype)


def merge_tiles(own_tiles, owners, span, index_args, tile_weights):
    sources, targets, count, labels = index_args
    _, capacity, rows, _ = tile_weights.shape
    places = owners * own_tiles
    row = lax.axis_index("row").astype(jnp.int32).reshape(1)
    column = lax.axis_index("col").astype(jnp.int32).reshape(1)
    return pl.pallas_call(
        functools.partial(merge_kernel, own_tiles, labels.shape[1] // owners),
        out_shape=jax.ShapeDtypeStruct((places * rows, span * rows), jnp.bfloat16),
        in_specs=[SMEM] * 3 + [HBM] * 4,
        out_specs=VMEM,
        scratch_shapes=[
            pltpu.VMEM((places + 1, span, rows, rows), jnp.float32),
            pltpu.VMEM(tile_weights.shape[1:], tile_weights.dtype),
            pltpu.SMEM(sources.shape, jnp.int32),
            pltpu.SMEM(targets.shape, jnp.int32),
            pltpu.SMEM(labels.shape, jnp.int32),
            pltpu.SemaphoreType.DMA((3,)),
            pltpu.SemaphoreType.DMA((4 if capacity % 4 == 0 else 1,)),
        ],
        compiler_params=params(24),
        cost_estimate=cost(8 * MIB, 12 * MIB),
    )(row, column, count, *in_hbm(sources, targets, labels, tile_weights))


def product_kernel(first, matrix, *refs):
    *blocks, out, gathered = refs
    rows = blocks[0].shape[0]
    for k, block in enumerate(blocks):
        gathered[k * rows : (k + 1) * rows, :] = block[...]
    value = jnp.dot(
        matrix[first : first + out.shape[0], :],
        gathered[...],
        preferred_element_type=jnp.float32,
    )
    out[...] = value.astype(out.dtype)


def product(matrix, blocks, half, dtype, weight):
    rows, width = blocks[0].shape
    total, depth = matrix.shape
    return pl.pallas_call(
        functools.partial(product_kernel, half * (total // 2)),
        out_shape=jax.ShapeDtypeStruct((total // 2, width), dtype),
        in_specs=[VMEM] * (1 + len(blocks)),
        out_specs=VMEM,
        scratch_shapes=[pltpu.VMEM((depth, width), blocks[0].dtype)],
        compiler_params=params(16),
        cost_estimate=cost(weight * total * depth * width, 1),
    )(matrix, *blocks)


def join_kernel(stay, came, sent, kept):
    value = stay[...] + came[...].astype(jnp.float32)
    away = sent.shape[0]
    sent[...] = value[:away].astype(sent.dtype)
    kept[...] = value[away:]


def join(stay, came):
    rows, width = stay.shape
    return pl.pallas_call(
        join_kernel,
        out_shape=[
            jax.ShapeDtypeStruct((rows // 2, width), jnp.bfloat16),
            jax.ShapeDtypeStruct((rows // 2, width), jnp.float32),
        ],
        in_specs=[VMEM] * 2,
        out_specs=[VMEM] * 2,
        compiler_params=params(12),
        cost_estimate=cost(1, 1),
    )(stay, came)


def finish_kernel(row, projected, norm, *refs):
    *pieces, out = refs
    lanes = norm.shape[1]
    half, width = pieces[0].shape
    core = row[0] % 2
    for part in range(2):
        base = (core if part == 0 else 1 - core) * half
        for step in range(0, half, lanes):
            here = pl.ds(pl.multiple_of(base + step, lanes), lanes)
            factor = rows_to_lanes(norm[pl.ds(base // lanes + step // lanes, 1), :], lanes)
            for column in range(0, out.shape[1], lanes):
                piece = pieces[column // width * 2 + part]
                start = column % width
                value = projected[here, column : column + lanes] + piece[
                    step : step + lanes, start : start + lanes
                ].astype(jnp.float32)
                out[here, column : column + lanes] = jnp.maximum(factor * value, 0.0).astype(
                    out.dtype
                )


def finish(row, projected, target_norm, pieces):
    rows, hidden = projected.shape
    return pl.pallas_call(
        finish_kernel,
        out_shape=jax.ShapeDtypeStruct((rows, hidden), jnp.bfloat16),
        in_specs=[SMEM] + [VMEM] * (2 + len(pieces)),
        out_specs=VMEM,
        compiler_params=params(12),
        cost_estimate=cost(6 * rows * hidden, 16 * rows * hidden),
    )(row, projected, target_norm.reshape(-1, 128), *pieces)


def visit_kernel(own_tiles, per_owner, sources, targets, count, labels, tiles, blocks, out, total):
    spare, rows = total.shape[0] - 1, total.shape[1]
    total[...] = jnp.zeros_like(total)

    @pl.loop(0, count[0])
    def _(slot):
        target = targets[0, slot]
        label = labels[0, target]
        place = jnp.where(label < own_tiles, target // per_owner * own_tiles + label, spare)
        start = pl.multiple_of(sources[0, slot] * rows, rows)
        total[place] += jnp.dot(
            tiles[0, slot], blocks[pl.ds(start, rows), :], preferred_element_type=jnp.float32
        )

    @pl.loop(0, spare)
    def _(place):
        out[pl.ds(pl.multiple_of(place * rows, rows), rows), :] = total[place].astype(out.dtype)


def visit_tiles(own_tiles, owners, index_args, tile_weights, blocks):
    slots = index_args[-1].shape[1]
    rows = tile_weights.shape[-1]
    places = owners * own_tiles
    hidden = blocks.shape[1]
    return pl.pallas_call(
        functools.partial(visit_kernel, own_tiles, slots // owners),
        out_shape=jax.ShapeDtypeStruct((places * rows, hidden), jnp.bfloat16),
        in_specs=[SMEM] * 4 + [VMEM] * 2,
        out_specs=VMEM,
        scratch_shapes=[pltpu.VMEM((places + 1, rows, hidden), jnp.float32)],
        compiler_params=params(56),
    )(*index_args, tile_weights, blocks)


def swap(value, axis, apart):
    pairs = [(i, i ^ apart) for i in range(lax.axis_size(axis))]
    return lax.ppermute(value, axis, pairs)


def swap_round(value, round_):
    owners = lax.axis_size("row")
    pairs = [(i, i ^ (2 if (i + round_) % 2 == 0 else 4)) for i in range(owners)]
    return lax.ppermute(value, "row", pairs)


def per_device(
    features,
    weight,
    source_norm,
    target_norm,
    tile_weights,
    tile_source,
    tile_target,
    tile_count,
    mirror_tile,
):
    tile_rows = tile_weights.shape[-1]
    own_rows = features.shape[0]
    own_tiles = own_rows // tile_rows
    owners, columns = lax.axis_size("row"), lax.axis_size("col")
    span = own_tiles * columns
    index_args = (tile_source, tile_target, tile_count, mirror_tile)

    cells = owners * own_tiles * span * tile_rows * tile_rows
    if columns != 4 or owners != 8 or own_tiles % 2 or cells > DENSE_ELEMENTS:
        projected = jnp.dot(features, weight, preferred_element_type=jnp.float32)
        scaled = (source_norm[:, None] * projected).astype(jnp.bfloat16)
        blocks = lax.all_gather(scaled, "col", axis=0, tiled=True)
        partial_value = visit_tiles(own_tiles, owners, index_args, tile_weights, blocks)
        outgoing = partial_value.reshape(owners, own_rows, -1)
        arrived = lax.all_to_all(outgoing, "row", split_axis=0, concat_axis=0, tiled=True)
        gathered = jnp.sum(arrived.astype(jnp.float32), axis=0) + projected
        return jnp.maximum(target_norm[:, None] * gathered, 0.0).astype(jnp.bfloat16)

    projected, *scaled = project(features, weight, source_norm, CHUNKS)
    matrix = merge_tiles(own_tiles, owners, span, index_args, tile_weights)
    across = [swap(own, "col", 3) for own in scaled]
    across[0], matrix = lax.optimization_barrier((across[0], matrix))
    passed = [swap(value, "col", 1) for value in across]
    pieces, sent = [], None
    for own, far, near, wait in zip(scaled, across, passed, WEIGHTS):
        ready = own
        if sent is not None:
            ready, _ = lax.optimization_barrier((own, away))
        blocks = own, swap(ready, "col", 1), near, far
        if sent is not None:
            blocks, _ = lax.optimization_barrier((blocks, sent))
        away = product(matrix, blocks, 0, jnp.bfloat16, wait[0])
        stay = product(matrix, blocks, 1, jnp.float32, wait[1])
        sent, kept = join(stay, swap(away, "row", 1))
        last, kept = join(kept, swap_round(sent, 0))
        last, kept = join(kept, swap_round(last, 1))
        pieces += [kept, swap(last, "row", 1)]
    row = lax.axis_index("row").astype(jnp.int32).reshape(1)
    return finish(row, projected, target_norm, pieces)


def solution(mesh):
    in_specs = (
        P(("row", "col"), None),
        P(),
        P(("row", "col")),
        P(("row", "col")),
        P(("row", "col"), None, None, None),
        P(("row", "col"), None),
        P(("row", "col"), None),
        P(("row", "col")),
        P(("row", "col"), None),
    )
    out_specs = P(("row", "col"), None)
    return jax.shard_map(
        per_device, mesh=mesh, in_specs=in_specs, out_specs=out_specs, check_vma=False
    )
```

```python
import functools

import jax
import jax.numpy as jnp
from jax import lax
from jax.experimental import pallas as pl
from jax.experimental.pallas import tpu as pltpu
from jax.sharding import PartitionSpec as P

DENSE_ELEMENTS = 4 * 1024 * 1024
CHUNKS = 2
WEIGHTS = ((20, 20), (0, 20))
MIB = 1024 * 1024
SMEM = pl.BlockSpec(memory_space=pltpu.SMEM)
VMEM = pl.BlockSpec(memory_space=pltpu.VMEM)
HBM = pl.BlockSpec(memory_space=pltpu.HBM)


def params(mib):
    return pltpu.CompilerParams(vmem_limit_bytes=int(mib * MIB))


def cost(flops, moved):
    return pl.CostEstimate(flops=flops, bytes_accessed=moved, transcendentals=0)


def in_hbm(*values):
    return [pltpu.with_memory_space_constraint(value, pltpu.HBM) for value in values]


def rows_to_lanes(row, lanes):
    return jnp.broadcast_to(row, (lanes, row.shape[1])).T


def project_kernel(features_hbm, weight_hbm, norm_hbm, projected, *refs):
    *scaled, features, weight, norm, sems = refs
    copies = [
        pltpu.make_async_copy(source, target, sems.at[k])
        for k, (source, target) in enumerate(
            [(weight_hbm, weight), (features_hbm, features), (norm_hbm, norm)]
        )
    ]
    for copy in copies:
        copy.start()
    for copy in copies:
        copy.wait()
    lanes = norm.shape[1]
    value = jnp.dot(features[...], weight[...], preferred_element_type=jnp.float32)
    projected[...] = value
    width = scaled[0].shape[1]
    for part in range(norm.shape[0]):
        factor = rows_to_lanes(norm[part : part + 1, :], lanes)
        for column in range(0, value.shape[1], lanes):
            piece = value[part * lanes : (part + 1) * lanes, column : column + lanes]
            target = scaled[column // width]
            start = column % width
            target[part * lanes : (part + 1) * lanes, start : start + lanes] = (
                factor * piece
            ).astype(target.dtype)


def project(features, weight, source_norm, chunks):
    rows, depth = features.shape
    hidden = weight.shape[1]
    norm = source_norm.reshape(-1, 128)
    return pl.pallas_call(
        project_kernel,
        out_shape=[jax.ShapeDtypeStruct((rows, hidden), jnp.float32)]
        + [jax.ShapeDtypeStruct((rows, hidden // chunks), jnp.bfloat16)] * chunks,
        in_specs=[HBM] * 3,
        out_specs=[VMEM] * (1 + chunks),
        scratch_shapes=[
            pltpu.VMEM(features.shape, features.dtype),
            pltpu.VMEM(weight.shape, weight.dtype),
            pltpu.VMEM(norm.shape, norm.dtype),
            pltpu.SemaphoreType.DMA((3,)),
        ],
        compiler_params=params(12),
        cost_estimate=cost(2 * rows * depth * hidden, 2 * depth * (rows + hidden)),
    )(*in_hbm(features, weight, norm))


def merge_kernel(
    own_tiles, per_owner, row, column, count, sources_hbm, targets_hbm, labels_hbm, tiles_hbm, out,
    total, tiles, sources, targets, labels, sems, tile_sems,
):
    small = [
        pltpu.make_async_copy(source, target, sems.at[k])
        for k, (source, target) in enumerate(
            [(sources_hbm, sources), (targets_hbm, targets), (labels_hbm, labels)]
        )
    ]
    parts = tile_sems.shape[0]
    each = tiles.shape[0] // parts
    large = [
        pltpu.make_async_copy(
            tiles_hbm.at[0, pl.ds(k * each, each)],
            tiles.at[pl.ds(k * each, each)],
            tile_sems.at[k],
        )
        for k in range(parts)
    ]
    for copy in small + large:
        copy.start()
    spare, span = total.shape[0] - 1, total.shape[1]
    total[...] = jnp.zeros_like(total)
    my_row, my_column, used = row[0], column[0], count[0]
    for copy in small:
        copy.wait()

    def add(slot):
        target, source = targets[0, slot], sources[0, slot]
        label = labels[0, target]
        owner = target // per_owner
        core, apart = owner % 2, lax.bitwise_xor(owner, my_row)
        x, y = apart // 2 % 2, apart // 4
        first, second = jnp.where(core == 0, x, y), jnp.where(core == 0, y, x)
        position = jnp.where(core == my_row % 2, 4, 0) + second * 2 + first
        place = jnp.where(label < own_tiles, position * own_tiles + label, spare)
        block = lax.bitwise_xor(source // own_tiles, my_column)
        total[place, block * own_tiles + source % own_tiles] += tiles[slot].astype(jnp.float32)

    for k, copy in enumerate(large):
        copy.wait()
        pl.loop(k * each, jnp.minimum(used, (k + 1) * each))(add)

    rows = total.shape[2]
    for source in range(span):
        for place in range(spare):
            out[place * rows : (place + 1) * rows, source * rows : (source + 1) * rows] = total[
                place, source
            ].astype(out.dtype)


def merge_tiles(own_tiles, owners, span, index_args, tile_weights):
    sources, targets, count, labels = index_args
    _, capacity, rows, _ = tile_weights.shape
    places = owners * own_tiles
    row = lax.axis_index("row").astype(jnp.int32).reshape(1)
    column = lax.axis_index("col").astype(jnp.int32).reshape(1)
    return pl.pallas_call(
        functools.partial(merge_kernel, own_tiles, labels.shape[1] // owners),
        out_shape=jax.ShapeDtypeStruct((places * rows, span * rows), jnp.bfloat16),
        in_specs=[SMEM] * 3 + [HBM] * 4,
        out_specs=VMEM,
        scratch_shapes=[
            pltpu.VMEM((places + 1, span, rows, rows), jnp.float32),
            pltpu.VMEM(tile_weights.shape[1:], tile_weights.dtype),
            pltpu.SMEM(sources.shape, jnp.int32),
            pltpu.SMEM(targets.shape, jnp.int32),
            pltpu.SMEM(labels.shape, jnp.int32),
            pltpu.SemaphoreType.DMA((3,)),
            pltpu.SemaphoreType.DMA((4 if capacity % 4 == 0 else 1,)),
        ],
        compiler_params=params(24),
        cost_estimate=cost(8 * MIB, 12 * MIB),
    )(row, column, count, *in_hbm(sources, targets, labels, tile_weights))


def product_kernel(first, matrix, *refs):
    *blocks, out, gathered = refs
    rows = blocks[0].shape[0]
    for k, block in enumerate(blocks):
        gathered[k * rows : (k + 1) * rows, :] = block[...]
    value = jnp.dot(
        matrix[first : first + out.shape[0], :],
        gathered[...],
        preferred_element_type=jnp.float32,
    )
    out[...] = value.astype(out.dtype)


def product(matrix, blocks, half, dtype, weight):
    rows, width = blocks[0].shape
    total, depth = matrix.shape
    return pl.pallas_call(
        functools.partial(product_kernel, half * (total // 2)),
        out_shape=jax.ShapeDtypeStruct((total // 2, width), dtype),
        in_specs=[VMEM] * (1 + len(blocks)),
        out_specs=VMEM,
        scratch_shapes=[pltpu.VMEM((depth, width), blocks[0].dtype)],
        compiler_params=params(16),
        cost_estimate=cost(weight * total * depth * width, 1),
    )(matrix, *blocks)


def join_kernel(stay, came, kept, *sent):
    rows = kept.shape[0]
    value = stay[...].astype(jnp.float32) + came[...].astype(jnp.float32)
    kept[...] = value[:rows]
    for place, out in enumerate(sent):
        out[...] = value[(place + 1) * rows : (place + 2) * rows].astype(out.dtype)


def join(stay, came, rows):
    total, width = stay.shape
    parts = total // rows
    return pl.pallas_call(
        join_kernel,
        out_shape=[jax.ShapeDtypeStruct((rows, width), jnp.float32)]
        + [jax.ShapeDtypeStruct((rows, width), jnp.bfloat16)] * (parts - 1),
        in_specs=[VMEM] * 2,
        out_specs=[VMEM] * parts,
        compiler_params=params(12),
        cost_estimate=cost(1, 1),
    )(stay, came)


def finish_kernel(chunks, projected, norm, *refs):
    out = refs[-1]
    per_chunk = (len(refs) - 1) // chunks
    lanes = norm.shape[1]
    width = refs[0].shape[1]
    for part in range(norm.shape[0]):
        factor = rows_to_lanes(norm[part : part + 1, :], lanes)
        here = slice(part * lanes, (part + 1) * lanes)
        for column in range(0, out.shape[1], lanes):
            pieces = refs[column // width * per_chunk : (column // width + 1) * per_chunk]
            start = column % width
            value = projected[here, column : column + lanes]
            for piece in pieces:
                value += piece[here, start : start + lanes].astype(jnp.float32)
            out[here, column : column + lanes] = jnp.maximum(factor * value, 0.0).astype(out.dtype)


def finish(projected, target_norm, pieces):
    rows, hidden = projected.shape
    flat = [piece for chunk in pieces for piece in chunk]
    return pl.pallas_call(
        functools.partial(finish_kernel, len(pieces)),
        out_shape=jax.ShapeDtypeStruct((rows, hidden), jnp.bfloat16),
        in_specs=[VMEM] * (2 + len(flat)),
        out_specs=VMEM,
        compiler_params=params(12),
        cost_estimate=cost(6 * rows * hidden, 16 * rows * hidden),
    )(projected, target_norm.reshape(-1, 128), *flat)


def visit_kernel(own_tiles, per_owner, sources, targets, count, labels, tiles, blocks, out, total):
    spare, rows = total.shape[0] - 1, total.shape[1]
    total[...] = jnp.zeros_like(total)

    @pl.loop(0, count[0])
    def _(slot):
        target = targets[0, slot]
        label = labels[0, target]
        place = jnp.where(label < own_tiles, target // per_owner * own_tiles + label, spare)
        start = pl.multiple_of(sources[0, slot] * rows, rows)
        total[place] += jnp.dot(
            tiles[0, slot], blocks[pl.ds(start, rows), :], preferred_element_type=jnp.float32
        )

    @pl.loop(0, spare)
    def _(place):
        out[pl.ds(pl.multiple_of(place * rows, rows), rows), :] = total[place].astype(out.dtype)


def visit_tiles(own_tiles, owners, index_args, tile_weights, blocks):
    slots = index_args[-1].shape[1]
    rows = tile_weights.shape[-1]
    places = owners * own_tiles
    hidden = blocks.shape[1]
    return pl.pallas_call(
        functools.partial(visit_kernel, own_tiles, slots // owners),
        out_shape=jax.ShapeDtypeStruct((places * rows, hidden), jnp.bfloat16),
        in_specs=[SMEM] * 4 + [VMEM] * 2,
        out_specs=VMEM,
        scratch_shapes=[pltpu.VMEM((places + 1, rows, hidden), jnp.float32)],
        compiler_params=params(56),
    )(*index_args, tile_weights, blocks)


def swap(value, axis, apart):
    pairs = [(i, i ^ apart) for i in range(lax.axis_size(axis))]
    return lax.ppermute(value, axis, pairs)


def exchange(sent):
    owners = lax.axis_size("row")
    steps = [(2, 4), (4, 2), (6, 6)]
    return [
        lax.ppermute(value, "row", [(i, i ^ step[i % 2]) for i in range(owners)])
        for value, step in zip(sent, steps)
    ]


def per_device(
    features,
    weight,
    source_norm,
    target_norm,
    tile_weights,
    tile_source,
    tile_target,
    tile_count,
    mirror_tile,
):
    tile_rows = tile_weights.shape[-1]
    own_rows = features.shape[0]
    own_tiles = own_rows // tile_rows
    owners, columns = lax.axis_size("row"), lax.axis_size("col")
    span = own_tiles * columns
    index_args = (tile_source, tile_target, tile_count, mirror_tile)

    cells = owners * own_tiles * span * tile_rows * tile_rows
    if columns != 4 or owners != 8 or cells > DENSE_ELEMENTS:
        projected = jnp.dot(features, weight, preferred_element_type=jnp.float32)
        scaled = (source_norm[:, None] * projected).astype(jnp.bfloat16)
        blocks = lax.all_gather(scaled, "col", axis=0, tiled=True)
        partial_value = visit_tiles(own_tiles, owners, index_args, tile_weights, blocks)
        outgoing = partial_value.reshape(owners, own_rows, -1)
        arrived = lax.all_to_all(outgoing, "row", split_axis=0, concat_axis=0, tiled=True)
        gathered = jnp.sum(arrived.astype(jnp.float32), axis=0) + projected
        return jnp.maximum(target_norm[:, None] * gathered, 0.0).astype(jnp.bfloat16)

    projected, *scaled = project(features, weight, source_norm, CHUNKS)
    matrix = merge_tiles(own_tiles, owners, span, index_args, tile_weights)
    across = [swap(own, "col", 3) for own in scaled]
    beside = [swap(own, "col", 1) for own in scaled]
    across[0], matrix = lax.optimization_barrier((across[0], matrix))
    passed = [swap(value, "col", 1) for value in across]
    pieces, sent = [], None
    for blocks, wait in zip(zip(scaled, beside, passed, across), WEIGHTS):
        if sent is not None:
            pieces[-1] += exchange(sent)
            blocks, _ = lax.optimization_barrier((blocks, sent))
        away = product(matrix, blocks, 0, jnp.bfloat16, wait[0])
        stay = product(matrix, blocks, 1, jnp.float32, wait[1])
        kept, *sent = join(stay, swap(away, "row", 1), own_rows)
        pieces.append([kept])
    pieces[-1] += exchange(sent)
    return finish(projected, target_norm, pieces)


def solution(mesh):
    in_specs = (
        P(("row", "col"), None),
        P(),
        P(("row", "col")),
        P(("row", "col")),
        P(("row", "col"), None, None, None),
        P(("row", "col"), None),
        P(("row", "col"), None),
        P(("row", "col")),
        P(("row", "col"), None),
    )
    out_specs = P(("row", "col"), None)
    return jax.shard_map(
        per_device, mesh=mesh, in_specs=in_specs, out_specs=out_specs, check_vma=False
    )
```

```python
import functools

import jax
import jax.numpy as jnp
from jax import lax
from jax.experimental import pallas as pl
from jax.experimental.pallas import tpu as pltpu
from jax.sharding import PartitionSpec as P

DENSE_ELEMENTS = 4 * 1024 * 1024
CHUNKS = 2
WEIGHTS = ((20, 20), (0, 20))
MIB = 1024 * 1024
SMEM = pl.BlockSpec(memory_space=pltpu.SMEM)
VMEM = pl.BlockSpec(memory_space=pltpu.VMEM)
HBM = pl.BlockSpec(memory_space=pltpu.HBM)


def params(mib):
    return pltpu.CompilerParams(vmem_limit_bytes=int(mib * MIB))


def cost(flops, moved):
    return pl.CostEstimate(flops=flops, bytes_accessed=moved, transcendentals=0)


def in_hbm(*values):
    return [pltpu.with_memory_space_constraint(value, pltpu.HBM) for value in values]


def rows_to_lanes(row, lanes):
    return jnp.broadcast_to(row, (lanes, row.shape[1])).T


def project_kernel(features_hbm, weight_hbm, norm_hbm, projected, *refs):
    *scaled, features, weight, norm, sems = refs
    copies = [
        pltpu.make_async_copy(source, target, sems.at[k])
        for k, (source, target) in enumerate(
            [(weight_hbm, weight), (features_hbm, features), (norm_hbm, norm)]
        )
    ]
    for copy in copies:
        copy.start()
    for copy in copies:
        copy.wait()
    lanes = norm.shape[1]
    value = jnp.dot(features[...], weight[...], preferred_element_type=jnp.float32)
    projected[...] = value
    width = scaled[0].shape[1]
    for part in range(norm.shape[0]):
        factor = rows_to_lanes(norm[part : part + 1, :], lanes)
        for column in range(0, value.shape[1], lanes):
            piece = value[part * lanes : (part + 1) * lanes, column : column + lanes]
            target = scaled[column // width]
            start = column % width
            target[part * lanes : (part + 1) * lanes, start : start + lanes] = (
                factor * piece
            ).astype(target.dtype)


def project(features, weight, source_norm, chunks):
    rows, depth = features.shape
    hidden = weight.shape[1]
    norm = source_norm.reshape(-1, 128)
    return pl.pallas_call(
        project_kernel,
        out_shape=[jax.ShapeDtypeStruct((rows, hidden), jnp.float32)]
        + [jax.ShapeDtypeStruct((rows, hidden // chunks), jnp.bfloat16)] * chunks,
        in_specs=[HBM] * 3,
        out_specs=[VMEM] * (1 + chunks),
        scratch_shapes=[
            pltpu.VMEM(features.shape, features.dtype),
            pltpu.VMEM(weight.shape, weight.dtype),
            pltpu.VMEM(norm.shape, norm.dtype),
            pltpu.SemaphoreType.DMA((3,)),
        ],
        compiler_params=params(12),
        cost_estimate=cost(2 * rows * depth * hidden, 2 * depth * (rows + hidden)),
    )(*in_hbm(features, weight, norm))


def merge_kernel(
    own_tiles, per_owner, row, column, count, sources_hbm, targets_hbm, labels_hbm, tiles_hbm, out,
    total, tiles, sources, targets, labels, sems, tile_sems,
):
    small = [
        pltpu.make_async_copy(source, target, sems.at[k])
        for k, (source, target) in enumerate(
            [(sources_hbm, sources), (targets_hbm, targets), (labels_hbm, labels)]
        )
    ]
    parts = tile_sems.shape[0]
    each = tiles.shape[0] // parts
    large = [
        pltpu.make_async_copy(
            tiles_hbm.at[0, pl.ds(k * each, each)],
            tiles.at[pl.ds(k * each, each)],
            tile_sems.at[k],
        )
        for k in range(parts)
    ]
    for copy in small + large:
        copy.start()
    spare, span = total.shape[0] - 1, total.shape[1]
    total[...] = jnp.zeros_like(total)
    my_row, my_column, used = row[0], column[0], count[0]
    for copy in small:
        copy.wait()

    def add(slot):
        target, source = targets[0, slot], sources[0, slot]
        label = labels[0, target]
        owner = target // per_owner
        core, apart = owner % 2, lax.bitwise_xor(owner, my_row)
        x, y = apart // 2 % 2, apart // 4
        first, second = jnp.where(core == 0, x, y), jnp.where(core == 0, y, x)
        position = jnp.where(core == my_row % 2, 4, 0) + second * 2 + first
        place = jnp.where(label < own_tiles, position * own_tiles + label, spare)
        block = lax.bitwise_xor(source // own_tiles, my_column)
        total[place, block * own_tiles + source % own_tiles] += tiles[slot].astype(jnp.float32)

    for k, copy in enumerate(large):
        copy.wait()
        pl.loop(k * each, jnp.minimum(used, (k + 1) * each))(add)

    rows = total.shape[2]
    for source in range(span):
        for place in range(spare):
            out[place * rows : (place + 1) * rows, source * rows : (source + 1) * rows] = total[
                place, source
            ].astype(out.dtype)


def merge_tiles(own_tiles, owners, span, index_args, tile_weights):
    sources, targets, count, labels = index_args
    _, capacity, rows, _ = tile_weights.shape
    places = owners * own_tiles
    row = lax.axis_index("row").astype(jnp.int32).reshape(1)
    column = lax.axis_index("col").astype(jnp.int32).reshape(1)
    return pl.pallas_call(
        functools.partial(merge_kernel, own_tiles, labels.shape[1] // owners),
        out_shape=jax.ShapeDtypeStruct((places * rows, span * rows), jnp.bfloat16),
        in_specs=[SMEM] * 3 + [HBM] * 4,
        out_specs=VMEM,
        scratch_shapes=[
            pltpu.VMEM((places + 1, span, rows, rows), jnp.float32),
            pltpu.VMEM(tile_weights.shape[1:], tile_weights.dtype),
            pltpu.SMEM(sources.shape, jnp.int32),
            pltpu.SMEM(targets.shape, jnp.int32),
            pltpu.SMEM(labels.shape, jnp.int32),
            pltpu.SemaphoreType.DMA((3,)),
            pltpu.SemaphoreType.DMA((4 if capacity % 4 == 0 else 1,)),
        ],
        compiler_params=params(24),
        cost_estimate=cost(8 * MIB, 12 * MIB),
    )(row, column, count, *in_hbm(sources, targets, labels, tile_weights))


def early_kernel(matrix, own, beside, across, out):
    rows = own.shape[0]
    value = jnp.dot(matrix[:, :rows], own[...], preferred_element_type=jnp.float32)
    value += jnp.dot(
        matrix[:, rows : 2 * rows], beside[...], preferred_element_type=jnp.float32
    )
    value += jnp.dot(matrix[:, 3 * rows :], across[...], preferred_element_type=jnp.float32)
    out[...] = value


def early_product(matrix, own, beside, across):
    total, depth = matrix.shape
    width = own.shape[1]
    return pl.pallas_call(
        early_kernel,
        out_shape=jax.ShapeDtypeStruct((total, width), jnp.float32),
        in_specs=[VMEM] * 4,
        out_specs=VMEM,
        compiler_params=params(16),
        cost_estimate=cost(20 * total * depth * width, 1),
    )(matrix, own, beside, across)


def late_kernel(first, matrix, early, passed, out):
    rows = passed.shape[0]
    here = slice(first, first + out.shape[0])
    value = early[here, :] + jnp.dot(
        matrix[here, 2 * rows : 3 * rows], passed[...], preferred_element_type=jnp.float32
    )
    out[...] = value.astype(out.dtype)


def late_product(matrix, early, passed, first, count, dtype, weight):
    total, depth = matrix.shape
    width = passed.shape[1]
    return pl.pallas_call(
        functools.partial(late_kernel, first),
        out_shape=jax.ShapeDtypeStruct((count, width), dtype),
        in_specs=[VMEM] * 3,
        out_specs=VMEM,
        compiler_params=params(16),
        cost_estimate=cost(weight * total * depth * width, 1),
    )(matrix, early, passed)


def join_kernel(stay, *refs):
    came, (kept, *sent) = refs[:2], refs[2:]
    rows, half = kept.shape[0], came[0].shape[0]
    for place, out in enumerate([kept] + sent):
        start = place * rows
        other = came[start // half][start % half : start % half + rows, :]
        value = stay[start : start + rows, :] + other.astype(jnp.float32)
        out[...] = value.astype(out.dtype)


def join(stay, came, rows):
    total, width = stay.shape
    parts = total // rows
    return pl.pallas_call(
        join_kernel,
        out_shape=[jax.ShapeDtypeStruct((rows, width), jnp.float32)]
        + [jax.ShapeDtypeStruct((rows, width), jnp.bfloat16)] * (parts - 1),
        in_specs=[VMEM] * 3,
        out_specs=[VMEM] * parts,
        compiler_params=params(12),
        cost_estimate=cost(1, 1),
    )(stay, *came)


def finish_kernel(chunks, projected, norm, *refs):
    out = refs[-1]
    per_chunk = (len(refs) - 1) // chunks
    lanes = norm.shape[1]
    width = refs[0].shape[1]
    for part in range(norm.shape[0]):
        factor = rows_to_lanes(norm[part : part + 1, :], lanes)
        here = slice(part * lanes, (part + 1) * lanes)
        for column in range(0, out.shape[1], lanes):
            pieces = refs[column // width * per_chunk : (column // width + 1) * per_chunk]
            start = column % width
            value = projected[here, column : column + lanes]
            for piece in pieces:
                value += piece[here, start : start + lanes].astype(jnp.float32)
            out[here, column : column + lanes] = jnp.maximum(factor * value, 0.0).astype(out.dtype)


def finish(projected, target_norm, pieces):
    rows, hidden = projected.shape
    flat = [piece for chunk in pieces for piece in chunk]
    return pl.pallas_call(
        functools.partial(finish_kernel, len(pieces)),
        out_shape=jax.ShapeDtypeStruct((rows, hidden), jnp.bfloat16),
        in_specs=[VMEM] * (2 + len(flat)),
        out_specs=VMEM,
        compiler_params=params(12),
        cost_estimate=cost(6 * rows * hidden, 16 * rows * hidden),
    )(projected, target_norm.reshape(-1, 128), *flat)


def visit_kernel(own_tiles, per_owner, sources, targets, count, labels, tiles, blocks, out, total):
    spare, rows = total.shape[0] - 1, total.shape[1]
    total[...] = jnp.zeros_like(total)

    @pl.loop(0, count[0])
    def _(slot):
        target = targets[0, slot]
        label = labels[0, target]
        place = jnp.where(label < own_tiles, target // per_owner * own_tiles + label, spare)
        start = pl.multiple_of(sources[0, slot] * rows, rows)
        total[place] += jnp.dot(
            tiles[0, slot], blocks[pl.ds(start, rows), :], preferred_element_type=jnp.float32
        )

    @pl.loop(0, spare)
    def _(place):
        out[pl.ds(pl.multiple_of(place * rows, rows), rows), :] = total[place].astype(out.dtype)


def visit_tiles(own_tiles, owners, index_args, tile_weights, blocks):
    slots = index_args[-1].shape[1]
    rows = tile_weights.shape[-1]
    places = owners * own_tiles
    hidden = blocks.shape[1]
    return pl.pallas_call(
        functools.partial(visit_kernel, own_tiles, slots // owners),
        out_shape=jax.ShapeDtypeStruct((places * rows, hidden), jnp.bfloat16),
        in_specs=[SMEM] * 4 + [VMEM] * 2,
        out_specs=VMEM,
        scratch_shapes=[pltpu.VMEM((places + 1, rows, hidden), jnp.float32)],
        compiler_params=params(56),
    )(*index_args, tile_weights, blocks)


def swap(value, axis, apart):
    pairs = [(i, i ^ apart) for i in range(lax.axis_size(axis))]
    return lax.ppermute(value, axis, pairs)


def exchange(sent):
    owners = lax.axis_size("row")
    steps = [(2, 4), (4, 2), (6, 6)]
    return [
        lax.ppermute(value, "row", [(i, i ^ step[i % 2]) for i in range(owners)])
        for value, step in zip(sent, steps)
    ]


def per_device(
    features,
    weight,
    source_norm,
    target_norm,
    tile_weights,
    tile_source,
    tile_target,
    tile_count,
    mirror_tile,
):
    tile_rows = tile_weights.shape[-1]
    own_rows = features.shape[0]
    own_tiles = own_rows // tile_rows
    owners, columns = lax.axis_size("row"), lax.axis_size("col")
    span = own_tiles * columns
    index_args = (tile_source, tile_target, tile_count, mirror_tile)

    cells = owners * own_tiles * span * tile_rows * tile_rows
    if columns != 4 or owners != 8 or cells > DENSE_ELEMENTS:
        projected = jnp.dot(features, weight, preferred_element_type=jnp.float32)
        scaled = (source_norm[:, None] * projected).astype(jnp.bfloat16)
        blocks = lax.all_gather(scaled, "col", axis=0, tiled=True)
        partial_value = visit_tiles(own_tiles, owners, index_args, tile_weights, blocks)
        outgoing = partial_value.reshape(owners, own_rows, -1)
        arrived = lax.all_to_all(outgoing, "row", split_axis=0, concat_axis=0, tiled=True)
        gathered = jnp.sum(arrived.astype(jnp.float32), axis=0) + projected
        return jnp.maximum(target_norm[:, None] * gathered, 0.0).astype(jnp.bfloat16)

    projected, *scaled = project(features, weight, source_norm, CHUNKS)
    built = merge_tiles(own_tiles, owners, span, index_args, tile_weights)
    half = built.shape[0] // 2
    across = [swap(own, "col", 3) for own in scaled]
    pieces, sent, away, early = [], None, None, None
    for chunk, (own, far, wait) in enumerate(zip(scaled, across, WEIGHTS)):
        ready, onward = own, far
        if chunk:
            ready, _ = lax.optimization_barrier((own, built))
            onward, _ = lax.optimization_barrier((far, early))
        else:
            onward, matrix = lax.optimization_barrier((far, built))
        last, near = swap(onward, "col", 1), swap(ready, "col", 1)
        if chunk:
            near, _ = lax.optimization_barrier((near, away))
        early = early_product(matrix, own, near, far)
        if chunk:
            pieces[-1] += exchange(sent)
            last, _ = lax.optimization_barrier((last, sent))
        away = [
            late_product(matrix, early, last, k * half // 2, half // 2, jnp.bfloat16, wait[0])
            for k in range(2)
        ]
        stay = late_product(matrix, early, last, half, half, jnp.float32, wait[1])
        kept, *sent = join(stay, [swap(value, "row", 1) for value in away], own_rows)
        pieces.append([kept])
    pieces[-1] += exchange(sent)
    return finish(projected, target_norm, pieces)


def solution(mesh):
    in_specs = (
        P(("row", "col"), None),
        P(),
        P(("row", "col")),
        P(("row", "col")),
        P(("row", "col"), None, None, None),
        P(("row", "col"), None),
        P(("row", "col"), None),
        P(("row", "col")),
        P(("row", "col"), None),
    )
    out_specs = P(("row", "col"), None)
    return jax.shard_map(
        per_device, mesh=mesh, in_specs=in_specs, out_specs=out_specs, check_vma=False
    )
```

```python
import functools

import jax
import jax.numpy as jnp
from jax import lax
from jax.experimental import pallas as pl
from jax.experimental.pallas import tpu as pltpu
from jax.sharding import PartitionSpec as P

DENSE_ELEMENTS = 4 * 1024 * 1024
CHUNKS = 2
WEIGHTS = ((20, 20), (0, 20))
MIB = 1024 * 1024
SMEM = pl.BlockSpec(memory_space=pltpu.SMEM)
VMEM = pl.BlockSpec(memory_space=pltpu.VMEM)
HBM = pl.BlockSpec(memory_space=pltpu.HBM)


def params(mib):
    return pltpu.CompilerParams(vmem_limit_bytes=int(mib * MIB))


def cost(flops, moved):
    return pl.CostEstimate(flops=flops, bytes_accessed=moved, transcendentals=0)


def in_hbm(*values):
    return [pltpu.with_memory_space_constraint(value, pltpu.HBM) for value in values]


def rows_to_lanes(row, lanes):
    return jnp.broadcast_to(row, (lanes, row.shape[1])).T


def project_kernel(features_hbm, weight_hbm, norm_hbm, projected, *refs):
    *scaled, features, weight, norm, sems = refs
    copies = [
        pltpu.make_async_copy(source, target, sems.at[k])
        for k, (source, target) in enumerate(
            [(weight_hbm, weight), (features_hbm, features), (norm_hbm, norm)]
        )
    ]
    for copy in copies:
        copy.start()
    for copy in copies:
        copy.wait()
    lanes = norm.shape[1]
    value = jnp.dot(features[...], weight[...], preferred_element_type=jnp.float32)
    projected[...] = value
    width = scaled[0].shape[1]
    for part in range(norm.shape[0]):
        factor = rows_to_lanes(norm[part : part + 1, :], lanes)
        for column in range(0, value.shape[1], lanes):
            piece = value[part * lanes : (part + 1) * lanes, column : column + lanes]
            target = scaled[column // width]
            start = column % width
            target[part * lanes : (part + 1) * lanes, start : start + lanes] = (
                factor * piece
            ).astype(target.dtype)


def project(features, weight, source_norm, chunks):
    rows, depth = features.shape
    hidden = weight.shape[1]
    norm = source_norm.reshape(-1, 128)
    return pl.pallas_call(
        project_kernel,
        out_shape=[jax.ShapeDtypeStruct((rows, hidden), jnp.float32)]
        + [jax.ShapeDtypeStruct((rows, hidden // chunks), jnp.bfloat16)] * chunks,
        in_specs=[HBM] * 3,
        out_specs=[VMEM] * (1 + chunks),
        scratch_shapes=[
            pltpu.VMEM(features.shape, features.dtype),
            pltpu.VMEM(weight.shape, weight.dtype),
            pltpu.VMEM(norm.shape, norm.dtype),
            pltpu.SemaphoreType.DMA((3,)),
        ],
        compiler_params=params(12),
        cost_estimate=cost(2 * rows * depth * hidden, 2 * depth * (rows + hidden)),
    )(*in_hbm(features, weight, norm))


def merge_kernel(
    own_tiles, per_owner, row, column, count, sources_hbm, targets_hbm, labels_hbm, tiles_hbm, out,
    total, tiles, sources, targets, labels, bases, seen, sems, tile_sems,
):
    small = [
        pltpu.make_async_copy(source, target, sems.at[k])
        for k, (source, target) in enumerate(
            [(sources_hbm, sources), (targets_hbm, targets), (labels_hbm, labels)]
        )
    ]
    parts = tile_sems.shape[0]
    each = tiles.shape[0] // parts
    large = [
        pltpu.make_async_copy(
            tiles_hbm.at[0, pl.ds(k * each, each)],
            tiles.at[pl.ds(k * each, each)],
            tile_sems.at[k],
        )
        for k in range(parts)
    ]
    for copy in small + large:
        copy.start()
    rows = total.shape[1]
    places, span = out.shape[0] // rows, out.shape[1] // rows
    spare = places * span
    for cell in range(spare + 1):
        seen[cell] = 0
    my_core, used = row[0] % 2, count[0]
    toggle = column[0] * own_tiles
    for copy in small:
        copy.wait()

    for slot in range(bases.shape[0]):
        owner, label = slot // per_owner, labels[0, slot]
        core, apart = owner % 2, lax.bitwise_xor(row[0], owner)
        x, y = lax.bitwise_and(apart, 2), lax.bitwise_and(lax.shift_right_logical(apart, 1), 2)
        first, second = (x, y) if core == 0 else (y, x)
        position = jnp.where(my_core == core, 4, 0) + second + lax.shift_right_logical(first, 1)
        base = (position * own_tiles + label) * span
        bases[slot] = jnp.where(label < own_tiles, base, spare)

    def add(slot):
        base = bases[targets[0, slot]]
        here = base + lax.bitwise_xor(sources[0, slot], toggle)
        cell = jnp.where((base < spare) & (slot < used), here, spare)
        before = jnp.where(seen[cell] > 0, total[cell], 0.0)
        seen[cell] = 1
        total[cell] = before + tiles[slot].astype(jnp.float32)

    for k, copy in enumerate(large):
        copy.wait()
        pl.loop(k * each, (k + 1) * each, unroll=4)(add)

    for place in range(places):
        for source in range(span):
            cell = place * span + source
            value = jnp.where(seen[cell] > 0, total[cell], 0.0)
            out[place * rows : (place + 1) * rows, source * rows : (source + 1) * rows] = (
                value.astype(out.dtype)
            )


def merge_tiles(own_tiles, owners, span, index_args, tile_weights):
    sources, targets, count, labels = index_args
    _, capacity, rows, _ = tile_weights.shape
    places = owners * own_tiles
    row = lax.axis_index("row").astype(jnp.int32).reshape(1)
    column = lax.axis_index("col").astype(jnp.int32).reshape(1)
    return pl.pallas_call(
        functools.partial(merge_kernel, own_tiles, labels.shape[1] // owners),
        out_shape=jax.ShapeDtypeStruct((places * rows, span * rows), jnp.bfloat16),
        in_specs=[SMEM] * 3 + [HBM] * 4,
        out_specs=VMEM,
        scratch_shapes=[
            pltpu.VMEM((places * span + 1, rows, rows), jnp.float32),
            pltpu.VMEM(tile_weights.shape[1:], tile_weights.dtype),
            pltpu.SMEM(sources.shape, jnp.int32),
            pltpu.SMEM(targets.shape, jnp.int32),
            pltpu.SMEM(labels.shape, jnp.int32),
            pltpu.SMEM((labels.shape[1],), jnp.int32),
            pltpu.SMEM((places * span + 1,), jnp.int32),
            pltpu.SemaphoreType.DMA((3,)),
            pltpu.SemaphoreType.DMA((4 if capacity % 4 == 0 else 1,)),
        ],
        compiler_params=params(24),
        cost_estimate=cost(8 * MIB, 12 * MIB),
    )(row, column, count, *in_hbm(sources, targets, labels, tile_weights))


def product_kernel(first, matrix, *refs):
    *blocks, out, gathered = refs
    rows = blocks[0].shape[0]
    for k, block in enumerate(blocks):
        gathered[k * rows : (k + 1) * rows, :] = block[...]
    value = jnp.dot(
        matrix[first : first + out.shape[0], :],
        gathered[...],
        preferred_element_type=jnp.float32,
    )
    out[...] = value.astype(out.dtype)


def product(matrix, blocks, half, dtype, weight):
    rows, width = blocks[0].shape
    total, depth = matrix.shape
    return pl.pallas_call(
        functools.partial(product_kernel, half * (total // 2)),
        out_shape=jax.ShapeDtypeStruct((total // 2, width), dtype),
        in_specs=[VMEM] * (1 + len(blocks)),
        out_specs=VMEM,
        scratch_shapes=[pltpu.VMEM((depth, width), blocks[0].dtype)],
        compiler_params=params(16),
        cost_estimate=cost(weight * total * depth * width, 1),
    )(matrix, *blocks)


def join_kernel(stay, came, kept, *sent):
    rows = kept.shape[0]
    value = stay[...].astype(jnp.float32) + came[...].astype(jnp.float32)
    kept[...] = value[:rows]
    for place, out in enumerate(sent):
        out[...] = value[(place + 1) * rows : (place + 2) * rows].astype(out.dtype)


def join(stay, came, rows):
    total, width = stay.shape
    parts = total // rows
    return pl.pallas_call(
        join_kernel,
        out_shape=[jax.ShapeDtypeStruct((rows, width), jnp.float32)]
        + [jax.ShapeDtypeStruct((rows, width), jnp.bfloat16)] * (parts - 1),
        in_specs=[VMEM] * 2,
        out_specs=[VMEM] * parts,
        compiler_params=params(12),
        cost_estimate=cost(1, 1),
    )(stay, came)


def finish_kernel(chunks, projected, norm, *refs):
    out = refs[-1]
    per_chunk = (len(refs) - 1) // chunks
    lanes = norm.shape[1]
    width = refs[0].shape[1]
    for part in range(norm.shape[0]):
        factor = rows_to_lanes(norm[part : part + 1, :], lanes)
        here = slice(part * lanes, (part + 1) * lanes)
        for column in range(0, out.shape[1], lanes):
            pieces = refs[column // width * per_chunk : (column // width + 1) * per_chunk]
            start = column % width
            value = projected[here, column : column + lanes]
            for piece in pieces:
                value += piece[here, start : start + lanes].astype(jnp.float32)
            out[here, column : column + lanes] = jnp.maximum(factor * value, 0.0).astype(out.dtype)


def finish(projected, target_norm, pieces):
    rows, hidden = projected.shape
    flat = [piece for chunk in pieces for piece in chunk]
    return pl.pallas_call(
        functools.partial(finish_kernel, len(pieces)),
        out_shape=jax.ShapeDtypeStruct((rows, hidden), jnp.bfloat16),
        in_specs=[VMEM] * (2 + len(flat)),
        out_specs=VMEM,
        compiler_params=params(12),
        cost_estimate=cost(6 * rows * hidden, 16 * rows * hidden),
    )(projected, target_norm.reshape(-1, 128), *flat)


def visit_kernel(own_tiles, per_owner, sources, targets, count, labels, tiles, blocks, out, total):
    spare, rows = total.shape[0] - 1, total.shape[1]
    total[...] = jnp.zeros_like(total)

    @pl.loop(0, count[0])
    def _(slot):
        target = targets[0, slot]
        label = labels[0, target]
        place = jnp.where(label < own_tiles, target // per_owner * own_tiles + label, spare)
        start = pl.multiple_of(sources[0, slot] * rows, rows)
        total[place] += jnp.dot(
            tiles[0, slot], blocks[pl.ds(start, rows), :], preferred_element_type=jnp.float32
        )

    @pl.loop(0, spare)
    def _(place):
        out[pl.ds(pl.multiple_of(place * rows, rows), rows), :] = total[place].astype(out.dtype)


def visit_tiles(own_tiles, owners, index_args, tile_weights, blocks):
    slots = index_args[-1].shape[1]
    rows = tile_weights.shape[-1]
    places = owners * own_tiles
    hidden = blocks.shape[1]
    return pl.pallas_call(
        functools.partial(visit_kernel, own_tiles, slots // owners),
        out_shape=jax.ShapeDtypeStruct((places * rows, hidden), jnp.bfloat16),
        in_specs=[SMEM] * 4 + [VMEM] * 2,
        out_specs=VMEM,
        scratch_shapes=[pltpu.VMEM((places + 1, rows, hidden), jnp.float32)],
        compiler_params=params(56),
    )(*index_args, tile_weights, blocks)


def swap(value, axis, apart):
    pairs = [(i, i ^ apart) for i in range(lax.axis_size(axis))]
    return lax.ppermute(value, axis, pairs)


def exchange(sent):
    owners = lax.axis_size("row")
    steps = [(2, 4), (4, 2), (6, 6)]
    return [
        lax.ppermute(value, "row", [(i, i ^ step[i % 2]) for i in range(owners)])
        for value, step in zip(sent, steps)
    ]


def per_device(
    features,
    weight,
    source_norm,
    target_norm,
    tile_weights,
    tile_source,
    tile_target,
    tile_count,
    mirror_tile,
):
    tile_rows = tile_weights.shape[-1]
    own_rows = features.shape[0]
    own_tiles = own_rows // tile_rows
    owners, columns = lax.axis_size("row"), lax.axis_size("col")
    span = own_tiles * columns
    index_args = (tile_source, tile_target, tile_count, mirror_tile)

    cells = owners * own_tiles * span * tile_rows * tile_rows
    if columns != 4 or owners != 8 or own_tiles & (own_tiles - 1) or cells > DENSE_ELEMENTS:
        projected = jnp.dot(features, weight, preferred_element_type=jnp.float32)
        scaled = (source_norm[:, None] * projected).astype(jnp.bfloat16)
        blocks = lax.all_gather(scaled, "col", axis=0, tiled=True)
        partial_value = visit_tiles(own_tiles, owners, index_args, tile_weights, blocks)
        outgoing = partial_value.reshape(owners, own_rows, -1)
        arrived = lax.all_to_all(outgoing, "row", split_axis=0, concat_axis=0, tiled=True)
        gathered = jnp.sum(arrived.astype(jnp.float32), axis=0) + projected
        return jnp.maximum(target_norm[:, None] * gathered, 0.0).astype(jnp.bfloat16)

    projected, *scaled = project(features, weight, source_norm, CHUNKS)
    matrix = merge_tiles(own_tiles, owners, span, index_args, tile_weights)
    across = [swap(own, "col", 3) for own in scaled]
    beside = [swap(own, "col", 1) for own in scaled]
    across[0], matrix = lax.optimization_barrier((across[0], matrix))
    passed = [swap(value, "col", 1) for value in across]
    pieces, sent = [], None
    for blocks, wait in zip(zip(scaled, beside, passed, across), WEIGHTS):
        if sent is not None:
            pieces[-1] += exchange(sent)
            blocks, _ = lax.optimization_barrier((blocks, sent))
        away = product(matrix, blocks, 0, jnp.bfloat16, wait[0])
        stay = product(matrix, blocks, 1, jnp.float32, wait[1])
        kept, *sent = join(stay, swap(away, "row", 1), own_rows)
        pieces.append([kept])
    pieces[-1] += exchange(sent)
    return finish(projected, target_norm, pieces)


def solution(mesh):
    in_specs = (
        P(("row", "col"), None),
        P(),
        P(("row", "col")),
        P(("row", "col")),
        P(("row", "col"), None, None, None),
        P(("row", "col"), None),
        P(("row", "col"), None),
        P(("row", "col")),
        P(("row", "col"), None),
    )
    out_specs = P(("row", "col"), None)
    return jax.shard_map(
        per_device, mesh=mesh, in_specs=in_specs, out_specs=out_specs, check_vma=False
    )
```

```python
import functools

import jax
import jax.numpy as jnp
from jax import lax
from jax.experimental import pallas as pl
from jax.experimental.pallas import tpu as pltpu
from jax.sharding import PartitionSpec as P

DENSE_ELEMENTS = 4 * 1024 * 1024
CHUNKS = 2
WEIGHTS = (20, 20, 0, 20)
MIB = 1024 * 1024
SMEM = pl.BlockSpec(memory_space=pltpu.SMEM)
VMEM = pl.BlockSpec(memory_space=pltpu.VMEM)
HBM = pl.BlockSpec(memory_space=pltpu.HBM)


def params(mib):
    return pltpu.CompilerParams(vmem_limit_bytes=int(mib * MIB))


def cost(flops, moved):
    return pl.CostEstimate(flops=flops, bytes_accessed=moved, transcendentals=0)


def in_hbm(*values):
    return [pltpu.with_memory_space_constraint(value, pltpu.HBM) for value in values]


def rows_to_lanes(row, lanes):
    return jnp.broadcast_to(row, (lanes, row.shape[1])).T


def project_kernel(features_hbm, weight_hbm, norm_hbm, projected, *refs):
    *scaled, features, weight, norm, sems = refs
    copies = [
        pltpu.make_async_copy(source, target, sems.at[k])
        for k, (source, target) in enumerate(
            [(weight_hbm, weight), (features_hbm, features), (norm_hbm, norm)]
        )
    ]
    for copy in copies:
        copy.start()
    for copy in copies:
        copy.wait()
    lanes = norm.shape[1]
    value = jnp.dot(features[...], weight[...], preferred_element_type=jnp.float32)
    projected[...] = value
    width = scaled[0].shape[1]
    for part in range(norm.shape[0]):
        factor = rows_to_lanes(norm[part : part + 1, :], lanes)
        for column in range(0, value.shape[1], lanes):
            here = slice(part * lanes, (part + 1) * lanes)
            piece = factor * value[here, column : column + lanes]
            target = scaled[column // width]
            start = column % width
            target[here, start : start + lanes] = piece.astype(target.dtype)


def project(features, weight, source_norm, chunks):
    rows, depth = features.shape
    hidden = weight.shape[1]
    norm = source_norm.reshape(-1, 128)
    return pl.pallas_call(
        project_kernel,
        out_shape=[jax.ShapeDtypeStruct((rows, hidden), jnp.float32)]
        + [jax.ShapeDtypeStruct((rows, hidden // chunks), jnp.bfloat16)] * chunks,
        in_specs=[HBM] * 3,
        out_specs=[VMEM] * (1 + chunks),
        scratch_shapes=[
            pltpu.VMEM(features.shape, features.dtype),
            pltpu.VMEM(weight.shape, weight.dtype),
            pltpu.VMEM(norm.shape, norm.dtype),
            pltpu.SemaphoreType.DMA((3,)),
        ],
        compiler_params=params(12),
        cost_estimate=cost(2 * rows * depth * hidden, 2 * depth * (rows + hidden)),
    )(*in_hbm(features, weight, norm))


def merge_kernel(
    own_tiles, per_owner, row, column, count, sources_hbm, targets_hbm, labels_hbm, tiles_hbm, out,
    total, tiles, sources, targets, labels, bases, seen, sems, tile_sems,
):
    small = [
        pltpu.make_async_copy(source, target, sems.at[k])
        for k, (source, target) in enumerate(
            [(sources_hbm, sources), (targets_hbm, targets), (labels_hbm, labels)]
        )
    ]
    parts = tile_sems.shape[0]
    each = tiles.shape[0] // parts
    large = [
        pltpu.make_async_copy(
            tiles_hbm.at[0, pl.ds(k * each, each)],
            tiles.at[pl.ds(k * each, each)],
            tile_sems.at[k],
        )
        for k in range(parts)
    ]
    for copy in small + large:
        copy.start()
    rows = total.shape[1]
    places, span = out.shape[0] // rows, out.shape[1] // rows
    spare = places * span
    for cell in range(spare + 1):
        seen[cell] = 0
    my_core, used = row[0] % 2, count[0]
    toggle = column[0] * own_tiles
    for copy in small:
        copy.wait()

    for slot in range(bases.shape[0]):
        owner, label = slot // per_owner, labels[0, slot]
        core, apart = owner % 2, lax.bitwise_xor(row[0], owner)
        x, y = lax.bitwise_and(apart, 2), lax.bitwise_and(lax.shift_right_logical(apart, 1), 2)
        first, second = (x, y) if core == 0 else (y, x)
        position = jnp.where(my_core == core, 4, 0) + second + lax.shift_right_logical(first, 1)
        base = (position * own_tiles + label) * span
        bases[slot] = jnp.where(label < own_tiles, base, spare)

    def add(slot):
        base = bases[targets[0, slot]]
        here = base + lax.bitwise_xor(sources[0, slot], toggle)
        cell = jnp.where((base < spare) & (slot < used), here, spare)
        before = jnp.where(seen[cell] > 0, total[cell], 0.0)
        seen[cell] = 1
        total[cell] = before + tiles[slot].astype(jnp.float32)

    for k, copy in enumerate(large):
        copy.wait()
        pl.loop(k * each, (k + 1) * each, unroll=4)(add)

    for place in range(places):
        for source in range(span):
            cell = place * span + source
            value = jnp.where(seen[cell] > 0, total[cell], 0.0)
            out[place * rows : (place + 1) * rows, source * rows : (source + 1) * rows] = (
                value.astype(out.dtype)
            )


def merge_tiles(own_tiles, owners, span, index_args, tile_weights):
    sources, targets, count, labels = index_args
    _, capacity, rows, _ = tile_weights.shape
    places = owners * own_tiles
    row = lax.axis_index("row").astype(jnp.int32).reshape(1)
    column = lax.axis_index("col").astype(jnp.int32).reshape(1)
    return pl.pallas_call(
        functools.partial(merge_kernel, own_tiles, labels.shape[1] // owners),
        out_shape=jax.ShapeDtypeStruct((places * rows, span * rows), jnp.bfloat16),
        in_specs=[SMEM] * 3 + [HBM] * 4,
        out_specs=VMEM,
        scratch_shapes=[
            pltpu.VMEM((places * span + 1, rows, rows), jnp.float32),
            pltpu.VMEM(tile_weights.shape[1:], tile_weights.dtype),
            pltpu.SMEM(sources.shape, jnp.int32),
            pltpu.SMEM(targets.shape, jnp.int32),
            pltpu.SMEM(labels.shape, jnp.int32),
            pltpu.SMEM((labels.shape[1],), jnp.int32),
            pltpu.SMEM((places * span + 1,), jnp.int32),
            pltpu.SemaphoreType.DMA((3,)),
            pltpu.SemaphoreType.DMA((4 if capacity % 4 == 0 else 1,)),
        ],
        compiler_params=params(24),
        cost_estimate=cost(8 * MIB, 12 * MIB),
    )(row, column, count, *in_hbm(sources, targets, labels, tile_weights))


def early_kernel(matrix, own, beside, across, out):
    rows = own.shape[0]
    value = jnp.dot(matrix[:, :rows], own[...], preferred_element_type=jnp.float32)
    value += jnp.dot(
        matrix[:, rows : 2 * rows], beside[...], preferred_element_type=jnp.float32
    )
    value += jnp.dot(matrix[:, 3 * rows :], across[...], preferred_element_type=jnp.float32)
    out[...] = value


def early_product(matrix, own, beside, across):
    total, depth = matrix.shape
    width = own.shape[1]
    return pl.pallas_call(
        early_kernel,
        out_shape=jax.ShapeDtypeStruct((total, width), jnp.float32),
        in_specs=[VMEM] * 4,
        out_specs=VMEM,
        compiler_params=params(16),
        cost_estimate=cost(20 * total * depth * width, 1),
    )(matrix, own, beside, across)


def late_kernel(first, matrix, early, passed, out):
    rows = passed.shape[0]
    here = slice(first, first + out.shape[0])
    value = early[here, :] + jnp.dot(
        matrix[here, 2 * rows : 3 * rows], passed[...], preferred_element_type=jnp.float32
    )
    out[...] = value.astype(out.dtype)


def late_product(matrix, early, passed, first, count, dtype, weight):
    total, depth = matrix.shape
    width = passed.shape[1]
    return pl.pallas_call(
        functools.partial(late_kernel, first),
        out_shape=jax.ShapeDtypeStruct((count, width), dtype),
        in_specs=[VMEM] * 3,
        out_specs=VMEM,
        compiler_params=params(16),
        cost_estimate=cost(weight * total * depth * width, 1),
    )(matrix, early, passed)


def product_kernel(first, matrix, *refs):
    *blocks, out, gathered = refs
    rows = blocks[0].shape[0]
    for k, block in enumerate(blocks):
        gathered[k * rows : (k + 1) * rows, :] = block[...]
    value = jnp.dot(
        matrix[first : first + out.shape[0], :],
        gathered[...],
        preferred_element_type=jnp.float32,
    )
    out[...] = value.astype(out.dtype)


def product(matrix, blocks, first, count, dtype, weight):
    rows, width = blocks[0].shape
    total, depth = matrix.shape
    return pl.pallas_call(
        functools.partial(product_kernel, first),
        out_shape=jax.ShapeDtypeStruct((count, width), dtype),
        in_specs=[VMEM] * (1 + len(blocks)),
        out_specs=VMEM,
        scratch_shapes=[pltpu.VMEM((depth, width), blocks[0].dtype)],
        compiler_params=params(16),
        cost_estimate=cost(weight * total * depth * width, 1),
    )(matrix, *blocks)


def join_kernel(count, stay, *refs):
    came, (kept, *sent) = refs[:count], refs[count:]
    rows, part = kept.shape[0], came[0].shape[0]
    for place, out in enumerate([kept] + sent):
        start = place * rows
        other = came[start // part][start % part : start % part + rows, :]
        value = stay[start : start + rows, :] + other.astype(jnp.float32)
        out[...] = value.astype(out.dtype)


def join(stay, came, rows):
    total, width = stay.shape
    parts = total // rows
    return pl.pallas_call(
        functools.partial(join_kernel, len(came)),
        out_shape=[jax.ShapeDtypeStruct((rows, width), jnp.float32)]
        + [jax.ShapeDtypeStruct((rows, width), jnp.bfloat16)] * (parts - 1),
        in_specs=[VMEM] * (1 + len(came)),
        out_specs=[VMEM] * parts,
        compiler_params=params(12),
        cost_estimate=cost(1, 1),
    )(stay, *came)


def finish_kernel(chunks, projected, norm, *refs):
    out = refs[-1]
    per_chunk = (len(refs) - 1) // chunks
    lanes = norm.shape[1]
    width = refs[0].shape[1]
    for part in range(norm.shape[0]):
        factor = rows_to_lanes(norm[part : part + 1, :], lanes)
        here = slice(part * lanes, (part + 1) * lanes)
        for column in range(0, out.shape[1], lanes):
            pieces = refs[column // width * per_chunk : (column // width + 1) * per_chunk]
            start = column % width
            value = projected[here, column : column + lanes]
            for piece in pieces:
                value += piece[here, start : start + lanes].astype(jnp.float32)
            out[here, column : column + lanes] = jnp.maximum(factor * value, 0.0).astype(out.dtype)


def finish(projected, target_norm, pieces):
    rows, hidden = projected.shape
    flat = [piece for chunk in pieces for piece in chunk]
    return pl.pallas_call(
        functools.partial(finish_kernel, len(pieces)),
        out_shape=jax.ShapeDtypeStruct((rows, hidden), jnp.bfloat16),
        in_specs=[VMEM] * (2 + len(flat)),
        out_specs=VMEM,
        compiler_params=params(12),
        cost_estimate=cost(6 * rows * hidden, 16 * rows * hidden),
    )(projected, target_norm.reshape(-1, 128), *flat)


def visit_kernel(own_tiles, per_owner, sources, targets, count, labels, tiles, blocks, out, total):
    spare, rows = total.shape[0] - 1, total.shape[1]
    total[...] = jnp.zeros_like(total)

    @pl.loop(0, count[0])
    def _(slot):
        target = targets[0, slot]
        label = labels[0, target]
        place = jnp.where(label < own_tiles, target // per_owner * own_tiles + label, spare)
        start = pl.multiple_of(sources[0, slot] * rows, rows)
        total[place] += jnp.dot(
            tiles[0, slot], blocks[pl.ds(start, rows), :], preferred_element_type=jnp.float32
        )

    @pl.loop(0, spare)
    def _(place):
        out[pl.ds(pl.multiple_of(place * rows, rows), rows), :] = total[place].astype(out.dtype)


def visit_tiles(own_tiles, owners, index_args, tile_weights, blocks):
    slots = index_args[-1].shape[1]
    rows = tile_weights.shape[-1]
    places = owners * own_tiles
    hidden = blocks.shape[1]
    return pl.pallas_call(
        functools.partial(visit_kernel, own_tiles, slots // owners),
        out_shape=jax.ShapeDtypeStruct((places * rows, hidden), jnp.bfloat16),
        in_specs=[SMEM] * 4 + [VMEM] * 2,
        out_specs=VMEM,
        scratch_shapes=[pltpu.VMEM((places + 1, rows, hidden), jnp.float32)],
        compiler_params=params(56),
    )(*index_args, tile_weights, blocks)


def swap(value, axis, apart):
    pairs = [(i, i ^ apart) for i in range(lax.axis_size(axis))]
    return lax.ppermute(value, axis, pairs)


def exchange(sent):
    owners = lax.axis_size("row")
    steps = [(2, 4), (4, 2), (6, 6)]
    return [
        lax.ppermute(value, "row", [(i, i ^ step[i % 2]) for i in range(owners)])
        for value, step in zip(sent, steps)
    ]


def per_device(
    features,
    weight,
    source_norm,
    target_norm,
    tile_weights,
    tile_source,
    tile_target,
    tile_count,
    mirror_tile,
):
    tile_rows = tile_weights.shape[-1]
    own_rows = features.shape[0]
    own_tiles = own_rows // tile_rows
    owners, columns = lax.axis_size("row"), lax.axis_size("col")
    span = own_tiles * columns
    index_args = (tile_source, tile_target, tile_count, mirror_tile)

    cells = owners * own_tiles * span * tile_rows * tile_rows
    if columns != 4 or owners != 8 or own_tiles & (own_tiles - 1) or cells > DENSE_ELEMENTS:
        projected = jnp.dot(features, weight, preferred_element_type=jnp.float32)
        scaled = (source_norm[:, None] * projected).astype(jnp.bfloat16)
        blocks = lax.all_gather(scaled, "col", axis=0, tiled=True)
        partial_value = visit_tiles(own_tiles, owners, index_args, tile_weights, blocks)
        outgoing = partial_value.reshape(owners, own_rows, -1)
        arrived = lax.all_to_all(outgoing, "row", split_axis=0, concat_axis=0, tiled=True)
        gathered = jnp.sum(arrived.astype(jnp.float32), axis=0) + projected
        return jnp.maximum(target_norm[:, None] * gathered, 0.0).astype(jnp.bfloat16)

    projected, *scaled = project(features, weight, source_norm, CHUNKS)
    built = merge_tiles(own_tiles, owners, span, index_args, tile_weights)
    half = built.shape[0] // 2
    across = [swap(own, "col", 3) for own in scaled]
    beside = [swap(own, "col", 1) for own in scaled]
    onward, matrix = lax.optimization_barrier((across[0], built))
    passed = swap(onward, "col", 1)
    early = early_product(matrix, scaled[0], beside[0], across[0])
    away = [
        late_product(matrix, early, passed, k * half // 2, half // 2, jnp.bfloat16, WEIGHTS[0])
        for k in range(2)
    ]
    stay = late_product(matrix, early, passed, half, half, jnp.float32, WEIGHTS[1])
    kept, *sent = join(stay, [swap(value, "row", 1) for value in away], own_rows)
    pieces = [[kept] + exchange(sent)]

    onward, _ = lax.optimization_barrier((across[1], early))
    blocks = scaled[1], beside[1], swap(onward, "col", 1), across[1]
    blocks, _ = lax.optimization_barrier((blocks, sent))
    away = [
        product(matrix, blocks, k * half // 2, half // 2, jnp.bfloat16, WEIGHTS[2])
        for k in range(2)
    ]
    stay = product(matrix, blocks, half, half, jnp.float32, WEIGHTS[3])
    kept, *sent = join(stay, [swap(value, "row", 1) for value in away], own_rows)
    pieces.append([kept] + exchange(sent))
    return finish(projected, target_norm, pieces)


def solution(mesh):
    in_specs = (
        P(("row", "col"), None),
        P(),
        P(("row", "col")),
        P(("row", "col")),
        P(("row", "col"), None, None, None),
        P(("row", "col"), None),
        P(("row", "col"), None),
        P(("row", "col")),
        P(("row", "col"), None),
    )
    out_specs = P(("row", "col"), None)
    return jax.shard_map(
        per_device, mesh=mesh, in_specs=in_specs, out_specs=out_specs, check_vma=False
    )
```

```python
import functools

import jax
import jax.numpy as jnp
from jax import lax
from jax.experimental import pallas as pl
from jax.experimental.pallas import tpu as pltpu
from jax.sharding import PartitionSpec as P

DENSE_ELEMENTS = 4 * 1024 * 1024
CHUNKS = 2
WEIGHTS = ((20, 20), (0, 20))
MIB = 1024 * 1024
SMEM = pl.BlockSpec(memory_space=pltpu.SMEM)
VMEM = pl.BlockSpec(memory_space=pltpu.VMEM)
HBM = pl.BlockSpec(memory_space=pltpu.HBM)


def params(mib):
    return pltpu.CompilerParams(vmem_limit_bytes=int(mib * MIB))


def cost(flops, moved):
    return pl.CostEstimate(flops=flops, bytes_accessed=moved, transcendentals=0)


def in_hbm(*values):
    return [pltpu.with_memory_space_constraint(value, pltpu.HBM) for value in values]


def rows_to_lanes(row, lanes):
    return jnp.broadcast_to(row, (lanes, row.shape[1])).T


def project_kernel(features_hbm, weight_hbm, norm_hbm, projected, *refs):
    *scaled, features, weight, norm, sems = refs
    copies = [
        pltpu.make_async_copy(source, target, sems.at[k])
        for k, (source, target) in enumerate(
            [(weight_hbm, weight), (features_hbm, features), (norm_hbm, norm)]
        )
    ]
    for copy in copies:
        copy.start()
    for copy in copies:
        copy.wait()
    lanes = norm.shape[1]
    value = jnp.dot(features[...], weight[...], preferred_element_type=jnp.float32)
    projected[...] = value
    width = scaled[0].shape[1]
    for part in range(norm.shape[0]):
        factor = rows_to_lanes(norm[part : part + 1, :], lanes)
        for column in range(0, value.shape[1], lanes):
            piece = value[part * lanes : (part + 1) * lanes, column : column + lanes]
            target = scaled[column // width]
            start = column % width
            target[part * lanes : (part + 1) * lanes, start : start + lanes] = (
                factor * piece
            ).astype(target.dtype)


def project(features, weight, source_norm, chunks):
    rows, depth = features.shape
    hidden = weight.shape[1]
    norm = source_norm.reshape(-1, 128)
    return pl.pallas_call(
        project_kernel,
        out_shape=[jax.ShapeDtypeStruct((rows, hidden), jnp.float32)]
        + [jax.ShapeDtypeStruct((rows, hidden // chunks), jnp.bfloat16)] * chunks,
        in_specs=[HBM] * 3,
        out_specs=[VMEM] * (1 + chunks),
        scratch_shapes=[
            pltpu.VMEM(features.shape, features.dtype),
            pltpu.VMEM(weight.shape, weight.dtype),
            pltpu.VMEM(norm.shape, norm.dtype),
            pltpu.SemaphoreType.DMA((3,)),
        ],
        compiler_params=params(12),
        cost_estimate=cost(2 * rows * depth * hidden, 2 * depth * (rows + hidden)),
    )(*in_hbm(features, weight, norm))


def merge_kernel(
    own_tiles, per_owner, row, column, count, sources_hbm, targets_hbm, labels_hbm, tiles_hbm, out,
    total, tiles, sources, targets, labels, bases, seen, sems, tile_sems,
):
    small = [
        pltpu.make_async_copy(source, target, sems.at[k])
        for k, (source, target) in enumerate(
            [(sources_hbm, sources), (targets_hbm, targets), (labels_hbm, labels)]
        )
    ]
    parts = tile_sems.shape[0]
    each = tiles.shape[0] // parts
    large = [
        pltpu.make_async_copy(
            tiles_hbm.at[0, pl.ds(k * each, each)],
            tiles.at[pl.ds(k * each, each)],
            tile_sems.at[k],
        )
        for k in range(parts)
    ]
    for copy in small + large:
        copy.start()
    rows = total.shape[1]
    places, span = out.shape[0] // rows, out.shape[1] // rows
    spare = places * span
    for cell in range(spare + 1):
        seen[cell] = 0
    my_core, used = row[0] % 2, count[0]
    toggle = column[0] * own_tiles
    for copy in small:
        copy.wait()

    for slot in range(bases.shape[0]):
        owner, label = slot // per_owner, labels[0, slot]
        core, apart = owner % 2, lax.bitwise_xor(row[0], owner)
        x, y = lax.bitwise_and(apart, 2), lax.bitwise_and(lax.shift_right_logical(apart, 1), 2)
        first, second = (x, y) if core == 0 else (y, x)
        position = jnp.where(my_core == core, 4, 0) + second + lax.shift_right_logical(first, 1)
        base = (position * own_tiles + label) * span
        bases[slot] = jnp.where(label < own_tiles, base, spare)

    def add(slot):
        base = bases[targets[0, slot]]
        here = base + lax.bitwise_xor(sources[0, slot], toggle)
        cell = jnp.where((base < spare) & (slot < used), here, spare)
        before = jnp.where(seen[cell] > 0, total[cell], 0.0)
        seen[cell] = 1
        total[cell] = before + tiles[slot].astype(jnp.float32)

    for k, copy in enumerate(large):
        copy.wait()
        pl.loop(k * each, (k + 1) * each, unroll=4)(add)

    for place in range(places):
        for source in range(span):
            cell = place * span + source
            value = jnp.where(seen[cell] > 0, total[cell], 0.0)
            out[place * rows : (place + 1) * rows, source * rows : (source + 1) * rows] = (
                value.astype(out.dtype)
            )


def merge_tiles(own_tiles, owners, span, index_args, tile_weights):
    sources, targets, count, labels = index_args
    _, capacity, rows, _ = tile_weights.shape
    places = owners * own_tiles
    row = lax.axis_index("row").astype(jnp.int32).reshape(1)
    column = lax.axis_index("col").astype(jnp.int32).reshape(1)
    return pl.pallas_call(
        functools.partial(merge_kernel, own_tiles, labels.shape[1] // owners),
        out_shape=jax.ShapeDtypeStruct((places * rows, span * rows), jnp.bfloat16),
        in_specs=[SMEM] * 3 + [HBM] * 4,
        out_specs=VMEM,
        scratch_shapes=[
            pltpu.VMEM((places * span + 1, rows, rows), jnp.float32),
            pltpu.VMEM(tile_weights.shape[1:], tile_weights.dtype),
            pltpu.SMEM(sources.shape, jnp.int32),
            pltpu.SMEM(targets.shape, jnp.int32),
            pltpu.SMEM(labels.shape, jnp.int32),
            pltpu.SMEM((labels.shape[1],), jnp.int32),
            pltpu.SMEM((places * span + 1,), jnp.int32),
            pltpu.SemaphoreType.DMA((3,)),
            pltpu.SemaphoreType.DMA((4 if capacity % 4 == 0 else 1,)),
        ],
        compiler_params=params(24),
        cost_estimate=cost(8 * MIB, 12 * MIB),
    )(row, column, count, *in_hbm(sources, targets, labels, tile_weights))


def product_kernel(first, matrix, *refs):
    *blocks, out, gathered = refs
    rows = blocks[0].shape[0]
    for k, block in enumerate(blocks):
        gathered[k * rows : (k + 1) * rows, :] = block[...]
    value = jnp.dot(
        matrix[first : first + out.shape[0], :],
        gathered[...],
        preferred_element_type=jnp.float32,
    )
    out[...] = value.astype(out.dtype)


def product(matrix, blocks, half, dtype, weight):
    rows, width = blocks[0].shape
    total, depth = matrix.shape
    return pl.pallas_call(
        functools.partial(product_kernel, half * (total // 2)),
        out_shape=jax.ShapeDtypeStruct((total // 2, width), dtype),
        in_specs=[VMEM] * (1 + len(blocks)),
        out_specs=VMEM,
        scratch_shapes=[pltpu.VMEM((depth, width), blocks[0].dtype)],
        compiler_params=params(16),
        cost_estimate=cost(weight * total * depth * width, 1),
    )(matrix, *blocks)


def join_kernel(stay, came, kept, *sent):
    rows = kept.shape[0]
    value = stay[...].astype(jnp.float32) + came[...].astype(jnp.float32)
    kept[...] = value[:rows]
    for place, out in enumerate(sent):
        out[...] = value[(place + 1) * rows : (place + 2) * rows].astype(out.dtype)


def join(stay, came, rows):
    total, width = stay.shape
    parts = total // rows
    return pl.pallas_call(
        join_kernel,
        out_shape=[jax.ShapeDtypeStruct((rows, width), jnp.float32)]
        + [jax.ShapeDtypeStruct((rows, width), jnp.bfloat16)] * (parts - 1),
        in_specs=[VMEM] * 2,
        out_specs=[VMEM] * parts,
        compiler_params=params(12),
        cost_estimate=cost(1, 1),
    )(stay, came)


def finish_kernel(chunks, projected, norm, *refs):
    out = refs[-1]
    per_chunk = (len(refs) - 1) // chunks
    lanes = norm.shape[1]
    width = refs[0].shape[1]
    for part in range(norm.shape[0]):
        factor = rows_to_lanes(norm[part : part + 1, :], lanes)
        here = slice(part * lanes, (part + 1) * lanes)
        for column in range(0, out.shape[1], lanes):
            pieces = refs[column // width * per_chunk : (column // width + 1) * per_chunk]
            start = column % width
            value = projected[here, column : column + lanes]
            for piece in pieces:
                value += piece[here, start : start + lanes].astype(jnp.float32)
            out[here, column : column + lanes] = jnp.maximum(factor * value, 0.0).astype(out.dtype)


def finish(projected, target_norm, pieces):
    rows, hidden = projected.shape
    flat = [piece for chunk in pieces for piece in chunk]
    return pl.pallas_call(
        functools.partial(finish_kernel, len(pieces)),
        out_shape=jax.ShapeDtypeStruct((rows, hidden), jnp.bfloat16),
        in_specs=[VMEM] * (2 + len(flat)),
        out_specs=VMEM,
        compiler_params=params(12),
        cost_estimate=cost(6 * rows * hidden, 16 * rows * hidden),
    )(projected, target_norm.reshape(-1, 128), *flat)


def visit_kernel(own_tiles, per_owner, sources, targets, count, labels, tiles, blocks, out, total):
    spare, rows = total.shape[0] - 1, total.shape[1]
    total[...] = jnp.zeros_like(total)

    @pl.loop(0, count[0])
    def _(slot):
        target = targets[0, slot]
        label = labels[0, target]
        place = jnp.where(label < own_tiles, target // per_owner * own_tiles + label, spare)
        start = pl.multiple_of(sources[0, slot] * rows, rows)
        total[place] += jnp.dot(
            tiles[0, slot], blocks[pl.ds(start, rows), :], preferred_element_type=jnp.float32
        )

    @pl.loop(0, spare)
    def _(place):
        out[pl.ds(pl.multiple_of(place * rows, rows), rows), :] = total[place].astype(out.dtype)


def visit_tiles(own_tiles, owners, index_args, tile_weights, blocks):
    slots = index_args[-1].shape[1]
    rows = tile_weights.shape[-1]
    places = owners * own_tiles
    hidden = blocks.shape[1]
    return pl.pallas_call(
        functools.partial(visit_kernel, own_tiles, slots // owners),
        out_shape=jax.ShapeDtypeStruct((places * rows, hidden), jnp.bfloat16),
        in_specs=[SMEM] * 4 + [VMEM] * 2,
        out_specs=VMEM,
        scratch_shapes=[pltpu.VMEM((places + 1, rows, hidden), jnp.float32)],
        compiler_params=params(56),
    )(*index_args, tile_weights, blocks)


def swap(value, axis, apart):
    pairs = [(i, i ^ apart) for i in range(lax.axis_size(axis))]
    return lax.ppermute(value, axis, pairs)


def exchange(sent):
    owners = lax.axis_size("row")
    steps = [(2, 4), (4, 2), (6, 6)]
    return [
        lax.ppermute(value, "row", [(i, i ^ step[i % 2]) for i in range(owners)])
        for value, step in zip(sent, steps)
    ]


def per_device(
    features,
    weight,
    source_norm,
    target_norm,
    tile_weights,
    tile_source,
    tile_target,
    tile_count,
    mirror_tile,
):
    tile_rows = tile_weights.shape[-1]
    own_rows = features.shape[0]
    own_tiles = own_rows // tile_rows
    owners, columns = lax.axis_size("row"), lax.axis_size("col")
    span = own_tiles * columns
    index_args = (tile_source, tile_target, tile_count, mirror_tile)

    cells = owners * own_tiles * span * tile_rows * tile_rows
    if columns != 4 or owners != 8 or own_tiles & (own_tiles - 1) or cells > DENSE_ELEMENTS:
        projected = jnp.dot(features, weight, preferred_element_type=jnp.float32)
        scaled = (source_norm[:, None] * projected).astype(jnp.bfloat16)
        blocks = lax.all_gather(scaled, "col", axis=0, tiled=True)
        partial_value = visit_tiles(own_tiles, owners, index_args, tile_weights, blocks)
        outgoing = partial_value.reshape(owners, own_rows, -1)
        arrived = lax.all_to_all(outgoing, "row", split_axis=0, concat_axis=0, tiled=True)
        gathered = jnp.sum(arrived.astype(jnp.float32), axis=0) + projected
        return jnp.maximum(target_norm[:, None] * gathered, 0.0).astype(jnp.bfloat16)

    projected, *scaled = project(features, weight, source_norm, CHUNKS)
    matrix = merge_tiles(own_tiles, owners, span, index_args, tile_weights)
    across = [swap(own, "col", 2) for own in scaled]
    beside = [swap(own, "col", 1) for own in scaled]
    across[0], matrix = lax.optimization_barrier((across[0], matrix))
    passed = [swap(value, "col", 1) for value in across]
    pieces, sent = [], None
    for blocks, wait in zip(zip(scaled, beside, across, passed), WEIGHTS):
        if sent is not None:
            pieces[-1] += exchange(sent)
            blocks, _ = lax.optimization_barrier((blocks, sent))
        away = product(matrix, blocks, 0, jnp.bfloat16, wait[0])
        stay = product(matrix, blocks, 1, jnp.float32, wait[1])
        kept, *sent = join(stay, swap(away, "row", 1), own_rows)
        pieces.append([kept])
    pieces[-1] += exchange(sent)
    return finish(projected, target_norm, pieces)


def solution(mesh):
    in_specs = (
        P(("row", "col"), None),
        P(),
        P(("row", "col")),
        P(("row", "col")),
        P(("row", "col"), None, None, None),
        P(("row", "col"), None),
        P(("row", "col"), None),
        P(("row", "col")),
        P(("row", "col"), None),
    )
    out_specs = P(("row", "col"), None)
    return jax.shard_map(
        per_device, mesh=mesh, in_specs=in_specs, out_specs=out_specs, check_vma=False
    )
```

```python
import functools

import jax
import jax.numpy as jnp
from jax import lax
from jax.experimental import pallas as pl
from jax.experimental.pallas import tpu as pltpu
from jax.sharding import PartitionSpec as P

DENSE_ELEMENTS = 4 * 1024 * 1024
CHUNKS = 2
WEIGHTS = (20, 20, 0, 20)
MIB = 1024 * 1024
SMEM = pl.BlockSpec(memory_space=pltpu.SMEM)
VMEM = pl.BlockSpec(memory_space=pltpu.VMEM)
HBM = pl.BlockSpec(memory_space=pltpu.HBM)


def params(mib):
    return pltpu.CompilerParams(vmem_limit_bytes=int(mib * MIB))


def cost(flops, moved):
    return pl.CostEstimate(flops=flops, bytes_accessed=moved, transcendentals=0)


def in_hbm(*values):
    return [pltpu.with_memory_space_constraint(value, pltpu.HBM) for value in values]


def rows_to_lanes(row, lanes):
    return jnp.broadcast_to(row, (lanes, row.shape[1])).T


def project_kernel(features_hbm, weight_hbm, norm_hbm, projected, *refs):
    *scaled, features, weight, norm, sems = refs
    copies = [
        pltpu.make_async_copy(source, target, sems.at[k])
        for k, (source, target) in enumerate(
            [(weight_hbm, weight), (features_hbm, features), (norm_hbm, norm)]
        )
    ]
    for copy in copies:
        copy.start()
    for copy in copies:
        copy.wait()
    lanes = norm.shape[1]
    value = jnp.dot(features[...], weight[...], preferred_element_type=jnp.float32)
    projected[...] = value
    width = scaled[0].shape[1]
    for part in range(norm.shape[0]):
        factor = rows_to_lanes(norm[part : part + 1, :], lanes)
        for column in range(0, value.shape[1], lanes):
            here = slice(part * lanes, (part + 1) * lanes)
            piece = factor * value[here, column : column + lanes]
            target = scaled[column // width]
            start = column % width
            target[here, start : start + lanes] = piece.astype(target.dtype)


def project(features, weight, source_norm, chunks):
    rows, depth = features.shape
    hidden = weight.shape[1]
    norm = source_norm.reshape(-1, 128)
    return pl.pallas_call(
        project_kernel,
        out_shape=[jax.ShapeDtypeStruct((rows, hidden), jnp.float32)]
        + [jax.ShapeDtypeStruct((rows, hidden // chunks), jnp.bfloat16)] * chunks,
        in_specs=[HBM] * 3,
        out_specs=[VMEM] * (1 + chunks),
        scratch_shapes=[
            pltpu.VMEM(features.shape, features.dtype),
            pltpu.VMEM(weight.shape, weight.dtype),
            pltpu.VMEM(norm.shape, norm.dtype),
            pltpu.SemaphoreType.DMA((3,)),
        ],
        compiler_params=params(12),
        cost_estimate=cost(2 * rows * depth * hidden, 2 * depth * (rows + hidden)),
    )(*in_hbm(features, weight, norm))


def merge_kernel(
    own_tiles, per_owner, row, column, count, sources_hbm, targets_hbm, labels_hbm, tiles_hbm, out,
    total, tiles, sources, targets, labels, bases, seen, sems, tile_sems,
):
    small = [
        pltpu.make_async_copy(source, target, sems.at[k])
        for k, (source, target) in enumerate(
            [(sources_hbm, sources), (targets_hbm, targets), (labels_hbm, labels)]
        )
    ]
    parts = tile_sems.shape[0]
    each = tiles.shape[0] // parts
    large = [
        pltpu.make_async_copy(
            tiles_hbm.at[0, pl.ds(k * each, each)],
            tiles.at[pl.ds(k * each, each)],
            tile_sems.at[k],
        )
        for k in range(parts)
    ]
    for copy in small + large:
        copy.start()
    rows = total.shape[1]
    places, span = out.shape[0] // rows, out.shape[1] // rows
    spare = places * span
    for cell in range(spare + 1):
        seen[cell] = 0
    my_core, used = row[0] % 2, count[0]
    toggle = column[0] * own_tiles
    for copy in small:
        copy.wait()

    for slot in range(bases.shape[0]):
        owner, label = slot // per_owner, labels[0, slot]
        core, apart = owner % 2, lax.bitwise_xor(row[0], owner)
        x, y = lax.bitwise_and(apart, 2), lax.bitwise_and(lax.shift_right_logical(apart, 1), 2)
        first, second = (x, y) if core == 0 else (y, x)
        position = jnp.where(my_core == core, 4, 0) + second + lax.shift_right_logical(first, 1)
        base = (position * own_tiles + label) * span
        bases[slot] = jnp.where(label < own_tiles, base, spare)

    def add(slot):
        base = bases[targets[0, slot]]
        here = base + lax.bitwise_xor(sources[0, slot], toggle)
        cell = jnp.where((base < spare) & (slot < used), here, spare)
        before = jnp.where(seen[cell] > 0, total[cell], 0.0)
        seen[cell] = 1
        total[cell] = before + tiles[slot].astype(jnp.float32)

    for k, copy in enumerate(large):
        copy.wait()
        pl.loop(k * each, (k + 1) * each, unroll=4)(add)

    for place in range(places):
        for source in range(span):
            cell = place * span + source
            value = jnp.where(seen[cell] > 0, total[cell], 0.0)
            out[place * rows : (place + 1) * rows, source * rows : (source + 1) * rows] = (
                value.astype(out.dtype)
            )


def merge_tiles(own_tiles, owners, span, index_args, tile_weights):
    sources, targets, count, labels = index_args
    _, capacity, rows, _ = tile_weights.shape
    places = owners * own_tiles
    row = lax.axis_index("row").astype(jnp.int32).reshape(1)
    column = lax.axis_index("col").astype(jnp.int32).reshape(1)
    return pl.pallas_call(
        functools.partial(merge_kernel, own_tiles, labels.shape[1] // owners),
        out_shape=jax.ShapeDtypeStruct((places * rows, span * rows), jnp.bfloat16),
        in_specs=[SMEM] * 3 + [HBM] * 4,
        out_specs=VMEM,
        scratch_shapes=[
            pltpu.VMEM((places * span + 1, rows, rows), jnp.float32),
            pltpu.VMEM(tile_weights.shape[1:], tile_weights.dtype),
            pltpu.SMEM(sources.shape, jnp.int32),
            pltpu.SMEM(targets.shape, jnp.int32),
            pltpu.SMEM(labels.shape, jnp.int32),
            pltpu.SMEM((labels.shape[1],), jnp.int32),
            pltpu.SMEM((places * span + 1,), jnp.int32),
            pltpu.SemaphoreType.DMA((3,)),
            pltpu.SemaphoreType.DMA((4 if capacity % 4 == 0 else 1,)),
        ],
        compiler_params=params(24),
        cost_estimate=cost(8 * MIB, 12 * MIB),
    )(row, column, count, *in_hbm(sources, targets, labels, tile_weights))


def early_kernel(matrix, own, beside, across, out):
    rows = own.shape[0]
    value = jnp.dot(matrix[:, :rows], own[...], preferred_element_type=jnp.float32)
    value += jnp.dot(
        matrix[:, rows : 2 * rows], beside[...], preferred_element_type=jnp.float32
    )
    value += jnp.dot(matrix[:, 3 * rows :], across[...], preferred_element_type=jnp.float32)
    out[...] = value


def early_product(matrix, own, beside, across):
    total, depth = matrix.shape
    width = own.shape[1]
    return pl.pallas_call(
        early_kernel,
        out_shape=jax.ShapeDtypeStruct((total, width), jnp.float32),
        in_specs=[VMEM] * 4,
        out_specs=VMEM,
        compiler_params=params(16),
        cost_estimate=cost(total * depth * width, 1),
    )(matrix, own, beside, across)


def late_kernel(first, matrix, early, passed, out):
    rows = passed.shape[0]
    here = slice(first, first + out.shape[0])
    value = early[here, :] + jnp.dot(
        matrix[here, 2 * rows : 3 * rows], passed[...], preferred_element_type=jnp.float32
    )
    out[...] = value.astype(out.dtype)


def late_product(matrix, early, passed, first, count, dtype, weight):
    total, depth = matrix.shape
    width = passed.shape[1]
    return pl.pallas_call(
        functools.partial(late_kernel, first),
        out_shape=jax.ShapeDtypeStruct((count, width), dtype),
        in_specs=[VMEM] * 3,
        out_specs=VMEM,
        compiler_params=params(16),
        cost_estimate=cost(weight * total * depth * width, 1),
    )(matrix, early, passed)


def product_kernel(first, matrix, *refs):
    *blocks, out, gathered = refs
    rows = blocks[0].shape[0]
    for k, block in enumerate(blocks):
        gathered[k * rows : (k + 1) * rows, :] = block[...]
    value = jnp.dot(
        matrix[first : first + out.shape[0], :],
        gathered[...],
        preferred_element_type=jnp.float32,
    )
    out[...] = value.astype(out.dtype)


def product(matrix, blocks, first, count, dtype, weight):
    rows, width = blocks[0].shape
    total, depth = matrix.shape
    return pl.pallas_call(
        functools.partial(product_kernel, first),
        out_shape=jax.ShapeDtypeStruct((count, width), dtype),
        in_specs=[VMEM] * (1 + len(blocks)),
        out_specs=VMEM,
        scratch_shapes=[pltpu.VMEM((depth, width), blocks[0].dtype)],
        compiler_params=params(16),
        cost_estimate=cost(weight * total * depth * width, 1),
    )(matrix, *blocks)


def join_kernel(stay, came, kept, *sent):
    rows = kept.shape[0]
    value = stay[...].astype(jnp.float32) + came[...].astype(jnp.float32)
    kept[...] = value[:rows]
    for place, out in enumerate(sent):
        out[...] = value[(place + 1) * rows : (place + 2) * rows].astype(out.dtype)


def join(stay, came, rows):
    total, width = stay.shape
    parts = total // rows
    return pl.pallas_call(
        join_kernel,
        out_shape=[jax.ShapeDtypeStruct((rows, width), jnp.float32)]
        + [jax.ShapeDtypeStruct((rows, width), jnp.bfloat16)] * (parts - 1),
        in_specs=[VMEM] * 2,
        out_specs=[VMEM] * parts,
        compiler_params=params(12),
        cost_estimate=cost(1, 1),
    )(stay, came)


def finish_kernel(chunks, projected, norm, *refs):
    out = refs[-1]
    per_chunk = (len(refs) - 1) // chunks
    lanes = norm.shape[1]
    width = refs[0].shape[1]
    for part in range(norm.shape[0]):
        factor = rows_to_lanes(norm[part : part + 1, :], lanes)
        here = slice(part * lanes, (part + 1) * lanes)
        for column in range(0, out.shape[1], lanes):
            pieces = refs[column // width * per_chunk : (column // width + 1) * per_chunk]
            start = column % width
            value = projected[here, column : column + lanes]
            for piece in pieces:
                value += piece[here, start : start + lanes].astype(jnp.float32)
            out[here, column : column + lanes] = jnp.maximum(factor * value, 0.0).astype(out.dtype)


def finish(projected, target_norm, pieces):
    rows, hidden = projected.shape
    flat = [piece for chunk in pieces for piece in chunk]
    return pl.pallas_call(
        functools.partial(finish_kernel, len(pieces)),
        out_shape=jax.ShapeDtypeStruct((rows, hidden), jnp.bfloat16),
        in_specs=[VMEM] * (2 + len(flat)),
        out_specs=VMEM,
        compiler_params=params(12),
        cost_estimate=cost(6 * rows * hidden, 16 * rows * hidden),
    )(projected, target_norm.reshape(-1, 128), *flat)


def visit_kernel(own_tiles, per_owner, sources, targets, count, labels, tiles, blocks, out, total):
    spare, rows = total.shape[0] - 1, total.shape[1]
    total[...] = jnp.zeros_like(total)

    @pl.loop(0, count[0])
    def _(slot):
        target = targets[0, slot]
        label = labels[0, target]
        place = jnp.where(label < own_tiles, target // per_owner * own_tiles + label, spare)
        start = pl.multiple_of(sources[0, slot] * rows, rows)
        total[place] += jnp.dot(
            tiles[0, slot], blocks[pl.ds(start, rows), :], preferred_element_type=jnp.float32
        )

    @pl.loop(0, spare)
    def _(place):
        out[pl.ds(pl.multiple_of(place * rows, rows), rows), :] = total[place].astype(out.dtype)


def visit_tiles(own_tiles, owners, index_args, tile_weights, blocks):
    slots = index_args[-1].shape[1]
    rows = tile_weights.shape[-1]
    places = owners * own_tiles
    hidden = blocks.shape[1]
    return pl.pallas_call(
        functools.partial(visit_kernel, own_tiles, slots // owners),
        out_shape=jax.ShapeDtypeStruct((places * rows, hidden), jnp.bfloat16),
        in_specs=[SMEM] * 4 + [VMEM] * 2,
        out_specs=VMEM,
        scratch_shapes=[pltpu.VMEM((places + 1, rows, hidden), jnp.float32)],
        compiler_params=params(56),
    )(*index_args, tile_weights, blocks)


def swap(value, axis, apart):
    pairs = [(i, i ^ apart) for i in range(lax.axis_size(axis))]
    return lax.ppermute(value, axis, pairs)


def exchange(sent):
    owners = lax.axis_size("row")
    steps = [(2, 4), (4, 2), (6, 6)]
    return [
        lax.ppermute(value, "row", [(i, i ^ step[i % 2]) for i in range(owners)])
        for value, step in zip(sent, steps)
    ]


def per_device(
    features,
    weight,
    source_norm,
    target_norm,
    tile_weights,
    tile_source,
    tile_target,
    tile_count,
    mirror_tile,
):
    tile_rows = tile_weights.shape[-1]
    own_rows = features.shape[0]
    own_tiles = own_rows // tile_rows
    owners, columns = lax.axis_size("row"), lax.axis_size("col")
    span = own_tiles * columns
    index_args = (tile_source, tile_target, tile_count, mirror_tile)

    cells = owners * own_tiles * span * tile_rows * tile_rows
    if columns != 4 or owners != 8 or own_tiles & (own_tiles - 1) or cells > DENSE_ELEMENTS:
        projected = jnp.dot(features, weight, preferred_element_type=jnp.float32)
        scaled = (source_norm[:, None] * projected).astype(jnp.bfloat16)
        blocks = lax.all_gather(scaled, "col", axis=0, tiled=True)
        partial_value = visit_tiles(own_tiles, owners, index_args, tile_weights, blocks)
        outgoing = partial_value.reshape(owners, own_rows, -1)
        arrived = lax.all_to_all(outgoing, "row", split_axis=0, concat_axis=0, tiled=True)
        gathered = jnp.sum(arrived.astype(jnp.float32), axis=0) + projected
        return jnp.maximum(target_norm[:, None] * gathered, 0.0).astype(jnp.bfloat16)

    projected, *scaled = project(features, weight, source_norm, CHUNKS)
    built = merge_tiles(own_tiles, owners, span, index_args, tile_weights)
    half = built.shape[0] // 2
    across = [swap(own, "col", 3) for own in scaled]
    beside = [swap(own, "col", 1) for own in scaled]
    onward, matrix = lax.optimization_barrier((across[0], built))
    passed = swap(onward, "col", 1)
    early = early_product(matrix, scaled[0], beside[0], across[0])
    away = late_product(matrix, early, passed, 0, half, jnp.bfloat16, WEIGHTS[0])
    stay = late_product(matrix, early, passed, half, half, jnp.float32, WEIGHTS[1])
    kept, *sent = join(stay, swap(away, "row", 1), own_rows)
    pieces = [[kept] + exchange(sent)]

    onward, _ = lax.optimization_barrier((across[1], early))
    blocks = scaled[1], beside[1], swap(onward, "col", 1), across[1]
    blocks, _ = lax.optimization_barrier((blocks, sent))
    away = product(matrix, blocks, 0, half, jnp.bfloat16, WEIGHTS[2])
    stay = product(matrix, blocks, half, half, jnp.float32, WEIGHTS[3])
    kept, *sent = join(stay, swap(away, "row", 1), own_rows)
    pieces.append([kept] + exchange(sent))
    return finish(projected, target_norm, pieces)


def solution(mesh):
    in_specs = (
        P(("row", "col"), None),
        P(),
        P(("row", "col")),
        P(("row", "col")),
        P(("row", "col"), None, None, None),
        P(("row", "col"), None),
        P(("row", "col"), None),
        P(("row", "col")),
        P(("row", "col"), None),
    )
    out_specs = P(("row", "col"), None)
    return jax.shard_map(
        per_device, mesh=mesh, in_specs=in_specs, out_specs=out_specs, check_vma=False
    )
```

```python
import functools

import jax
import jax.numpy as jnp
from jax import lax
from jax.experimental import pallas as pl
from jax.experimental.pallas import tpu as pltpu
from jax.sharding import PartitionSpec as P

DENSE_ELEMENTS = 4 * 1024 * 1024
CHUNKS = 2
WEIGHTS = (20, 20, 0, 20)
MIB = 1024 * 1024
SMEM = pl.BlockSpec(memory_space=pltpu.SMEM)
VMEM = pl.BlockSpec(memory_space=pltpu.VMEM)
HBM = pl.BlockSpec(memory_space=pltpu.HBM)


def params(mib):
    return pltpu.CompilerParams(vmem_limit_bytes=int(mib * MIB))


def cost(flops, moved):
    return pl.CostEstimate(flops=flops, bytes_accessed=moved, transcendentals=0)


def in_hbm(*values):
    return [pltpu.with_memory_space_constraint(value, pltpu.HBM) for value in values]


def rows_to_lanes(row, lanes):
    return jnp.broadcast_to(row, (lanes, row.shape[1])).T


def project_kernel(features_hbm, weight_hbm, norm_hbm, projected, *refs):
    *scaled, features, weight, norm, sems = refs
    copies = [
        pltpu.make_async_copy(source, target, sems.at[k])
        for k, (source, target) in enumerate(
            [(weight_hbm, weight), (features_hbm, features), (norm_hbm, norm)]
        )
    ]
    for copy in copies:
        copy.start()
    for copy in copies:
        copy.wait()
    lanes = norm.shape[1]
    value = jnp.dot(features[...], weight[...], preferred_element_type=jnp.float32)
    projected[...] = value
    width = scaled[0].shape[1]
    for part in range(norm.shape[0]):
        factor = rows_to_lanes(norm[part : part + 1, :], lanes)
        for column in range(0, value.shape[1], lanes):
            here = slice(part * lanes, (part + 1) * lanes)
            piece = factor * value[here, column : column + lanes]
            target = scaled[column // width]
            start = column % width
            target[here, start : start + lanes] = piece.astype(target.dtype)


def project(features, weight, source_norm, chunks):
    rows, depth = features.shape
    hidden = weight.shape[1]
    norm = source_norm.reshape(-1, 128)
    return pl.pallas_call(
        project_kernel,
        out_shape=[jax.ShapeDtypeStruct((rows, hidden), jnp.float32)]
        + [jax.ShapeDtypeStruct((rows, hidden // chunks), jnp.bfloat16)] * chunks,
        in_specs=[HBM] * 3,
        out_specs=[VMEM] * (1 + chunks),
        scratch_shapes=[
            pltpu.VMEM(features.shape, features.dtype),
            pltpu.VMEM(weight.shape, weight.dtype),
            pltpu.VMEM(norm.shape, norm.dtype),
            pltpu.SemaphoreType.DMA((3,)),
        ],
        compiler_params=params(12),
        cost_estimate=cost(2 * rows * depth * hidden, 2 * depth * (rows + hidden)),
    )(*in_hbm(features, weight, norm))


def merge_kernel(
    own_tiles, per_owner, row, column, count, sources_hbm, targets_hbm, labels_hbm, tiles_hbm, out,
    total, tiles, sources, targets, labels, bases, seen, sems, tile_sems,
):
    small = [
        pltpu.make_async_copy(source, target, sems.at[k])
        for k, (source, target) in enumerate(
            [(sources_hbm, sources), (targets_hbm, targets), (labels_hbm, labels)]
        )
    ]
    parts = tile_sems.shape[0]
    each = tiles.shape[0] // parts
    large = [
        pltpu.make_async_copy(
            tiles_hbm.at[0, pl.ds(k * each, each)],
            tiles.at[pl.ds(k * each, each)],
            tile_sems.at[k],
        )
        for k in range(parts)
    ]
    for copy in small + large:
        copy.start()
    rows = total.shape[1]
    places, span = out.shape[0] // rows, out.shape[1] // rows
    spare = places * span
    for cell in range(spare + 1):
        seen[cell] = 0
    my_core, used = row[0] % 2, count[0]
    toggle = column[0] * own_tiles
    for copy in small:
        copy.wait()

    for slot in range(bases.shape[0]):
        owner, label = slot // per_owner, labels[0, slot]
        core, apart = owner % 2, lax.bitwise_xor(row[0], owner)
        x, y = lax.bitwise_and(apart, 2), lax.bitwise_and(lax.shift_right_logical(apart, 1), 2)
        first, second = (x, y) if core == 0 else (y, x)
        position = jnp.where(my_core == core, 4, 0) + second + lax.shift_right_logical(first, 1)
        base = (position * own_tiles + label) * span
        bases[slot] = jnp.where(label < own_tiles, base, spare)

    def add(slot):
        base = bases[targets[0, slot]]
        here = base + lax.bitwise_xor(sources[0, slot], toggle)
        cell = jnp.where((base < spare) & (slot < used), here, spare)
        before = jnp.where(seen[cell] > 0, total[cell], 0.0)
        seen[cell] = 1
        total[cell] = before + tiles[slot].astype(jnp.float32)

    for k, copy in enumerate(large):
        copy.wait()
        pl.loop(k * each, (k + 1) * each, unroll=4)(add)

    for place in range(places):
        for source in range(span):
            cell = place * span + source
            value = jnp.where(seen[cell] > 0, total[cell], 0.0)
            out[place * rows : (place + 1) * rows, source * rows : (source + 1) * rows] = (
                value.astype(out.dtype)
            )


def merge_tiles(own_tiles, owners, span, index_args, tile_weights):
    sources, targets, count, labels = index_args
    _, capacity, rows, _ = tile_weights.shape
    places = owners * own_tiles
    row = lax.axis_index("row").astype(jnp.int32).reshape(1)
    column = lax.axis_index("col").astype(jnp.int32).reshape(1)
    return pl.pallas_call(
        functools.partial(merge_kernel, own_tiles, labels.shape[1] // owners),
        out_shape=jax.ShapeDtypeStruct((places * rows, span * rows), jnp.bfloat16),
        in_specs=[SMEM] * 3 + [HBM] * 4,
        out_specs=VMEM,
        scratch_shapes=[
            pltpu.VMEM((places * span + 1, rows, rows), jnp.float32),
            pltpu.VMEM(tile_weights.shape[1:], tile_weights.dtype),
            pltpu.SMEM(sources.shape, jnp.int32),
            pltpu.SMEM(targets.shape, jnp.int32),
            pltpu.SMEM(labels.shape, jnp.int32),
            pltpu.SMEM((labels.shape[1],), jnp.int32),
            pltpu.SMEM((places * span + 1,), jnp.int32),
            pltpu.SemaphoreType.DMA((3,)),
            pltpu.SemaphoreType.DMA((4 if capacity % 4 == 0 else 1,)),
        ],
        compiler_params=params(24),
        cost_estimate=cost(8 * MIB, 12 * MIB),
    )(row, column, count, *in_hbm(sources, targets, labels, tile_weights))


def early_kernel(matrix, own, beside, across, out):
    rows = own.shape[0]
    value = jnp.dot(matrix[:, :rows], own[...], preferred_element_type=jnp.float32)
    value += jnp.dot(
        matrix[:, rows : 2 * rows], beside[...], preferred_element_type=jnp.float32
    )
    value += jnp.dot(matrix[:, 3 * rows :], across[...], preferred_element_type=jnp.float32)
    out[...] = value


def early_product(matrix, own, beside, across):
    total, depth = matrix.shape
    width = own.shape[1]
    return pl.pallas_call(
        early_kernel,
        out_shape=jax.ShapeDtypeStruct((total, width), jnp.float32),
        in_specs=[VMEM] * 4,
        out_specs=VMEM,
        compiler_params=params(16),
        cost_estimate=cost(total * depth * width, 1),
    )(matrix, own, beside, across)


def late_kernel(first, matrix, early, passed, out):
    rows = passed.shape[0]
    here = slice(first, first + out.shape[0])
    value = early[here, :] + jnp.dot(
        matrix[here, 2 * rows : 3 * rows], passed[...], preferred_element_type=jnp.float32
    )
    out[...] = value.astype(out.dtype)


def late_product(matrix, early, passed, first, count, dtype, weight):
    total, depth = matrix.shape
    width = passed.shape[1]
    return pl.pallas_call(
        functools.partial(late_kernel, first),
        out_shape=jax.ShapeDtypeStruct((count, width), dtype),
        in_specs=[VMEM] * 3,
        out_specs=VMEM,
        compiler_params=params(16),
        cost_estimate=cost(weight * total * depth * width, 1),
    )(matrix, early, passed)


def product_kernel(first, matrix, *refs):
    *blocks, out, gathered = refs
    rows = blocks[0].shape[0]
    for k, block in enumerate(blocks):
        gathered[k * rows : (k + 1) * rows, :] = block[...]
    value = jnp.dot(
        matrix[first : first + out.shape[0], :],
        gathered[...],
        preferred_element_type=jnp.float32,
    )
    out[...] = value.astype(out.dtype)


def product(matrix, blocks, first, count, dtype, weight):
    rows, width = blocks[0].shape
    total, depth = matrix.shape
    return pl.pallas_call(
        functools.partial(product_kernel, first),
        out_shape=jax.ShapeDtypeStruct((count, width), dtype),
        in_specs=[VMEM] * (1 + len(blocks)),
        out_specs=VMEM,
        scratch_shapes=[pltpu.VMEM((depth, width), blocks[0].dtype)],
        compiler_params=params(16),
        cost_estimate=cost(weight * total * depth * width, 1),
    )(matrix, *blocks)


def join_kernel(stay, came, kept, *sent):
    rows = kept.shape[0]
    value = stay[...].astype(jnp.float32) + came[...].astype(jnp.float32)
    kept[...] = value[:rows]
    for place, out in enumerate(sent):
        out[...] = value[(place + 1) * rows : (place + 2) * rows].astype(out.dtype)


def join(stay, came, rows):
    total, width = stay.shape
    parts = total // rows
    return pl.pallas_call(
        join_kernel,
        out_shape=[jax.ShapeDtypeStruct((rows, width), jnp.float32)]
        + [jax.ShapeDtypeStruct((rows, width), jnp.bfloat16)] * (parts - 1),
        in_specs=[VMEM] * 2,
        out_specs=[VMEM] * parts,
        compiler_params=params(12),
        cost_estimate=cost(1, 1),
    )(stay, came)


def finish_kernel(chunks, projected, norm, *refs):
    out = refs[-1]
    per_chunk = (len(refs) - 1) // chunks
    lanes = norm.shape[1]
    width = refs[0].shape[1]
    for part in range(norm.shape[0]):
        factor = rows_to_lanes(norm[part : part + 1, :], lanes)
        here = slice(part * lanes, (part + 1) * lanes)
        for column in range(0, out.shape[1], lanes):
            pieces = refs[column // width * per_chunk : (column // width + 1) * per_chunk]
            start = column % width
            value = projected[here, column : column + lanes]
            for piece in pieces:
                value += piece[here, start : start + lanes].astype(jnp.float32)
            out[here, column : column + lanes] = jnp.maximum(factor * value, 0.0).astype(out.dtype)


def finish(projected, target_norm, pieces):
    rows, hidden = projected.shape
    flat = [piece for chunk in pieces for piece in chunk]
    return pl.pallas_call(
        functools.partial(finish_kernel, len(pieces)),
        out_shape=jax.ShapeDtypeStruct((rows, hidden), jnp.bfloat16),
        in_specs=[VMEM] * (2 + len(flat)),
        out_specs=VMEM,
        compiler_params=params(12),
        cost_estimate=cost(6 * rows * hidden, 16 * rows * hidden),
    )(projected, target_norm.reshape(-1, 128), *flat)


def visit_kernel(own_tiles, per_owner, sources, targets, count, labels, tiles, blocks, out, total):
    spare, rows = total.shape[0] - 1, total.shape[1]
    total[...] = jnp.zeros_like(total)

    @pl.loop(0, count[0])
    def _(slot):
        target = targets[0, slot]
        label = labels[0, target]
        place = jnp.where(label < own_tiles, target // per_owner * own_tiles + label, spare)
        start = pl.multiple_of(sources[0, slot] * rows, rows)
        total[place] += jnp.dot(
            tiles[0, slot], blocks[pl.ds(start, rows), :], preferred_element_type=jnp.float32
        )

    @pl.loop(0, spare)
    def _(place):
        out[pl.ds(pl.multiple_of(place * rows, rows), rows), :] = total[place].astype(out.dtype)


def visit_tiles(own_tiles, owners, index_args, tile_weights, blocks):
    slots = index_args[-1].shape[1]
    rows = tile_weights.shape[-1]
    places = owners * own_tiles
    hidden = blocks.shape[1]
    return pl.pallas_call(
        functools.partial(visit_kernel, own_tiles, slots // owners),
        out_shape=jax.ShapeDtypeStruct((places * rows, hidden), jnp.bfloat16),
        in_specs=[SMEM] * 4 + [VMEM] * 2,
        out_specs=VMEM,
        scratch_shapes=[pltpu.VMEM((places + 1, rows, hidden), jnp.float32)],
        compiler_params=params(56),
    )(*index_args, tile_weights, blocks)


def swap(value, axis, apart):
    pairs = [(i, i ^ apart) for i in range(lax.axis_size(axis))]
    return lax.ppermute(value, axis, pairs)


def exchange(value, k):
    step = [(2, 4), (4, 2), (6, 6)][k]
    return lax.ppermute(value, "row", [(i, i ^ step[i % 2]) for i in range(lax.axis_size("row"))])


def per_device(
    features,
    weight,
    source_norm,
    target_norm,
    tile_weights,
    tile_source,
    tile_target,
    tile_count,
    mirror_tile,
):
    tile_rows = tile_weights.shape[-1]
    own_rows = features.shape[0]
    own_tiles = own_rows // tile_rows
    owners, columns = lax.axis_size("row"), lax.axis_size("col")
    span = own_tiles * columns
    index_args = (tile_source, tile_target, tile_count, mirror_tile)

    cells = owners * own_tiles * span * tile_rows * tile_rows
    if columns != 4 or owners != 8 or own_tiles & (own_tiles - 1) or cells > DENSE_ELEMENTS:
        projected = jnp.dot(features, weight, preferred_element_type=jnp.float32)
        scaled = (source_norm[:, None] * projected).astype(jnp.bfloat16)
        blocks = lax.all_gather(scaled, "col", axis=0, tiled=True)
        partial_value = visit_tiles(own_tiles, owners, index_args, tile_weights, blocks)
        outgoing = partial_value.reshape(owners, own_rows, -1)
        arrived = lax.all_to_all(outgoing, "row", split_axis=0, concat_axis=0, tiled=True)
        gathered = jnp.sum(arrived.astype(jnp.float32), axis=0) + projected
        return jnp.maximum(target_norm[:, None] * gathered, 0.0).astype(jnp.bfloat16)

    projected, *scaled = project(features, weight, source_norm, CHUNKS)
    built = merge_tiles(own_tiles, owners, span, index_args, tile_weights)
    half = built.shape[0] // 2
    across = [swap(own, "col", 3) for own in scaled]
    beside = [swap(own, "col", 1) for own in scaled]
    onward, matrix = lax.optimization_barrier((across[0], built))
    passed = swap(onward, "col", 1)
    early = early_product(matrix, scaled[0], beside[0], across[0])
    away = late_product(matrix, early, passed, 0, half, jnp.bfloat16, WEIGHTS[0])
    stay = late_product(matrix, early, passed, half, half, jnp.float32, WEIGHTS[1])
    kept, *sent = join(stay, swap(away, "row", 1), own_rows)
    pieces = [[kept, exchange(sent[0], 0)]]

    onward, _ = lax.optimization_barrier((across[1], early))
    blocks = scaled[1], beside[1], swap(onward, "col", 1), across[1]
    blocks, _ = lax.optimization_barrier((blocks, sent))
    away = product(matrix, blocks, 0, half, jnp.bfloat16, WEIGHTS[2])
    sent, away = lax.optimization_barrier((sent, away))
    pieces[0] += [exchange(sent[k], k) for k in (1, 2)]
    stay = product(matrix, blocks, half, half, jnp.float32, WEIGHTS[3])
    kept, *sent = join(stay, swap(away, "row", 1), own_rows)
    pieces.append([kept] + [exchange(value, k) for k, value in enumerate(sent)])
    return finish(projected, target_norm, pieces)


def solution(mesh):
    in_specs = (
        P(("row", "col"), None),
        P(),
        P(("row", "col")),
        P(("row", "col")),
        P(("row", "col"), None, None, None),
        P(("row", "col"), None),
        P(("row", "col"), None),
        P(("row", "col")),
        P(("row", "col"), None),
    )
    out_specs = P(("row", "col"), None)
    return jax.shard_map(
        per_device, mesh=mesh, in_specs=in_specs, out_specs=out_specs, check_vma=False
    )
```

```python
import functools

import jax
import jax.numpy as jnp
from jax import lax
from jax.experimental import pallas as pl
from jax.experimental.pallas import tpu as pltpu
from jax.sharding import PartitionSpec as P

DENSE_ELEMENTS = 4 * 1024 * 1024
CHUNKS = 2
WEIGHTS = (20, 20, 0, 20)
MIB = 1024 * 1024
SMEM = pl.BlockSpec(memory_space=pltpu.SMEM)
VMEM = pl.BlockSpec(memory_space=pltpu.VMEM)
HBM = pl.BlockSpec(memory_space=pltpu.HBM)


def params(mib):
    return pltpu.CompilerParams(vmem_limit_bytes=int(mib * MIB))


def cost(flops, moved):
    return pl.CostEstimate(flops=flops, bytes_accessed=moved, transcendentals=0)


def in_hbm(*values):
    return [pltpu.with_memory_space_constraint(value, pltpu.HBM) for value in values]


def rows_to_lanes(row, lanes):
    return jnp.broadcast_to(row, (lanes, row.shape[1])).T


def project_kernel(features_hbm, weight_hbm, norm_hbm, projected, *refs):
    *scaled, features, weight, norm, sems = refs
    copies = [
        pltpu.make_async_copy(source, target, sems.at[k])
        for k, (source, target) in enumerate(
            [(weight_hbm, weight), (features_hbm, features), (norm_hbm, norm)]
        )
    ]
    for copy in copies:
        copy.start()
    for copy in copies:
        copy.wait()
    lanes = norm.shape[1]
    value = jnp.dot(features[...], weight[...], preferred_element_type=jnp.float32)
    projected[...] = value
    width = scaled[0].shape[1]
    for part in range(norm.shape[0]):
        factor = rows_to_lanes(norm[part : part + 1, :], lanes)
        for column in range(0, value.shape[1], lanes):
            here = slice(part * lanes, (part + 1) * lanes)
            piece = factor * value[here, column : column + lanes]
            target = scaled[column // width]
            start = column % width
            target[here, start : start + lanes] = piece.astype(target.dtype)


def project(features, weight, source_norm, chunks):
    rows, depth = features.shape
    hidden = weight.shape[1]
    norm = source_norm.reshape(-1, 128)
    return pl.pallas_call(
        project_kernel,
        out_shape=[jax.ShapeDtypeStruct((rows, hidden), jnp.float32)]
        + [jax.ShapeDtypeStruct((rows, hidden // chunks), jnp.bfloat16)] * chunks,
        in_specs=[HBM] * 3,
        out_specs=[VMEM] * (1 + chunks),
        scratch_shapes=[
            pltpu.VMEM(features.shape, features.dtype),
            pltpu.VMEM(weight.shape, weight.dtype),
            pltpu.VMEM(norm.shape, norm.dtype),
            pltpu.SemaphoreType.DMA((3,)),
        ],
        compiler_params=params(12),
        cost_estimate=cost(2 * rows * depth * hidden, 2 * depth * (rows + hidden)),
    )(*in_hbm(features, weight, norm))


def merge_kernel(
    own_tiles, per_owner, row, column, count, sources_hbm, targets_hbm, labels_hbm, tiles_hbm, out,
    total, tiles, sources, targets, labels, bases, seen, sems, tile_sems,
):
    small = [
        pltpu.make_async_copy(source, target, sems.at[k])
        for k, (source, target) in enumerate(
            [(sources_hbm, sources), (targets_hbm, targets), (labels_hbm, labels)]
        )
    ]
    parts = tile_sems.shape[0]
    each = tiles.shape[0] // parts
    large = [
        pltpu.make_async_copy(
            tiles_hbm.at[0, pl.ds(k * each, each)],
            tiles.at[pl.ds(k * each, each)],
            tile_sems.at[k],
        )
        for k in range(parts)
    ]
    for copy in small + large:
        copy.start()
    rows = total.shape[1]
    places, span = out.shape[0] // rows, out.shape[1] // rows
    spare = places * span
    for cell in range(spare + 1):
        seen[cell] = 0
    my_core, used = row[0] % 2, count[0]
    toggle = column[0] * own_tiles
    for copy in small:
        copy.wait()

    for slot in range(bases.shape[0]):
        owner, label = slot // per_owner, labels[0, slot]
        core, apart = owner % 2, lax.bitwise_xor(row[0], owner)
        x, y = lax.bitwise_and(apart, 2), lax.bitwise_and(lax.shift_right_logical(apart, 1), 2)
        first, second = (x, y) if core == 0 else (y, x)
        position = jnp.where(my_core == core, 4, 0) + second
        position += lax.shift_right_logical(jnp.where(second == 0, 2 - first, first), 1)
        base = (position * own_tiles + label) * span
        bases[slot] = jnp.where(label < own_tiles, base, spare)

    def add(slot):
        base = bases[targets[0, slot]]
        here = base + lax.bitwise_xor(sources[0, slot], toggle)
        cell = jnp.where((base < spare) & (slot < used), here, spare)
        before = jnp.where(seen[cell] > 0, total[cell], 0.0)
        seen[cell] = 1
        total[cell] = before + tiles[slot].astype(jnp.float32)

    for k, copy in enumerate(large):
        copy.wait()
        pl.loop(k * each, (k + 1) * each, unroll=4)(add)

    for place in range(places):
        for source in range(span):
            cell = place * span + source
            value = jnp.where(seen[cell] > 0, total[cell], 0.0)
            out[place * rows : (place + 1) * rows, source * rows : (source + 1) * rows] = (
                value.astype(out.dtype)
            )


def merge_tiles(own_tiles, owners, span, index_args, tile_weights):
    sources, targets, count, labels = index_args
    _, capacity, rows, _ = tile_weights.shape
    places = owners * own_tiles
    row = lax.axis_index("row").astype(jnp.int32).reshape(1)
    column = lax.axis_index("col").astype(jnp.int32).reshape(1)
    return pl.pallas_call(
        functools.partial(merge_kernel, own_tiles, labels.shape[1] // owners),
        out_shape=jax.ShapeDtypeStruct((places * rows, span * rows), jnp.bfloat16),
        in_specs=[SMEM] * 3 + [HBM] * 4,
        out_specs=VMEM,
        scratch_shapes=[
            pltpu.VMEM((places * span + 1, rows, rows), jnp.float32),
            pltpu.VMEM(tile_weights.shape[1:], tile_weights.dtype),
            pltpu.SMEM(sources.shape, jnp.int32),
            pltpu.SMEM(targets.shape, jnp.int32),
            pltpu.SMEM(labels.shape, jnp.int32),
            pltpu.SMEM((labels.shape[1],), jnp.int32),
            pltpu.SMEM((places * span + 1,), jnp.int32),
            pltpu.SemaphoreType.DMA((3,)),
            pltpu.SemaphoreType.DMA((4 if capacity % 4 == 0 else 1,)),
        ],
        compiler_params=params(24),
        cost_estimate=cost(8 * MIB, 12 * MIB),
    )(row, column, count, *in_hbm(sources, targets, labels, tile_weights))


def early_kernel(matrix, own, beside, across, out):
    rows = own.shape[0]
    value = jnp.dot(matrix[:, :rows], own[...], preferred_element_type=jnp.float32)
    value += jnp.dot(
        matrix[:, rows : 2 * rows], beside[...], preferred_element_type=jnp.float32
    )
    value += jnp.dot(matrix[:, 3 * rows :], across[...], preferred_element_type=jnp.float32)
    out[...] = value


def early_product(matrix, own, beside, across):
    total, depth = matrix.shape
    width = own.shape[1]
    return pl.pallas_call(
        early_kernel,
        out_shape=jax.ShapeDtypeStruct((total, width), jnp.float32),
        in_specs=[VMEM] * 4,
        out_specs=VMEM,
        compiler_params=params(16),
        cost_estimate=cost(total * depth * width, 1),
    )(matrix, own, beside, across)


def late_kernel(first, matrix, early, passed, out):
    rows = passed.shape[0]
    here = slice(first, first + out.shape[0])
    value = early[here, :] + jnp.dot(
        matrix[here, 2 * rows : 3 * rows], passed[...], preferred_element_type=jnp.float32
    )
    out[...] = value.astype(out.dtype)


def late_product(matrix, early, passed, first, count, dtype, weight):
    total, depth = matrix.shape
    width = passed.shape[1]
    return pl.pallas_call(
        functools.partial(late_kernel, first),
        out_shape=jax.ShapeDtypeStruct((count, width), dtype),
        in_specs=[VMEM] * 3,
        out_specs=VMEM,
        compiler_params=params(16),
        cost_estimate=cost(weight * total * depth * width, 1),
    )(matrix, early, passed)


def product_kernel(first, matrix, *refs):
    *blocks, out, gathered = refs
    rows = blocks[0].shape[0]
    for k, block in enumerate(blocks):
        gathered[k * rows : (k + 1) * rows, :] = block[...]
    value = jnp.dot(
        matrix[first : first + out.shape[0], :],
        gathered[...],
        preferred_element_type=jnp.float32,
    )
    out[...] = value.astype(out.dtype)


def product(matrix, blocks, first, count, dtype, weight):
    rows, width = blocks[0].shape
    total, depth = matrix.shape
    return pl.pallas_call(
        functools.partial(product_kernel, first),
        out_shape=jax.ShapeDtypeStruct((count, width), dtype),
        in_specs=[VMEM] * (1 + len(blocks)),
        out_specs=VMEM,
        scratch_shapes=[pltpu.VMEM((depth, width), blocks[0].dtype)],
        compiler_params=params(16),
        cost_estimate=cost(weight * total * depth * width, 1),
    )(matrix, *blocks)


def join_kernel(first, stay, came, *outs):
    start = 0
    for out in outs:
        rows = out.shape[0]
        value = stay[first + start : first + start + rows, :]
        out[...] = (value + came[start : start + rows, :].astype(jnp.float32)).astype(out.dtype)
        start += rows


def join(stay, came, first, rows, dtypes):
    width = stay.shape[1]
    return pl.pallas_call(
        functools.partial(join_kernel, first),
        out_shape=[jax.ShapeDtypeStruct((rows, width), dtype) for dtype in dtypes],
        in_specs=[VMEM] * 2,
        out_specs=[VMEM] * len(dtypes),
        compiler_params=params(12),
        cost_estimate=cost(1, 1),
    )(stay, came)


def finish_kernel(chunks, projected, norm, *refs):
    out = refs[-1]
    per_chunk = (len(refs) - 1) // chunks
    lanes = norm.shape[1]
    width = refs[0].shape[1]
    for part in range(norm.shape[0]):
        factor = rows_to_lanes(norm[part : part + 1, :], lanes)
        here = slice(part * lanes, (part + 1) * lanes)
        for column in range(0, out.shape[1], lanes):
            pieces = refs[column // width * per_chunk : (column // width + 1) * per_chunk]
            start = column % width
            value = projected[here, column : column + lanes]
            for piece in pieces:
                value += piece[here, start : start + lanes].astype(jnp.float32)
            out[here, column : column + lanes] = jnp.maximum(factor * value, 0.0).astype(out.dtype)


def finish(projected, target_norm, pieces):
    rows, hidden = projected.shape
    flat = [piece for chunk in pieces for piece in chunk]
    return pl.pallas_call(
        functools.partial(finish_kernel, len(pieces)),
        out_shape=jax.ShapeDtypeStruct((rows, hidden), jnp.bfloat16),
        in_specs=[VMEM] * (2 + len(flat)),
        out_specs=VMEM,
        compiler_params=params(12),
        cost_estimate=cost(6 * rows * hidden, 16 * rows * hidden),
    )(projected, target_norm.reshape(-1, 128), *flat)


def visit_kernel(own_tiles, per_owner, sources, targets, count, labels, tiles, blocks, out, total):
    spare, rows = total.shape[0] - 1, total.shape[1]
    total[...] = jnp.zeros_like(total)

    @pl.loop(0, count[0])
    def _(slot):
        target = targets[0, slot]
        label = labels[0, target]
        place = jnp.where(label < own_tiles, target // per_owner * own_tiles + label, spare)
        start = pl.multiple_of(sources[0, slot] * rows, rows)
        total[place] += jnp.dot(
            tiles[0, slot], blocks[pl.ds(start, rows), :], preferred_element_type=jnp.float32
        )

    @pl.loop(0, spare)
    def _(place):
        out[pl.ds(pl.multiple_of(place * rows, rows), rows), :] = total[place].astype(out.dtype)


def visit_tiles(own_tiles, owners, index_args, tile_weights, blocks):
    slots = index_args[-1].shape[1]
    rows = tile_weights.shape[-1]
    places = owners * own_tiles
    hidden = blocks.shape[1]
    return pl.pallas_call(
        functools.partial(visit_kernel, own_tiles, slots // owners),
        out_shape=jax.ShapeDtypeStruct((places * rows, hidden), jnp.bfloat16),
        in_specs=[SMEM] * 4 + [VMEM] * 2,
        out_specs=VMEM,
        scratch_shapes=[pltpu.VMEM((places + 1, rows, hidden), jnp.float32)],
        compiler_params=params(56),
    )(*index_args, tile_weights, blocks)


def swap(value, axis, apart):
    pairs = [(i, i ^ apart) for i in range(lax.axis_size(axis))]
    return lax.ppermute(value, axis, pairs)


def exchange(sent):
    owners = lax.axis_size("row")
    steps = [(2, 4), (4, 2), (6, 6)]
    return [
        lax.ppermute(value, "row", [(i, i ^ step[i % 2]) for i in range(owners)])
        for value, step in zip(sent, steps)
    ]


def per_device(
    features,
    weight,
    source_norm,
    target_norm,
    tile_weights,
    tile_source,
    tile_target,
    tile_count,
    mirror_tile,
):
    tile_rows = tile_weights.shape[-1]
    own_rows = features.shape[0]
    own_tiles = own_rows // tile_rows
    owners, columns = lax.axis_size("row"), lax.axis_size("col")
    span = own_tiles * columns
    index_args = (tile_source, tile_target, tile_count, mirror_tile)

    cells = owners * own_tiles * span * tile_rows * tile_rows
    if columns != 4 or owners != 8 or own_tiles & (own_tiles - 1) or cells > DENSE_ELEMENTS:
        projected = jnp.dot(features, weight, preferred_element_type=jnp.float32)
        scaled = (source_norm[:, None] * projected).astype(jnp.bfloat16)
        blocks = lax.all_gather(scaled, "col", axis=0, tiled=True)
        partial_value = visit_tiles(own_tiles, owners, index_args, tile_weights, blocks)
        outgoing = partial_value.reshape(owners, own_rows, -1)
        arrived = lax.all_to_all(outgoing, "row", split_axis=0, concat_axis=0, tiled=True)
        gathered = jnp.sum(arrived.astype(jnp.float32), axis=0) + projected
        return jnp.maximum(target_norm[:, None] * gathered, 0.0).astype(jnp.bfloat16)

    projected, *scaled = project(features, weight, source_norm, CHUNKS)
    built = merge_tiles(own_tiles, owners, span, index_args, tile_weights)
    half = built.shape[0] // 2
    across = [swap(own, "col", 3) for own in scaled]
    beside = [swap(own, "col", 1) for own in scaled]
    onward, matrix = lax.optimization_barrier((across[0], built))
    passed = swap(onward, "col", 1)
    early = early_product(matrix, scaled[0], beside[0], across[0])
    away = [
        late_product(matrix, early, passed, start, count, jnp.bfloat16, WEIGHTS[0])
        for start, count in ((0, own_rows), (own_rows, half - own_rows))
    ]
    stay = late_product(matrix, early, passed, half, half, jnp.float32, WEIGHTS[1])
    came = [swap(value, "row", 1) for value in away]
    (lead,) = join(stay, came[0], 0, own_rows, [jnp.bfloat16])
    kept, *sent = join(stay, came[1], own_rows, own_rows, [jnp.float32] + [jnp.bfloat16] * 2)
    pieces = [[kept] + exchange([lead] + sent)]

    onward, _ = lax.optimization_barrier((across[1], early))
    blocks = scaled[1], beside[1], swap(onward, "col", 1), across[1]
    blocks, _ = lax.optimization_barrier((blocks, sent))
    away = product(matrix, blocks, 0, half, jnp.bfloat16, WEIGHTS[2])
    stay = product(matrix, blocks, half, half, jnp.float32, WEIGHTS[3])
    came = swap(away, "row", 1)
    lead, kept, *sent = join(
        stay, came, 0, own_rows, [jnp.bfloat16, jnp.float32] + [jnp.bfloat16] * 2
    )
    pieces.append([kept] + exchange([lead] + sent))
    return finish(projected, target_norm, pieces)


def solution(mesh):
    in_specs = (
        P(("row", "col"), None),
        P(),
        P(("row", "col")),
        P(("row", "col")),
        P(("row", "col"), None, None, None),
        P(("row", "col"), None),
        P(("row", "col"), None),
        P(("row", "col")),
        P(("row", "col"), None),
    )
    out_specs = P(("row", "col"), None)
    return jax.shard_map(
        per_device, mesh=mesh, in_specs=in_specs, out_specs=out_specs, check_vma=False
    )
```

```python
import functools

import jax
import jax.numpy as jnp
from jax import lax
from jax.experimental import pallas as pl
from jax.experimental.pallas import tpu as pltpu
from jax.sharding import PartitionSpec as P

DENSE_ELEMENTS = 4 * 1024 * 1024
CHUNKS = 2
WEIGHTS = (20, 20, 0, 20)
MIB = 1024 * 1024
SMEM = pl.BlockSpec(memory_space=pltpu.SMEM)
VMEM = pl.BlockSpec(memory_space=pltpu.VMEM)
HBM = pl.BlockSpec(memory_space=pltpu.HBM)


def params(mib):
    return pltpu.CompilerParams(vmem_limit_bytes=int(mib * MIB))


def cost(flops, moved):
    return pl.CostEstimate(flops=flops, bytes_accessed=moved, transcendentals=0)


def in_hbm(*values):
    return [pltpu.with_memory_space_constraint(value, pltpu.HBM) for value in values]


def rows_to_lanes(row, lanes):
    return jnp.broadcast_to(row, (lanes, row.shape[1])).T


def project_kernel(features_hbm, weight_hbm, norm_hbm, projected, *refs):
    *scaled, features, weight, norm, sems = refs
    width, lanes = scaled[0].shape[1], norm.shape[1]
    spans = [slice(k * width, (k + 1) * width) for k in range(len(scaled))]
    copies = [
        pltpu.make_async_copy(features_hbm, features, sems.at[0]),
        pltpu.make_async_copy(norm_hbm, norm, sems.at[1]),
    ]
    copies += [
        pltpu.make_async_copy(weight_hbm.at[:, span], weight.at[:, span], sems.at[2 + k])
        for k, span in enumerate(spans)
    ]
    for k in (0, 2, 1, *range(3, len(copies))):
        copies[k].start()
    copies[0].wait()
    copies[1].wait()
    for k, (span, target) in enumerate(zip(spans, scaled)):
        copies[2 + k].wait()
        value = jnp.dot(features[...], weight[:, span], preferred_element_type=jnp.float32)
        projected[:, span] = value
        for part in range(norm.shape[0]):
            factor = rows_to_lanes(norm[part : part + 1, :], lanes)
            here = slice(part * lanes, (part + 1) * lanes)
            for column in range(0, width, lanes):
                piece = factor * value[here, column : column + lanes]
                target[here, column : column + lanes] = piece.astype(target.dtype)


def project(features, weight, source_norm, chunks):
    rows, depth = features.shape
    hidden = weight.shape[1]
    norm = source_norm.reshape(-1, 128)
    return pl.pallas_call(
        project_kernel,
        out_shape=[jax.ShapeDtypeStruct((rows, hidden), jnp.float32)]
        + [jax.ShapeDtypeStruct((rows, hidden // chunks), jnp.bfloat16)] * chunks,
        in_specs=[HBM] * 3,
        out_specs=[VMEM] * (1 + chunks),
        scratch_shapes=[
            pltpu.VMEM(features.shape, features.dtype),
            pltpu.VMEM(weight.shape, weight.dtype),
            pltpu.VMEM(norm.shape, norm.dtype),
            pltpu.SemaphoreType.DMA((2 + chunks,)),
        ],
        compiler_params=params(12),
        cost_estimate=cost(2 * rows * depth * hidden, 2 * depth * (rows + hidden)),
    )(*in_hbm(features, weight, norm))


def merge_kernel(
    own_tiles, per_owner, row, column, count, sources_hbm, targets_hbm, labels_hbm, tiles_hbm, out,
    total, tiles, sources, targets, labels, bases, seen, sems, tile_sems,
):
    small = [
        pltpu.make_async_copy(source, target, sems.at[k])
        for k, (source, target) in enumerate(
            [(sources_hbm, sources), (targets_hbm, targets), (labels_hbm, labels)]
        )
    ]
    parts = tile_sems.shape[0]
    each = tiles.shape[0] // parts
    large = [
        pltpu.make_async_copy(
            tiles_hbm.at[0, pl.ds(k * each, each)],
            tiles.at[pl.ds(k * each, each)],
            tile_sems.at[k],
        )
        for k in range(parts)
    ]
    for copy in small + large:
        copy.start()
    rows = total.shape[1]
    places, span = out.shape[0] // rows, out.shape[1] // rows
    spare = places * span
    for cell in range(spare + 1):
        seen[cell] = 0
    my_core, used = row[0] % 2, count[0]
    toggle = column[0] * own_tiles
    for copy in small:
        copy.wait()

    for slot in range(bases.shape[0]):
        owner, label = slot // per_owner, labels[0, slot]
        core, apart = owner % 2, lax.bitwise_xor(row[0], owner)
        x, y = lax.bitwise_and(apart, 2), lax.bitwise_and(lax.shift_right_logical(apart, 1), 2)
        first, second = (x, y) if core == 0 else (y, x)
        position = jnp.where(my_core == core, 4, 0) + second
        position += lax.shift_right_logical(jnp.where(second == 0, 2 - first, first), 1)
        base = (position * own_tiles + label) * span
        bases[slot] = jnp.where(label < own_tiles, base, spare)

    def add(slot):
        base = bases[targets[0, slot]]
        here = base + lax.bitwise_xor(sources[0, slot], toggle)
        cell = jnp.where((base < spare) & (slot < used), here, spare)
        before = jnp.where(seen[cell] > 0, total[cell], 0.0)
        seen[cell] = 1
        total[cell] = before + tiles[slot].astype(jnp.float32)

    for k, copy in enumerate(large):
        copy.wait()
        pl.loop(k * each, (k + 1) * each, unroll=4)(add)

    for place in range(places):
        for source in range(span):
            cell = place * span + source
            value = jnp.where(seen[cell] > 0, total[cell], 0.0)
            out[place * rows : (place + 1) * rows, source * rows : (source + 1) * rows] = (
                value.astype(out.dtype)
            )


def merge_tiles(own_tiles, owners, span, index_args, tile_weights):
    sources, targets, count, labels = index_args
    _, capacity, rows, _ = tile_weights.shape
    places = owners * own_tiles
    row = lax.axis_index("row").astype(jnp.int32).reshape(1)
    column = lax.axis_index("col").astype(jnp.int32).reshape(1)
    return pl.pallas_call(
        functools.partial(merge_kernel, own_tiles, labels.shape[1] // owners),
        out_shape=jax.ShapeDtypeStruct((places * rows, span * rows), jnp.bfloat16),
        in_specs=[SMEM] * 3 + [HBM] * 4,
        out_specs=VMEM,
        scratch_shapes=[
            pltpu.VMEM((places * span + 1, rows, rows), jnp.float32),
            pltpu.VMEM(tile_weights.shape[1:], tile_weights.dtype),
            pltpu.SMEM(sources.shape, jnp.int32),
            pltpu.SMEM(targets.shape, jnp.int32),
            pltpu.SMEM(labels.shape, jnp.int32),
            pltpu.SMEM((labels.shape[1],), jnp.int32),
            pltpu.SMEM((places * span + 1,), jnp.int32),
            pltpu.SemaphoreType.DMA((3,)),
            pltpu.SemaphoreType.DMA((4 if capacity % 4 == 0 else 1,)),
        ],
        compiler_params=params(24),
        cost_estimate=cost(8 * MIB, 12 * MIB),
    )(row, column, count, *in_hbm(sources, targets, labels, tile_weights))


def early_kernel(matrix, own, beside, across, out):
    rows = own.shape[0]
    value = jnp.dot(matrix[:, :rows], own[...], preferred_element_type=jnp.float32)
    value += jnp.dot(
        matrix[:, rows : 2 * rows], beside[...], preferred_element_type=jnp.float32
    )
    value += jnp.dot(matrix[:, 3 * rows :], across[...], preferred_element_type=jnp.float32)
    out[...] = value


def early_product(matrix, own, beside, across):
    total, depth = matrix.shape
    width = own.shape[1]
    return pl.pallas_call(
        early_kernel,
        out_shape=jax.ShapeDtypeStruct((total, width), jnp.float32),
        in_specs=[VMEM] * 4,
        out_specs=VMEM,
        compiler_params=params(16),
        cost_estimate=cost(total * depth * width, 1),
    )(matrix, own, beside, across)


def late_kernel(first, matrix, early, passed, out):
    rows = passed.shape[0]
    here = slice(first, first + out.shape[0])
    value = early[here, :] + jnp.dot(
        matrix[here, 2 * rows : 3 * rows], passed[...], preferred_element_type=jnp.float32
    )
    out[...] = value.astype(out.dtype)


def late_product(matrix, early, passed, first, count, dtype, weight):
    total, depth = matrix.shape
    width = passed.shape[1]
    return pl.pallas_call(
        functools.partial(late_kernel, first),
        out_shape=jax.ShapeDtypeStruct((count, width), dtype),
        in_specs=[VMEM] * 3,
        out_specs=VMEM,
        compiler_params=params(16),
        cost_estimate=cost(weight * total * depth * width, 1),
    )(matrix, early, passed)


def product_kernel(first, matrix, *refs):
    *blocks, out, gathered = refs
    rows = blocks[0].shape[0]
    for k, block in enumerate(blocks):
        gathered[k * rows : (k + 1) * rows, :] = block[...]
    value = jnp.dot(
        matrix[first : first + out.shape[0], :],
        gathered[...],
        preferred_element_type=jnp.float32,
    )
    out[...] = value.astype(out.dtype)


def product(matrix, blocks, first, count, dtype, weight):
    rows, width = blocks[0].shape
    total, depth = matrix.shape
    return pl.pallas_call(
        functools.partial(product_kernel, first),
        out_shape=jax.ShapeDtypeStruct((count, width), dtype),
        in_specs=[VMEM] * (1 + len(blocks)),
        out_specs=VMEM,
        scratch_shapes=[pltpu.VMEM((depth, width), blocks[0].dtype)],
        compiler_params=params(16),
        cost_estimate=cost(weight * total * depth * width, 1),
    )(matrix, *blocks)


def join_kernel(first, stay, came, *outs):
    start = 0
    for out in outs:
        rows = out.shape[0]
        value = stay[first + start : first + start + rows, :]
        out[...] = (value + came[start : start + rows, :].astype(jnp.float32)).astype(out.dtype)
        start += rows


def join(stay, came, first, rows, dtypes):
    width = stay.shape[1]
    return pl.pallas_call(
        functools.partial(join_kernel, first),
        out_shape=[jax.ShapeDtypeStruct((rows, width), dtype) for dtype in dtypes],
        in_specs=[VMEM] * 2,
        out_specs=[VMEM] * len(dtypes),
        compiler_params=params(12),
        cost_estimate=cost(1, 1),
    )(stay, came)


def activate(projected, norm, pieces, start, out):
    lanes = norm.shape[1]
    for part in range(norm.shape[0]):
        factor = rows_to_lanes(norm[part : part + 1, :], lanes)
        here = slice(part * lanes, (part + 1) * lanes)
        for column in range(0, out.shape[1], lanes):
            span = slice(column, column + lanes)
            value = projected[here, start + column : start + column + lanes]
            for piece in pieces:
                value += piece[here, span].astype(jnp.float32)
            out[here, span] = jnp.maximum(factor * value, 0.0).astype(out.dtype)


def first_kernel(projected, norm, *refs):
    *pieces, out = refs
    activate(projected, norm, pieces, 0, out)


def last_kernel(ready, projected, norm, *refs):
    *pieces, out, rest, sems = refs
    width = ready.shape[1]
    early = pltpu.make_async_copy(ready, out.at[:, :width], sems.at[0])
    early.start()
    activate(projected, norm, pieces, width, rest)
    late = pltpu.make_async_copy(rest, out.at[:, width:], sems.at[1])
    late.start()
    early.wait()
    late.wait()


def finish(projected, target_norm, pieces):
    rows, hidden = projected.shape
    norm = target_norm.reshape(-1, 128)
    width = pieces[0][0].shape[1]
    ready = pl.pallas_call(
        first_kernel,
        out_shape=jax.ShapeDtypeStruct((rows, width), jnp.bfloat16),
        in_specs=[VMEM] * (2 + len(pieces[0])),
        out_specs=VMEM,
        compiler_params=params(12),
        cost_estimate=cost(6 * rows * width, 16 * rows * width),
    )(projected, norm, *pieces[0])
    return pl.pallas_call(
        last_kernel,
        out_shape=jax.ShapeDtypeStruct((rows, hidden), jnp.bfloat16),
        in_specs=[VMEM] * (3 + len(pieces[1])),
        out_specs=HBM,
        scratch_shapes=[
            pltpu.VMEM((rows, hidden - width), jnp.bfloat16),
            pltpu.SemaphoreType.DMA((2,)),
        ],
        compiler_params=params(12),
        cost_estimate=cost(6 * rows * width, 16 * rows * width),
    )(ready, projected, norm, *pieces[1])


def visit_kernel(own_tiles, per_owner, sources, targets, count, labels, tiles, blocks, out, total):
    spare, rows = total.shape[0] - 1, total.shape[1]
    total[...] = jnp.zeros_like(total)

    @pl.loop(0, count[0])
    def _(slot):
        target = targets[0, slot]
        label = labels[0, target]
        place = jnp.where(label < own_tiles, target // per_owner * own_tiles + label, spare)
        start = pl.multiple_of(sources[0, slot] * rows, rows)
        total[place] += jnp.dot(
            tiles[0, slot], blocks[pl.ds(start, rows), :], preferred_element_type=jnp.float32
        )

    @pl.loop(0, spare)
    def _(place):
        out[pl.ds(pl.multiple_of(place * rows, rows), rows), :] = total[place].astype(out.dtype)


def visit_tiles(own_tiles, owners, index_args, tile_weights, blocks):
    slots = index_args[-1].shape[1]
    rows = tile_weights.shape[-1]
    places = owners * own_tiles
    hidden = blocks.shape[1]
    return pl.pallas_call(
        functools.partial(visit_kernel, own_tiles, slots // owners),
        out_shape=jax.ShapeDtypeStruct((places * rows, hidden), jnp.bfloat16),
        in_specs=[SMEM] * 4 + [VMEM] * 2,
        out_specs=VMEM,
        scratch_shapes=[pltpu.VMEM((places + 1, rows, hidden), jnp.float32)],
        compiler_params=params(56),
    )(*index_args, tile_weights, blocks)


def swap(value, axis, apart):
    pairs = [(i, i ^ apart) for i in range(lax.axis_size(axis))]
    return lax.ppermute(value, axis, pairs)


def exchange(sent):
    owners = lax.axis_size("row")
    steps = [(2, 4), (4, 2), (6, 6)]
    return [
        lax.ppermute(value, "row", [(i, i ^ step[i % 2]) for i in range(owners)])
        for value, step in zip(sent, steps)
    ]


def per_device(
    features,
    weight,
    source_norm,
    target_norm,
    tile_weights,
    tile_source,
    tile_target,
    tile_count,
    mirror_tile,
):
    tile_rows = tile_weights.shape[-1]
    own_rows = features.shape[0]
    own_tiles = own_rows // tile_rows
    owners, columns = lax.axis_size("row"), lax.axis_size("col")
    span = own_tiles * columns
    index_args = (tile_source, tile_target, tile_count, mirror_tile)

    cells = owners * own_tiles * span * tile_rows * tile_rows
    if columns != 4 or owners != 8 or own_tiles & (own_tiles - 1) or cells > DENSE_ELEMENTS:
        projected = jnp.dot(features, weight, preferred_element_type=jnp.float32)
        scaled = (source_norm[:, None] * projected).astype(jnp.bfloat16)
        blocks = lax.all_gather(scaled, "col", axis=0, tiled=True)
        partial_value = visit_tiles(own_tiles, owners, index_args, tile_weights, blocks)
        outgoing = partial_value.reshape(owners, own_rows, -1)
        arrived = lax.all_to_all(outgoing, "row", split_axis=0, concat_axis=0, tiled=True)
        gathered = jnp.sum(arrived.astype(jnp.float32), axis=0) + projected
        return jnp.maximum(target_norm[:, None] * gathered, 0.0).astype(jnp.bfloat16)

    projected, *scaled = project(features, weight, source_norm, CHUNKS)
    built = merge_tiles(own_tiles, owners, span, index_args, tile_weights)
    half = built.shape[0] // 2
    across = [swap(own, "col", 3) for own in scaled]
    beside = [swap(own, "col", 1) for own in scaled]
    onward, matrix = lax.optimization_barrier((across[0], built))
    passed = swap(onward, "col", 1)
    early = early_product(matrix, scaled[0], beside[0], across[0])
    away = [
        late_product(matrix, early, passed, start, count, jnp.bfloat16, WEIGHTS[0])
        for start, count in ((0, own_rows), (own_rows, half - own_rows))
    ]
    stay = late_product(matrix, early, passed, half, half, jnp.float32, WEIGHTS[1])
    came = [swap(value, "row", 1) for value in away]
    (lead,) = join(stay, came[0], 0, own_rows, [jnp.bfloat16])
    kept, *sent = join(stay, came[1], own_rows, own_rows, [jnp.float32] + [jnp.bfloat16] * 2)
    pieces = [[kept] + exchange([lead] + sent)]

    onward, _ = lax.optimization_barrier((across[1], early))
    blocks = scaled[1], beside[1], swap(onward, "col", 1), across[1]
    blocks, _ = lax.optimization_barrier((blocks, sent))
    away = product(matrix, blocks, 0, half, jnp.bfloat16, WEIGHTS[2])
    stay = product(matrix, blocks, half, half, jnp.float32, WEIGHTS[3])
    came = swap(away, "row", 1)
    lead, kept, *sent = join(
        stay, came, 0, own_rows, [jnp.bfloat16, jnp.float32] + [jnp.bfloat16] * 2
    )
    pieces.append([kept] + exchange([lead] + sent))
    return finish(projected, target_norm, pieces)


def solution(mesh):
    in_specs = (
        P(("row", "col"), None),
        P(),
        P(("row", "col")),
        P(("row", "col")),
        P(("row", "col"), None, None, None),
        P(("row", "col"), None),
        P(("row", "col"), None),
        P(("row", "col")),
        P(("row", "col"), None),
    )
    out_specs = P(("row", "col"), None)
    return jax.shard_map(
        per_device, mesh=mesh, in_specs=in_specs, out_specs=out_specs, check_vma=False
    )
```

```python
import functools

import jax
import jax.numpy as jnp
from jax import lax
from jax.experimental import pallas as pl
from jax.experimental.pallas import tpu as pltpu
from jax.sharding import PartitionSpec as P

DENSE_ELEMENTS = 4 * 1024 * 1024
CHUNKS = 2
WEIGHTS = (20, 20, 0, 20)
MIB = 1024 * 1024
SMEM = pl.BlockSpec(memory_space=pltpu.SMEM)
VMEM = pl.BlockSpec(memory_space=pltpu.VMEM)
HBM = pl.BlockSpec(memory_space=pltpu.HBM)


def params(mib):
    return pltpu.CompilerParams(vmem_limit_bytes=int(mib * MIB))


def cost(flops, moved):
    return pl.CostEstimate(flops=flops, bytes_accessed=moved, transcendentals=0)


def in_hbm(*values):
    return [pltpu.with_memory_space_constraint(value, pltpu.HBM) for value in values]


def rows_to_lanes(row, lanes):
    return jnp.broadcast_to(row, (lanes, row.shape[1])).T


def project_kernel(features_hbm, weight_hbm, norm_hbm, projected, *refs):
    *scaled, features, weight, norm, sems = refs
    width, lanes = scaled[0].shape[1], norm.shape[1]
    half = weight.shape[0] // 2
    top, bottom = slice(0, half), slice(half, 2 * half)
    copies = [
        pltpu.make_async_copy(source, target, sems.at[k])
        for k, (source, target) in enumerate(
            [
                (weight_hbm.at[top], weight.at[top]),
                (features_hbm, features),
                (norm_hbm, norm),
                (weight_hbm.at[bottom], weight.at[bottom]),
            ]
        )
    ]
    for copy in copies:
        copy.start()
    for copy in copies[:3]:
        copy.wait()
    value = jnp.dot(features[:, top], weight[top, :], preferred_element_type=jnp.float32)
    copies[3].wait()
    value += jnp.dot(features[:, bottom], weight[bottom, :], preferred_element_type=jnp.float32)
    projected[...] = value
    for part in range(norm.shape[0]):
        factor = rows_to_lanes(norm[part : part + 1, :], lanes)
        for column in range(0, value.shape[1], lanes):
            piece = value[part * lanes : (part + 1) * lanes, column : column + lanes]
            target = scaled[column // width]
            start = column % width
            target[part * lanes : (part + 1) * lanes, start : start + lanes] = (
                factor * piece
            ).astype(target.dtype)


def project(features, weight, source_norm, chunks):
    rows, depth = features.shape
    hidden = weight.shape[1]
    norm = source_norm.reshape(-1, 128)
    return pl.pallas_call(
        project_kernel,
        out_shape=[jax.ShapeDtypeStruct((rows, hidden), jnp.float32)]
        + [jax.ShapeDtypeStruct((rows, hidden // chunks), jnp.bfloat16)] * chunks,
        in_specs=[HBM] * 3,
        out_specs=[VMEM] * (1 + chunks),
        scratch_shapes=[
            pltpu.VMEM(features.shape, features.dtype),
            pltpu.VMEM(weight.shape, weight.dtype),
            pltpu.VMEM(norm.shape, norm.dtype),
            pltpu.SemaphoreType.DMA((4,)),
        ],
        compiler_params=params(12),
        cost_estimate=cost(2 * rows * depth * hidden, 2 * depth * (rows + hidden)),
    )(*in_hbm(features, weight, norm))


def merge_kernel(
    own_tiles, per_owner, row, column, count, sources_hbm, targets_hbm, labels_hbm, tiles_hbm, out,
    total, tiles, sources, targets, labels, bases, seen, sems, tile_sems,
):
    small = [
        pltpu.make_async_copy(source, target, sems.at[k])
        for k, (source, target) in enumerate(
            [(sources_hbm, sources), (targets_hbm, targets), (labels_hbm, labels)]
        )
    ]
    parts = tile_sems.shape[0]
    each = tiles.shape[0] // parts
    large = [
        pltpu.make_async_copy(
            tiles_hbm.at[0, pl.ds(k * each, each)],
            tiles.at[pl.ds(k * each, each)],
            tile_sems.at[k],
        )
        for k in range(parts)
    ]
    for copy in small + large:
        copy.start()
    rows = total.shape[1]
    places, span = out.shape[0] // rows, out.shape[1] // rows
    spare = places * span
    for cell in range(spare + 1):
        seen[cell] = 0
    my_core, used = row[0] % 2, count[0]
    toggle = column[0] * own_tiles
    for copy in small:
        copy.wait()

    for slot in range(bases.shape[0]):
        owner, label = slot // per_owner, labels[0, slot]
        core, apart = owner % 2, lax.bitwise_xor(row[0], owner)
        x, y = lax.bitwise_and(apart, 2), lax.bitwise_and(lax.shift_right_logical(apart, 1), 2)
        first, second = (x, y) if core == 0 else (y, x)
        position = jnp.where(my_core == core, 4, 0) + second
        position += lax.shift_right_logical(jnp.where(second == 0, 2 - first, first), 1)
        base = (position * own_tiles + label) * span
        bases[slot] = jnp.where(label < own_tiles, base, spare)

    def add(slot):
        base = bases[targets[0, slot]]
        here = base + lax.bitwise_xor(sources[0, slot], toggle)
        cell = jnp.where((base < spare) & (slot < used), here, spare)
        before = jnp.where(seen[cell] > 0, total[cell], 0.0)
        seen[cell] = 1
        total[cell] = before + tiles[slot].astype(jnp.float32)

    for k, copy in enumerate(large):
        copy.wait()
        pl.loop(k * each, (k + 1) * each, unroll=4)(add)

    for place in range(places):
        for source in range(span):
            cell = place * span + source
            value = jnp.where(seen[cell] > 0, total[cell], 0.0)
            out[place * rows : (place + 1) * rows, source * rows : (source + 1) * rows] = (
                value.astype(out.dtype)
            )


def merge_tiles(own_tiles, owners, span, index_args, tile_weights):
    sources, targets, count, labels = index_args
    _, capacity, rows, _ = tile_weights.shape
    places = owners * own_tiles
    row = lax.axis_index("row").astype(jnp.int32).reshape(1)
    column = lax.axis_index("col").astype(jnp.int32).reshape(1)
    return pl.pallas_call(
        functools.partial(merge_kernel, own_tiles, labels.shape[1] // owners),
        out_shape=jax.ShapeDtypeStruct((places * rows, span * rows), jnp.bfloat16),
        in_specs=[SMEM] * 3 + [HBM] * 4,
        out_specs=VMEM,
        scratch_shapes=[
            pltpu.VMEM((places * span + 1, rows, rows), jnp.float32),
            pltpu.VMEM(tile_weights.shape[1:], tile_weights.dtype),
            pltpu.SMEM(sources.shape, jnp.int32),
            pltpu.SMEM(targets.shape, jnp.int32),
            pltpu.SMEM(labels.shape, jnp.int32),
            pltpu.SMEM((labels.shape[1],), jnp.int32),
            pltpu.SMEM((places * span + 1,), jnp.int32),
            pltpu.SemaphoreType.DMA((3,)),
            pltpu.SemaphoreType.DMA((4 if capacity % 4 == 0 else 1,)),
        ],
        compiler_params=params(24),
        cost_estimate=cost(8 * MIB, 12 * MIB),
    )(row, column, count, *in_hbm(sources, targets, labels, tile_weights))


def early_kernel(matrix, own, beside, across, out):
    rows = own.shape[0]
    value = jnp.dot(matrix[:, :rows], own[...], preferred_element_type=jnp.float32)
    value += jnp.dot(
        matrix[:, rows : 2 * rows], beside[...], preferred_element_type=jnp.float32
    )
    value += jnp.dot(matrix[:, 3 * rows :], across[...], preferred_element_type=jnp.float32)
    out[...] = value


def early_product(matrix, own, beside, across):
    total, depth = matrix.shape
    width = own.shape[1]
    return pl.pallas_call(
        early_kernel,
        out_shape=jax.ShapeDtypeStruct((total, width), jnp.float32),
        in_specs=[VMEM] * 4,
        out_specs=VMEM,
        compiler_params=params(16),
        cost_estimate=cost(total * depth * width, 1),
    )(matrix, own, beside, across)


def late_kernel(first, matrix, early, passed, out):
    rows = passed.shape[0]
    here = slice(first, first + out.shape[0])
    value = early[here, :] + jnp.dot(
        matrix[here, 2 * rows : 3 * rows], passed[...], preferred_element_type=jnp.float32
    )
    out[...] = value.astype(out.dtype)


def late_product(matrix, early, passed, first, count, dtype, weight):
    total, depth = matrix.shape
    width = passed.shape[1]
    return pl.pallas_call(
        functools.partial(late_kernel, first),
        out_shape=jax.ShapeDtypeStruct((count, width), dtype),
        in_specs=[VMEM] * 3,
        out_specs=VMEM,
        compiler_params=params(16),
        cost_estimate=cost(weight * total * depth * width, 1),
    )(matrix, early, passed)


def product_kernel(first, matrix, *refs):
    *blocks, out, gathered = refs
    rows = blocks[0].shape[0]
    for k, block in enumerate(blocks):
        gathered[k * rows : (k + 1) * rows, :] = block[...]
    value = jnp.dot(
        matrix[first : first + out.shape[0], :],
        gathered[...],
        preferred_element_type=jnp.float32,
    )
    out[...] = value.astype(out.dtype)


def product(matrix, blocks, first, count, dtype, weight):
    rows, width = blocks[0].shape
    total, depth = matrix.shape
    return pl.pallas_call(
        functools.partial(product_kernel, first),
        out_shape=jax.ShapeDtypeStruct((count, width), dtype),
        in_specs=[VMEM] * (1 + len(blocks)),
        out_specs=VMEM,
        scratch_shapes=[pltpu.VMEM((depth, width), blocks[0].dtype)],
        compiler_params=params(16),
        cost_estimate=cost(weight * total * depth * width, 1),
    )(matrix, *blocks)


def join_kernel(first, stay, came, *outs):
    start = 0
    for out in outs:
        rows = out.shape[0]
        value = stay[first + start : first + start + rows, :]
        out[...] = (value + came[start : start + rows, :].astype(jnp.float32)).astype(out.dtype)
        start += rows


def join(stay, came, first, rows, dtypes):
    width = stay.shape[1]
    return pl.pallas_call(
        functools.partial(join_kernel, first),
        out_shape=[jax.ShapeDtypeStruct((rows, width), dtype) for dtype in dtypes],
        in_specs=[VMEM] * 2,
        out_specs=[VMEM] * len(dtypes),
        compiler_params=params(12),
        cost_estimate=cost(1, 1),
    )(stay, came)


def activate(projected, norm, pieces, start, out):
    lanes = norm.shape[1]
    for part in range(norm.shape[0]):
        factor = rows_to_lanes(norm[part : part + 1, :], lanes)
        here = slice(part * lanes, (part + 1) * lanes)
        for column in range(0, out.shape[1], lanes):
            span = slice(column, column + lanes)
            value = projected[here, start + column : start + column + lanes]
            for piece in pieces:
                value += piece[here, span].astype(jnp.float32)
            out[here, span] = jnp.maximum(factor * value, 0.0).astype(out.dtype)


def first_kernel(projected, norm, *refs):
    *pieces, out = refs
    activate(projected, norm, pieces, 0, out)


def last_kernel(ready, projected, norm, *refs):
    *pieces, out, rest, sems = refs
    width = ready.shape[1]
    early = pltpu.make_async_copy(ready, out.at[:, :width], sems.at[0])
    early.start()
    activate(projected, norm, pieces, width, rest)
    late = pltpu.make_async_copy(rest, out.at[:, width:], sems.at[1])
    late.start()
    early.wait()
    late.wait()


def finish(projected, target_norm, pieces):
    rows, hidden = projected.shape
    norm = target_norm.reshape(-1, 128)
    width = pieces[0][0].shape[1]
    ready = pl.pallas_call(
        first_kernel,
        out_shape=jax.ShapeDtypeStruct((rows, width), jnp.bfloat16),
        in_specs=[VMEM] * (2 + len(pieces[0])),
        out_specs=VMEM,
        compiler_params=params(12),
        cost_estimate=cost(6 * rows * width, 16 * rows * width),
    )(projected, norm, *pieces[0])
    return pl.pallas_call(
        last_kernel,
        out_shape=jax.ShapeDtypeStruct((rows, hidden), jnp.bfloat16),
        in_specs=[VMEM] * (3 + len(pieces[1])),
        out_specs=HBM,
        scratch_shapes=[
            pltpu.VMEM((rows, hidden - width), jnp.bfloat16),
            pltpu.SemaphoreType.DMA((2,)),
        ],
        compiler_params=params(12),
        cost_estimate=cost(6 * rows * width, 16 * rows * width),
    )(ready, projected, norm, *pieces[1])


def visit_kernel(own_tiles, per_owner, sources, targets, count, labels, tiles, blocks, out, total):
    spare, rows = total.shape[0] - 1, total.shape[1]
    total[...] = jnp.zeros_like(total)

    @pl.loop(0, count[0])
    def _(slot):
        target = targets[0, slot]
        label = labels[0, target]
        place = jnp.where(label < own_tiles, target // per_owner * own_tiles + label, spare)
        start = pl.multiple_of(sources[0, slot] * rows, rows)
        total[place] += jnp.dot(
            tiles[0, slot], blocks[pl.ds(start, rows), :], preferred_element_type=jnp.float32
        )

    @pl.loop(0, spare)
    def _(place):
        out[pl.ds(pl.multiple_of(place * rows, rows), rows), :] = total[place].astype(out.dtype)


def visit_tiles(own_tiles, owners, index_args, tile_weights, blocks):
    slots = index_args[-1].shape[1]
    rows = tile_weights.shape[-1]
    places = owners * own_tiles
    hidden = blocks.shape[1]
    return pl.pallas_call(
        functools.partial(visit_kernel, own_tiles, slots // owners),
        out_shape=jax.ShapeDtypeStruct((places * rows, hidden), jnp.bfloat16),
        in_specs=[SMEM] * 4 + [VMEM] * 2,
        out_specs=VMEM,
        scratch_shapes=[pltpu.VMEM((places + 1, rows, hidden), jnp.float32)],
        compiler_params=params(56),
    )(*index_args, tile_weights, blocks)


def swap(value, axis, apart):
    pairs = [(i, i ^ apart) for i in range(lax.axis_size(axis))]
    return lax.ppermute(value, axis, pairs)


def exchange(sent):
    owners = lax.axis_size("row")
    steps = [(2, 4), (4, 2), (6, 6)]
    return [
        lax.ppermute(value, "row", [(i, i ^ step[i % 2]) for i in range(owners)])
        for value, step in zip(sent, steps)
    ]


def per_device(
    features,
    weight,
    source_norm,
    target_norm,
    tile_weights,
    tile_source,
    tile_target,
    tile_count,
    mirror_tile,
):
    tile_rows = tile_weights.shape[-1]
    own_rows = features.shape[0]
    own_tiles = own_rows // tile_rows
    owners, columns = lax.axis_size("row"), lax.axis_size("col")
    span = own_tiles * columns
    index_args = (tile_source, tile_target, tile_count, mirror_tile)

    cells = owners * own_tiles * span * tile_rows * tile_rows
    if columns != 4 or owners != 8 or own_tiles & (own_tiles - 1) or cells > DENSE_ELEMENTS:
        projected = jnp.dot(features, weight, preferred_element_type=jnp.float32)
        scaled = (source_norm[:, None] * projected).astype(jnp.bfloat16)
        blocks = lax.all_gather(scaled, "col", axis=0, tiled=True)
        partial_value = visit_tiles(own_tiles, owners, index_args, tile_weights, blocks)
        outgoing = partial_value.reshape(owners, own_rows, -1)
        arrived = lax.all_to_all(outgoing, "row", split_axis=0, concat_axis=0, tiled=True)
        gathered = jnp.sum(arrived.astype(jnp.float32), axis=0) + projected
        return jnp.maximum(target_norm[:, None] * gathered, 0.0).astype(jnp.bfloat16)

    projected, *scaled = project(features, weight, source_norm, CHUNKS)
    built = merge_tiles(own_tiles, owners, span, index_args, tile_weights)
    half = built.shape[0] // 2
    across = [swap(own, "col", 3) for own in scaled]
    beside = [swap(own, "col", 1) for own in scaled]
    onward, matrix = lax.optimization_barrier((across[0], built))
    passed = swap(onward, "col", 1)
    early = early_product(matrix, scaled[0], beside[0], across[0])
    away = [
        late_product(matrix, early, passed, start, count, jnp.bfloat16, WEIGHTS[0])
        for start, count in ((0, own_rows), (own_rows, half - own_rows))
    ]
    stay = late_product(matrix, early, passed, half, half, jnp.float32, WEIGHTS[1])
    came = [swap(value, "row", 1) for value in away]
    (lead,) = join(stay, came[0], 0, own_rows, [jnp.bfloat16])
    kept, *sent = join(stay, came[1], own_rows, own_rows, [jnp.float32] + [jnp.bfloat16] * 2)
    pieces = [[kept] + exchange([lead] + sent)]

    onward, _ = lax.optimization_barrier((across[1], early))
    blocks = scaled[1], beside[1], swap(onward, "col", 1), across[1]
    blocks, _ = lax.optimization_barrier((blocks, sent))
    away = product(matrix, blocks, 0, half, jnp.bfloat16, WEIGHTS[2])
    stay = product(matrix, blocks, half, half, jnp.float32, WEIGHTS[3])
    came = swap(away, "row", 1)
    lead, kept, *sent = join(
        stay, came, 0, own_rows, [jnp.bfloat16, jnp.float32] + [jnp.bfloat16] * 2
    )
    pieces.append([kept] + exchange([lead] + sent))
    return finish(projected, target_norm, pieces)


def solution(mesh):
    in_specs = (
        P(("row", "col"), None),
        P(),
        P(("row", "col")),
        P(("row", "col")),
        P(("row", "col"), None, None, None),
        P(("row", "col"), None),
        P(("row", "col"), None),
        P(("row", "col")),
        P(("row", "col"), None),
    )
    out_specs = P(("row", "col"), None)
    return jax.shard_map(
        per_device, mesh=mesh, in_specs=in_specs, out_specs=out_specs, check_vma=False
    )
```

```python
import functools

import jax
import jax.numpy as jnp
from jax import lax
from jax.experimental import pallas as pl
from jax.experimental.pallas import tpu as pltpu
from jax.sharding import PartitionSpec as P

DENSE_ELEMENTS = 4 * 1024 * 1024
CHUNKS = 2
WEIGHTS = (20, 20, 0, 20)
MIB = 1024 * 1024
SMEM = pl.BlockSpec(memory_space=pltpu.SMEM)
VMEM = pl.BlockSpec(memory_space=pltpu.VMEM)
HBM = pl.BlockSpec(memory_space=pltpu.HBM)


def params(mib):
    return pltpu.CompilerParams(vmem_limit_bytes=int(mib * MIB))


def cost(flops, moved):
    return pl.CostEstimate(flops=flops, bytes_accessed=moved, transcendentals=0)


def in_hbm(*values):
    return [pltpu.with_memory_space_constraint(value, pltpu.HBM) for value in values]


def rows_to_lanes(row, lanes):
    return jnp.broadcast_to(row, (lanes, row.shape[1])).T


def project_kernel(features_hbm, weight_hbm, norm_hbm, projected, *refs):
    *scaled, features, weight, norm, sems = refs
    width, lanes = scaled[0].shape[1], norm.shape[1]
    half = weight.shape[0] // 2
    top, bottom = slice(0, half), slice(half, 2 * half)
    copies = [
        pltpu.make_async_copy(source, target, sems.at[k])
        for k, (source, target) in enumerate(
            [
                (weight_hbm.at[top], weight.at[top]),
                (features_hbm, features),
                (norm_hbm, norm),
                (weight_hbm.at[bottom], weight.at[bottom]),
            ]
        )
    ]
    for copy in copies:
        copy.start()
    for copy in copies[:3]:
        copy.wait()
    value = jnp.dot(features[:, top], weight[top, :], preferred_element_type=jnp.float32)
    copies[3].wait()
    value += jnp.dot(features[:, bottom], weight[bottom, :], preferred_element_type=jnp.float32)
    projected[...] = value
    for part in range(norm.shape[0]):
        factor = rows_to_lanes(norm[part : part + 1, :], lanes)
        for column in range(0, value.shape[1], lanes):
            piece = value[part * lanes : (part + 1) * lanes, column : column + lanes]
            target = scaled[column // width]
            start = column % width
            target[part * lanes : (part + 1) * lanes, start : start + lanes] = (
                factor * piece
            ).astype(target.dtype)


def project(features, weight, source_norm, chunks):
    rows, depth = features.shape
    hidden = weight.shape[1]
    norm = source_norm.reshape(-1, 128)
    return pl.pallas_call(
        project_kernel,
        out_shape=[jax.ShapeDtypeStruct((rows, hidden), jnp.float32)]
        + [jax.ShapeDtypeStruct((rows, hidden // chunks), jnp.bfloat16)] * chunks,
        in_specs=[HBM] * 3,
        out_specs=[VMEM] * (1 + chunks),
        scratch_shapes=[
            pltpu.VMEM(features.shape, features.dtype),
            pltpu.VMEM(weight.shape, weight.dtype),
            pltpu.VMEM(norm.shape, norm.dtype),
            pltpu.SemaphoreType.DMA((4,)),
        ],
        compiler_params=params(12),
        cost_estimate=cost(2 * rows * depth * hidden, 2 * depth * (rows + hidden)),
    )(*in_hbm(features, weight, norm))


def merge_kernel(
    own_tiles, per_owner, row, column, count, sources_hbm, targets_hbm, labels_hbm, tiles_hbm, out,
    total, tiles, sources, targets, labels, bases, seen, sems, tile_sems,
):
    small = [
        pltpu.make_async_copy(source, target, sems.at[k])
        for k, (source, target) in enumerate(
            [(sources_hbm, sources), (targets_hbm, targets), (labels_hbm, labels)]
        )
    ]
    parts = tile_sems.shape[0]
    each = tiles.shape[0] // parts
    large = [
        pltpu.make_async_copy(
            tiles_hbm.at[0, pl.ds(k * each, each)],
            tiles.at[pl.ds(k * each, each)],
            tile_sems.at[k],
        )
        for k in range(parts)
    ]
    for copy in small + large:
        copy.start()
    rows = total.shape[1]
    places, span = out.shape[0] // rows, out.shape[1] // rows
    spare = places * span
    for cell in range(spare + 1):
        seen[cell] = 0
    my_core, used = row[0] % 2, count[0]
    toggle = column[0] * own_tiles
    for copy in small:
        copy.wait()

    for slot in range(bases.shape[0]):
        owner, label = slot // per_owner, labels[0, slot]
        core, apart = owner % 2, lax.bitwise_xor(row[0], owner)
        x, y = lax.bitwise_and(apart, 2), lax.bitwise_and(lax.shift_right_logical(apart, 1), 2)
        first, second = (x, y) if core == 0 else (y, x)
        position = jnp.where(my_core == core, 4, 0) + second
        position += lax.shift_right_logical(jnp.where(second == 0, 2 - first, first), 1)
        base = (position * own_tiles + label) * span
        bases[slot] = jnp.where(label < own_tiles, base, spare)

    def add(slot):
        base = bases[targets[0, slot]]
        here = base + lax.bitwise_xor(sources[0, slot], toggle)
        cell = jnp.where((base < spare) & (slot < used), here, spare)
        before = jnp.where(seen[cell] > 0, total[cell], 0.0)
        seen[cell] = 1
        total[cell] = before + tiles[slot].astype(jnp.float32)

    for k, copy in enumerate(large):
        copy.wait()
        pl.loop(k * each, (k + 1) * each, unroll=4)(add)

    for place in range(places):
        for source in range(span):
            cell = place * span + source
            value = jnp.where(seen[cell] > 0, total[cell], 0.0)
            out[place * rows : (place + 1) * rows, source * rows : (source + 1) * rows] = (
                value.astype(out.dtype)
            )


def merge_tiles(own_tiles, owners, span, index_args, tile_weights):
    sources, targets, count, labels = index_args
    _, capacity, rows, _ = tile_weights.shape
    places = owners * own_tiles
    row = lax.axis_index("row").astype(jnp.int32).reshape(1)
    column = lax.axis_index("col").astype(jnp.int32).reshape(1)
    return pl.pallas_call(
        functools.partial(merge_kernel, own_tiles, labels.shape[1] // owners),
        out_shape=jax.ShapeDtypeStruct((places * rows, span * rows), jnp.bfloat16),
        in_specs=[SMEM] * 3 + [HBM] * 4,
        out_specs=VMEM,
        scratch_shapes=[
            pltpu.VMEM((places * span + 1, rows, rows), jnp.float32),
            pltpu.VMEM(tile_weights.shape[1:], tile_weights.dtype),
            pltpu.SMEM(sources.shape, jnp.int32),
            pltpu.SMEM(targets.shape, jnp.int32),
            pltpu.SMEM(labels.shape, jnp.int32),
            pltpu.SMEM((labels.shape[1],), jnp.int32),
            pltpu.SMEM((places * span + 1,), jnp.int32),
            pltpu.SemaphoreType.DMA((3,)),
            pltpu.SemaphoreType.DMA((4 if capacity % 4 == 0 else 1,)),
        ],
        compiler_params=params(24),
        cost_estimate=cost(8 * MIB, 12 * MIB),
    )(row, column, count, *in_hbm(sources, targets, labels, tile_weights))


def early_kernel(matrix, own, beside, across, out):
    rows = own.shape[0]
    value = jnp.dot(matrix[:, :rows], own[...], preferred_element_type=jnp.float32)
    value += jnp.dot(
        matrix[:, rows : 2 * rows], beside[...], preferred_element_type=jnp.float32
    )
    value += jnp.dot(matrix[:, 3 * rows :], across[...], preferred_element_type=jnp.float32)
    out[...] = value


def early_product(matrix, own, beside, across):
    total, depth = matrix.shape
    width = own.shape[1]
    return pl.pallas_call(
        early_kernel,
        out_shape=jax.ShapeDtypeStruct((total, width), jnp.float32),
        in_specs=[VMEM] * 4,
        out_specs=VMEM,
        compiler_params=params(16),
        cost_estimate=cost(total * depth * width, 1),
    )(matrix, own, beside, across)


def late_kernel(first, matrix, early, passed, out):
    rows = passed.shape[0]
    here = slice(first, first + out.shape[0])
    value = early[here, :] + jnp.dot(
        matrix[here, 2 * rows : 3 * rows], passed[...], preferred_element_type=jnp.float32
    )
    out[...] = value.astype(out.dtype)


def late_product(matrix, early, passed, first, count, dtype, weight):
    total, depth = matrix.shape
    width = passed.shape[1]
    return pl.pallas_call(
        functools.partial(late_kernel, first),
        out_shape=jax.ShapeDtypeStruct((count, width), dtype),
        in_specs=[VMEM] * 3,
        out_specs=VMEM,
        compiler_params=params(16),
        cost_estimate=cost(weight * total * depth * width, 1),
    )(matrix, early, passed)


def product_kernel(first, matrix, *refs):
    *blocks, out, gathered = refs
    rows = blocks[0].shape[0]
    for k, block in enumerate(blocks):
        gathered[k * rows : (k + 1) * rows, :] = block[...]
    value = jnp.dot(
        matrix[first : first + out.shape[0], :],
        gathered[...],
        preferred_element_type=jnp.float32,
    )
    out[...] = value.astype(out.dtype)


def product(matrix, blocks, first, count, dtype, weight):
    rows, width = blocks[0].shape
    total, depth = matrix.shape
    return pl.pallas_call(
        functools.partial(product_kernel, first),
        out_shape=jax.ShapeDtypeStruct((count, width), dtype),
        in_specs=[VMEM] * (1 + len(blocks)),
        out_specs=VMEM,
        scratch_shapes=[pltpu.VMEM((depth, width), blocks[0].dtype)],
        compiler_params=params(16),
        cost_estimate=cost(weight * total * depth * width, 1),
    )(matrix, *blocks)


def join_kernel(first, stay, came, *outs):
    start = 0
    for out in outs:
        rows = out.shape[0]
        value = stay[first + start : first + start + rows, :]
        out[...] = (value + came[start : start + rows, :].astype(jnp.float32)).astype(out.dtype)
        start += rows


def join(stay, came, first, rows, dtypes):
    width = stay.shape[1]
    return pl.pallas_call(
        functools.partial(join_kernel, first),
        out_shape=[jax.ShapeDtypeStruct((rows, width), dtype) for dtype in dtypes],
        in_specs=[VMEM] * 2,
        out_specs=[VMEM] * len(dtypes),
        compiler_params=params(12),
        cost_estimate=cost(1, 1),
    )(stay, came)


def activate(projected, norm, pieces, start, out):
    lanes = norm.shape[1]
    for part in range(norm.shape[0]):
        factor = rows_to_lanes(norm[part : part + 1, :], lanes)
        here = slice(part * lanes, (part + 1) * lanes)
        for column in range(0, out.shape[1], lanes):
            span = slice(column, column + lanes)
            value = projected[here, start + column : start + column + lanes]
            for piece in pieces:
                value += piece[here, span].astype(jnp.float32)
            out[here, span] = jnp.maximum(factor * value, 0.0).astype(out.dtype)


def first_kernel(projected, norm, *refs):
    *pieces, out = refs
    activate(projected, norm, pieces, 0, out)


def last_kernel(ready, projected, norm, *refs):
    *pieces, out, rest, sems = refs
    width = ready.shape[1]
    early = pltpu.make_async_copy(ready, out.at[:, :width], sems.at[0])
    early.start()
    activate(projected, norm, pieces, width, rest)
    late = pltpu.make_async_copy(rest, out.at[:, width:], sems.at[1])
    late.start()
    early.wait()
    late.wait()


def finish(projected, target_norm, pieces):
    rows, hidden = projected.shape
    norm = target_norm.reshape(-1, 128)
    width = pieces[0][0].shape[1]
    ready = pl.pallas_call(
        first_kernel,
        out_shape=jax.ShapeDtypeStruct((rows, width), jnp.bfloat16),
        in_specs=[VMEM] * (2 + len(pieces[0])),
        out_specs=VMEM,
        compiler_params=params(12),
        cost_estimate=cost(6 * rows * width, 16 * rows * width),
    )(projected, norm, *pieces[0])
    return pl.pallas_call(
        last_kernel,
        out_shape=jax.ShapeDtypeStruct((rows, hidden), jnp.bfloat16),
        in_specs=[VMEM] * (3 + len(pieces[1])),
        out_specs=HBM,
        scratch_shapes=[
            pltpu.VMEM((rows, hidden - width), jnp.bfloat16),
            pltpu.SemaphoreType.DMA((2,)),
        ],
        compiler_params=params(12),
        cost_estimate=cost(6 * rows * width, 16 * rows * width),
    )(ready, projected, norm, *pieces[1])


def visit_kernel(own_tiles, per_owner, sources, targets, count, labels, tiles, blocks, out, total):
    spare, rows = total.shape[0] - 1, total.shape[1]
    total[...] = jnp.zeros_like(total)

    @pl.loop(0, count[0])
    def _(slot):
        target = targets[0, slot]
        label = labels[0, target]
        place = jnp.where(label < own_tiles, target // per_owner * own_tiles + label, spare)
        start = pl.multiple_of(sources[0, slot] * rows, rows)
        total[place] += jnp.dot(
            tiles[0, slot], blocks[pl.ds(start, rows), :], preferred_element_type=jnp.float32
        )

    @pl.loop(0, spare)
    def _(place):
        out[pl.ds(pl.multiple_of(place * rows, rows), rows), :] = total[place].astype(out.dtype)


def visit_tiles(own_tiles, owners, index_args, tile_weights, blocks):
    slots = index_args[-1].shape[1]
    rows = tile_weights.shape[-1]
    places = owners * own_tiles
    hidden = blocks.shape[1]
    return pl.pallas_call(
        functools.partial(visit_kernel, own_tiles, slots // owners),
        out_shape=jax.ShapeDtypeStruct((places * rows, hidden), jnp.bfloat16),
        in_specs=[SMEM] * 4 + [VMEM] * 2,
        out_specs=VMEM,
        scratch_shapes=[pltpu.VMEM((places + 1, rows, hidden), jnp.float32)],
        compiler_params=params(56),
    )(*index_args, tile_weights, blocks)


def swap(value, axis, apart):
    pairs = [(i, i ^ apart) for i in range(lax.axis_size(axis))]
    return lax.ppermute(value, axis, pairs)


def exchange(sent):
    owners = lax.axis_size("row")
    steps = [(2, 4), (4, 2), (6, 6)]
    return [
        lax.ppermute(value, "row", [(i, i ^ step[i % 2]) for i in range(owners)])
        for value, step in zip(sent, steps)
    ]


def per_device(
    features,
    weight,
    source_norm,
    target_norm,
    tile_weights,
    tile_source,
    tile_target,
    tile_count,
    mirror_tile,
):
    tile_rows = tile_weights.shape[-1]
    own_rows = features.shape[0]
    own_tiles = own_rows // tile_rows
    owners, columns = lax.axis_size("row"), lax.axis_size("col")
    span = own_tiles * columns
    index_args = (tile_source, tile_target, tile_count, mirror_tile)

    cells = owners * own_tiles * span * tile_rows * tile_rows
    if columns != 4 or owners != 8 or own_tiles & (own_tiles - 1) or cells > DENSE_ELEMENTS:
        projected = jnp.dot(features, weight, preferred_element_type=jnp.float32)
        scaled = (source_norm[:, None] * projected).astype(jnp.bfloat16)
        blocks = lax.all_gather(scaled, "col", axis=0, tiled=True)
        partial_value = visit_tiles(own_tiles, owners, index_args, tile_weights, blocks)
        outgoing = partial_value.reshape(owners, own_rows, -1)
        arrived = lax.all_to_all(outgoing, "row", split_axis=0, concat_axis=0, tiled=True)
        gathered = jnp.sum(arrived.astype(jnp.float32), axis=0) + projected
        return jnp.maximum(target_norm[:, None] * gathered, 0.0).astype(jnp.bfloat16)

    projected, *scaled = project(features, weight, source_norm, CHUNKS)
    built = merge_tiles(own_tiles, owners, span, index_args, tile_weights)
    half = built.shape[0] // 2
    across = [swap(own, "col", 3) for own in scaled]
    beside = [swap(own, "col", 1) for own in scaled]
    onward, matrix = lax.optimization_barrier((across[0], built))
    passed = swap(onward, "col", 1)
    early = early_product(matrix, scaled[0], beside[0], across[0])
    away = [
        late_product(matrix, early, passed, start, count, jnp.bfloat16, WEIGHTS[0])
        for start, count in ((0, own_rows), (own_rows, half - own_rows))
    ]
    stay = late_product(matrix, early, passed, half, half, jnp.float32, WEIGHTS[1])
    came = [swap(value, "row", 1) for value in away]
    (lead,) = join(stay, came[0], 0, own_rows, [jnp.bfloat16])
    kept, *sent = join(stay, came[1], own_rows, own_rows, [jnp.float32] + [jnp.bfloat16] * 2)
    pieces = [[kept] + exchange([lead] + sent)]

    onward, _ = lax.optimization_barrier((across[1], early))
    blocks = scaled[1], beside[1], swap(onward, "col", 1), across[1]
    blocks, _ = lax.optimization_barrier((blocks, sent))
    away = [
        product(matrix, blocks, start, count, jnp.bfloat16, WEIGHTS[2])
        for start, count in ((0, own_rows), (own_rows, half - own_rows))
    ]
    stay = product(matrix, blocks, half, half, jnp.float32, WEIGHTS[3])
    came = [swap(value, "row", 1) for value in away]
    (lead,) = join(stay, came[0], 0, own_rows, [jnp.bfloat16])
    kept, *sent = join(stay, came[1], own_rows, own_rows, [jnp.float32] + [jnp.bfloat16] * 2)
    pieces.append([kept] + exchange([lead] + sent))
    return finish(projected, target_norm, pieces)


def solution(mesh):
    in_specs = (
        P(("row", "col"), None),
        P(),
        P(("row", "col")),
        P(("row", "col")),
        P(("row", "col"), None, None, None),
        P(("row", "col"), None),
        P(("row", "col"), None),
        P(("row", "col")),
        P(("row", "col"), None),
    )
    out_specs = P(("row", "col"), None)
    return jax.shard_map(
        per_device, mesh=mesh, in_specs=in_specs, out_specs=out_specs, check_vma=False
    )
```

```python
import functools

import jax
import jax.numpy as jnp
from jax import lax
from jax.experimental import pallas as pl
from jax.experimental.pallas import tpu as pltpu
from jax.sharding import PartitionSpec as P

DENSE_ELEMENTS = 4 * 1024 * 1024
CHUNKS = 2
WEIGHTS = (20, 20, 0, 20)
MIB = 1024 * 1024
SMEM = pl.BlockSpec(memory_space=pltpu.SMEM)
VMEM = pl.BlockSpec(memory_space=pltpu.VMEM)
HBM = pl.BlockSpec(memory_space=pltpu.HBM)


def params(mib):
    return pltpu.CompilerParams(vmem_limit_bytes=int(mib * MIB))


def cost(flops, moved):
    return pl.CostEstimate(flops=flops, bytes_accessed=moved, transcendentals=0)


def in_hbm(*values):
    return [pltpu.with_memory_space_constraint(value, pltpu.HBM) for value in values]


def rows_to_lanes(row, lanes):
    return jnp.broadcast_to(row, (lanes, row.shape[1])).T


def project_kernel(start, features_hbm, weight_hbm, norm_hbm, projected, scaled, *refs):
    features, weight, norm, sems = refs
    width, lanes = scaled.shape[1], norm.shape[1]
    copies = [
        pltpu.make_async_copy(source, target, sems.at[k])
        for k, (source, target) in enumerate(
            [
                (weight_hbm.at[:, start : start + width], weight),
                (features_hbm, features),
                (norm_hbm, norm),
            ]
        )
    ]
    for copy in copies:
        copy.start()
    for copy in copies:
        copy.wait()
    value = jnp.dot(features[...], weight[...], preferred_element_type=jnp.float32)
    projected[...] = value
    for part in range(norm.shape[0]):
        factor = rows_to_lanes(norm[part : part + 1, :], lanes)
        here = slice(part * lanes, (part + 1) * lanes)
        for column in range(0, width, lanes):
            piece = factor * value[here, column : column + lanes]
            scaled[here, column : column + lanes] = piece.astype(scaled.dtype)


def project(features, weight, source_norm, start, width):
    rows, depth = features.shape
    norm = source_norm.reshape(-1, 128)
    return pl.pallas_call(
        functools.partial(project_kernel, start),
        out_shape=[
            jax.ShapeDtypeStruct((rows, width), jnp.float32),
            jax.ShapeDtypeStruct((rows, width), jnp.bfloat16),
        ],
        in_specs=[HBM] * 3,
        out_specs=[VMEM] * 2,
        scratch_shapes=[
            pltpu.VMEM(features.shape, features.dtype),
            pltpu.VMEM((depth, width), weight.dtype),
            pltpu.VMEM(norm.shape, norm.dtype),
            pltpu.SemaphoreType.DMA((3,)),
        ],
        compiler_params=params(12),
        cost_estimate=cost(2 * rows * depth * width, 2 * depth * (rows + width)),
    )(*in_hbm(features, weight, norm))


def merge_kernel(
    own_tiles, per_owner, row, column, count, sources_hbm, targets_hbm, labels_hbm, tiles_hbm, out,
    total, tiles, sources, targets, labels, bases, seen, sems, tile_sems,
):
    small = [
        pltpu.make_async_copy(source, target, sems.at[k])
        for k, (source, target) in enumerate(
            [(sources_hbm, sources), (targets_hbm, targets), (labels_hbm, labels)]
        )
    ]
    parts = tile_sems.shape[0]
    each = tiles.shape[0] // parts
    large = [
        pltpu.make_async_copy(
            tiles_hbm.at[0, pl.ds(k * each, each)],
            tiles.at[pl.ds(k * each, each)],
            tile_sems.at[k],
        )
        for k in range(parts)
    ]
    for copy in small + large:
        copy.start()
    rows = total.shape[1]
    places, span = out.shape[0] // rows, out.shape[1] // rows
    spare = places * span
    for cell in range(spare + 1):
        seen[cell] = 0
    my_core, used = row[0] % 2, count[0]
    toggle = column[0] * own_tiles
    for copy in small:
        copy.wait()

    for slot in range(bases.shape[0]):
        owner, label = slot // per_owner, labels[0, slot]
        core, apart = owner % 2, lax.bitwise_xor(row[0], owner)
        x, y = lax.bitwise_and(apart, 2), lax.bitwise_and(lax.shift_right_logical(apart, 1), 2)
        first, second = (x, y) if core == 0 else (y, x)
        position = jnp.where(my_core == core, 4, 0) + second
        position += lax.shift_right_logical(jnp.where(second == 0, 2 - first, first), 1)
        base = (position * own_tiles + label) * span
        bases[slot] = jnp.where(label < own_tiles, base, spare)

    def add(slot):
        base = bases[targets[0, slot]]
        here = base + lax.bitwise_xor(sources[0, slot], toggle)
        cell = jnp.where((base < spare) & (slot < used), here, spare)
        before = jnp.where(seen[cell] > 0, total[cell], 0.0)
        seen[cell] = 1
        total[cell] = before + tiles[slot].astype(jnp.float32)

    for k, copy in enumerate(large):
        copy.wait()
        pl.loop(k * each, (k + 1) * each, unroll=4)(add)

    for place in range(places):
        for source in range(span):
            cell = place * span + source
            value = jnp.where(seen[cell] > 0, total[cell], 0.0)
            out[place * rows : (place + 1) * rows, source * rows : (source + 1) * rows] = (
                value.astype(out.dtype)
            )


def merge_tiles(own_tiles, owners, span, index_args, tile_weights):
    sources, targets, count, labels = index_args
    _, capacity, rows, _ = tile_weights.shape
    places = owners * own_tiles
    row = lax.axis_index("row").astype(jnp.int32).reshape(1)
    column = lax.axis_index("col").astype(jnp.int32).reshape(1)
    return pl.pallas_call(
        functools.partial(merge_kernel, own_tiles, labels.shape[1] // owners),
        out_shape=jax.ShapeDtypeStruct((places * rows, span * rows), jnp.bfloat16),
        in_specs=[SMEM] * 3 + [HBM] * 4,
        out_specs=VMEM,
        scratch_shapes=[
            pltpu.VMEM((places * span + 1, rows, rows), jnp.float32),
            pltpu.VMEM(tile_weights.shape[1:], tile_weights.dtype),
            pltpu.SMEM(sources.shape, jnp.int32),
            pltpu.SMEM(targets.shape, jnp.int32),
            pltpu.SMEM(labels.shape, jnp.int32),
            pltpu.SMEM((labels.shape[1],), jnp.int32),
            pltpu.SMEM((places * span + 1,), jnp.int32),
            pltpu.SemaphoreType.DMA((3,)),
            pltpu.SemaphoreType.DMA((4 if capacity % 4 == 0 else 1,)),
        ],
        compiler_params=params(24),
        cost_estimate=cost(8 * MIB, 12 * MIB),
    )(row, column, count, *in_hbm(sources, targets, labels, tile_weights))


def early_kernel(matrix, own, beside, across, out):
    rows = own.shape[0]
    value = jnp.dot(matrix[:, :rows], own[...], preferred_element_type=jnp.float32)
    value += jnp.dot(
        matrix[:, rows : 2 * rows], beside[...], preferred_element_type=jnp.float32
    )
    value += jnp.dot(matrix[:, 3 * rows :], across[...], preferred_element_type=jnp.float32)
    out[...] = value


def early_product(matrix, own, beside, across):
    total, depth = matrix.shape
    width = own.shape[1]
    return pl.pallas_call(
        early_kernel,
        out_shape=jax.ShapeDtypeStruct((total, width), jnp.float32),
        in_specs=[VMEM] * 4,
        out_specs=VMEM,
        compiler_params=params(16),
        cost_estimate=cost(total * depth * width, 1),
    )(matrix, own, beside, across)


def late_kernel(first, matrix, early, passed, out):
    rows = passed.shape[0]
    here = slice(first, first + out.shape[0])
    value = early[here, :] + jnp.dot(
        matrix[here, 2 * rows : 3 * rows], passed[...], preferred_element_type=jnp.float32
    )
    out[...] = value.astype(out.dtype)


def late_product(matrix, early, passed, first, count, dtype, weight):
    total, depth = matrix.shape
    width = passed.shape[1]
    return pl.pallas_call(
        functools.partial(late_kernel, first),
        out_shape=jax.ShapeDtypeStruct((count, width), dtype),
        in_specs=[VMEM] * 3,
        out_specs=VMEM,
        compiler_params=params(16),
        cost_estimate=cost(weight * total * depth * width, 1),
    )(matrix, early, passed)


def product_kernel(first, matrix, *refs):
    *blocks, out, gathered = refs
    rows = blocks[0].shape[0]
    for k, block in enumerate(blocks):
        gathered[k * rows : (k + 1) * rows, :] = block[...]
    value = jnp.dot(
        matrix[first : first + out.shape[0], :],
        gathered[...],
        preferred_element_type=jnp.float32,
    )
    out[...] = value.astype(out.dtype)


def product(matrix, blocks, first, count, dtype, weight):
    rows, width = blocks[0].shape
    total, depth = matrix.shape
    return pl.pallas_call(
        functools.partial(product_kernel, first),
        out_shape=jax.ShapeDtypeStruct((count, width), dtype),
        in_specs=[VMEM] * (1 + len(blocks)),
        out_specs=VMEM,
        scratch_shapes=[pltpu.VMEM((depth, width), blocks[0].dtype)],
        compiler_params=params(16),
        cost_estimate=cost(weight * total * depth * width, 1),
    )(matrix, *blocks)


def join_kernel(first, stay, came, *outs):
    start = 0
    for out in outs:
        rows = out.shape[0]
        value = stay[first + start : first + start + rows, :]
        out[...] = (value + came[start : start + rows, :].astype(jnp.float32)).astype(out.dtype)
        start += rows


def join(stay, came, first, rows, dtypes):
    width = stay.shape[1]
    return pl.pallas_call(
        functools.partial(join_kernel, first),
        out_shape=[jax.ShapeDtypeStruct((rows, width), dtype) for dtype in dtypes],
        in_specs=[VMEM] * 2,
        out_specs=[VMEM] * len(dtypes),
        compiler_params=params(12),
        cost_estimate=cost(1, 1),
    )(stay, came)


def activate(projected, norm, pieces, out):
    lanes = norm.shape[1]
    for part in range(norm.shape[0]):
        factor = rows_to_lanes(norm[part : part + 1, :], lanes)
        here = slice(part * lanes, (part + 1) * lanes)
        for column in range(0, out.shape[1], lanes):
            span = slice(column, column + lanes)
            value = projected[here, span]
            for piece in pieces:
                value += piece[here, span].astype(jnp.float32)
            out[here, span] = jnp.maximum(factor * value, 0.0).astype(out.dtype)


def first_kernel(projected, norm, *refs):
    *pieces, out = refs
    activate(projected, norm, pieces, out)


def last_kernel(ready, projected, norm, *refs):
    *pieces, out, rest, sems = refs
    width = ready.shape[1]
    early = pltpu.make_async_copy(ready, out.at[:, :width], sems.at[0])
    early.start()
    activate(projected, norm, pieces, rest)
    late = pltpu.make_async_copy(rest, out.at[:, width:], sems.at[1])
    late.start()
    early.wait()
    late.wait()


def finish(projected, target_norm, pieces):
    norm = target_norm.reshape(-1, 128)
    rows, width = projected[0].shape
    rest = projected[1].shape[1]
    ready = pl.pallas_call(
        first_kernel,
        out_shape=jax.ShapeDtypeStruct((rows, width), jnp.bfloat16),
        in_specs=[VMEM] * (2 + len(pieces[0])),
        out_specs=VMEM,
        compiler_params=params(12),
        cost_estimate=cost(6 * rows * width, 16 * rows * width),
    )(projected[0], norm, *pieces[0])
    return pl.pallas_call(
        last_kernel,
        out_shape=jax.ShapeDtypeStruct((rows, width + rest), jnp.bfloat16),
        in_specs=[VMEM] * (3 + len(pieces[1])),
        out_specs=HBM,
        scratch_shapes=[
            pltpu.VMEM((rows, rest), jnp.bfloat16),
            pltpu.SemaphoreType.DMA((2,)),
        ],
        compiler_params=params(12),
        cost_estimate=cost(6 * rows * rest, 16 * rows * rest),
    )(ready, projected[1], norm, *pieces[1])


def visit_kernel(own_tiles, per_owner, sources, targets, count, labels, tiles, blocks, out, total):
    spare, rows = total.shape[0] - 1, total.shape[1]
    total[...] = jnp.zeros_like(total)

    @pl.loop(0, count[0])
    def _(slot):
        target = targets[0, slot]
        label = labels[0, target]
        place = jnp.where(label < own_tiles, target // per_owner * own_tiles + label, spare)
        start = pl.multiple_of(sources[0, slot] * rows, rows)
        total[place] += jnp.dot(
            tiles[0, slot], blocks[pl.ds(start, rows), :], preferred_element_type=jnp.float32
        )

    @pl.loop(0, spare)
    def _(place):
        out[pl.ds(pl.multiple_of(place * rows, rows), rows), :] = total[place].astype(out.dtype)


def visit_tiles(own_tiles, owners, index_args, tile_weights, blocks):
    slots = index_args[-1].shape[1]
    rows = tile_weights.shape[-1]
    places = owners * own_tiles
    hidden = blocks.shape[1]
    return pl.pallas_call(
        functools.partial(visit_kernel, own_tiles, slots // owners),
        out_shape=jax.ShapeDtypeStruct((places * rows, hidden), jnp.bfloat16),
        in_specs=[SMEM] * 4 + [VMEM] * 2,
        out_specs=VMEM,
        scratch_shapes=[pltpu.VMEM((places + 1, rows, hidden), jnp.float32)],
        compiler_params=params(56),
    )(*index_args, tile_weights, blocks)


def swap(value, axis, apart):
    pairs = [(i, i ^ apart) for i in range(lax.axis_size(axis))]
    return lax.ppermute(value, axis, pairs)


def exchange(sent):
    owners = lax.axis_size("row")
    steps = [(2, 4), (4, 2), (6, 6)]
    return [
        lax.ppermute(value, "row", [(i, i ^ step[i % 2]) for i in range(owners)])
        for value, step in zip(sent, steps)
    ]


def per_device(
    features,
    weight,
    source_norm,
    target_norm,
    tile_weights,
    tile_source,
    tile_target,
    tile_count,
    mirror_tile,
):
    tile_rows = tile_weights.shape[-1]
    own_rows = features.shape[0]
    own_tiles = own_rows // tile_rows
    owners, columns = lax.axis_size("row"), lax.axis_size("col")
    span = own_tiles * columns
    index_args = (tile_source, tile_target, tile_count, mirror_tile)

    cells = owners * own_tiles * span * tile_rows * tile_rows
    if columns != 4 or owners != 8 or own_tiles & (own_tiles - 1) or cells > DENSE_ELEMENTS:
        projected = jnp.dot(features, weight, preferred_element_type=jnp.float32)
        scaled = (source_norm[:, None] * projected).astype(jnp.bfloat16)
        blocks = lax.all_gather(scaled, "col", axis=0, tiled=True)
        partial_value = visit_tiles(own_tiles, owners, index_args, tile_weights, blocks)
        outgoing = partial_value.reshape(owners, own_rows, -1)
        arrived = lax.all_to_all(outgoing, "row", split_axis=0, concat_axis=0, tiled=True)
        gathered = jnp.sum(arrived.astype(jnp.float32), axis=0) + projected
        return jnp.maximum(target_norm[:, None] * gathered, 0.0).astype(jnp.bfloat16)

    width = weight.shape[1] // CHUNKS
    projected, scaled = zip(
        *(project(features, weight, source_norm, k * width, width) for k in range(CHUNKS))
    )
    built = merge_tiles(own_tiles, owners, span, index_args, tile_weights)
    half = built.shape[0] // 2
    across = [swap(own, "col", 3) for own in scaled]
    beside = [swap(own, "col", 1) for own in scaled]
    onward, matrix = lax.optimization_barrier((across[0], built))
    passed = swap(onward, "col", 1)
    early = early_product(matrix, scaled[0], beside[0], across[0])
    away = [
        late_product(matrix, early, passed, start, count, jnp.bfloat16, WEIGHTS[0])
        for start, count in ((0, own_rows), (own_rows, half - own_rows))
    ]
    stay = late_product(matrix, early, passed, half, half, jnp.float32, WEIGHTS[1])
    came = [swap(value, "row", 1) for value in away]
    (lead,) = join(stay, came[0], 0, own_rows, [jnp.bfloat16])
    kept, *sent = join(stay, came[1], own_rows, own_rows, [jnp.float32] + [jnp.bfloat16] * 2)
    pieces = [[kept] + exchange([lead] + sent)]

    onward, _ = lax.optimization_barrier((across[1], early))
    blocks = scaled[1], beside[1], swap(onward, "col", 1), across[1]
    blocks, _ = lax.optimization_barrier((blocks, sent))
    away = product(matrix, blocks, 0, half, jnp.bfloat16, WEIGHTS[2])
    stay = product(matrix, blocks, half, half, jnp.float32, WEIGHTS[3])
    came = swap(away, "row", 1)
    lead, kept, *sent = join(
        stay, came, 0, own_rows, [jnp.bfloat16, jnp.float32] + [jnp.bfloat16] * 2
    )
    pieces.append([kept] + exchange([lead] + sent))
    return finish(projected, target_norm, pieces)


def solution(mesh):
    in_specs = (
        P(("row", "col"), None),
        P(),
        P(("row", "col")),
        P(("row", "col")),
        P(("row", "col"), None, None, None),
        P(("row", "col"), None),
        P(("row", "col"), None),
        P(("row", "col")),
        P(("row", "col"), None),
    )
    out_specs = P(("row", "col"), None)
    return jax.shard_map(
        per_device, mesh=mesh, in_specs=in_specs, out_specs=out_specs, check_vma=False
    )
```

```python
import functools

import jax
import jax.numpy as jnp
from jax import lax
from jax.experimental import pallas as pl
from jax.experimental.pallas import tpu as pltpu
from jax.sharding import PartitionSpec as P

DENSE_ELEMENTS = 4 * 1024 * 1024
CHUNKS = 2
WEIGHTS = (20, 20, 0, 20)
MIB = 1024 * 1024
SMEM = pl.BlockSpec(memory_space=pltpu.SMEM)
VMEM = pl.BlockSpec(memory_space=pltpu.VMEM)
HBM = pl.BlockSpec(memory_space=pltpu.HBM)


def params(mib):
    return pltpu.CompilerParams(vmem_limit_bytes=int(mib * MIB))


def cost(flops, moved):
    return pl.CostEstimate(flops=flops, bytes_accessed=moved, transcendentals=0)


def in_hbm(*values):
    return [pltpu.with_memory_space_constraint(value, pltpu.HBM) for value in values]


def rows_to_lanes(row, lanes):
    return jnp.broadcast_to(row, (lanes, row.shape[1])).T


def project_kernel(start, features_hbm, weight_hbm, norm_hbm, projected, scaled, *refs):
    features, weight, norm, sems = refs
    width, lanes = scaled.shape[1], norm.shape[1]
    copies = [
        pltpu.make_async_copy(source, target, sems.at[k])
        for k, (source, target) in enumerate(
            [
                (weight_hbm.at[:, start : start + width], weight),
                (features_hbm, features),
                (norm_hbm, norm),
            ]
        )
    ]
    for copy in copies:
        copy.start()
    for copy in copies:
        copy.wait()
    value = jnp.dot(features[...], weight[...], preferred_element_type=jnp.float32)
    projected[...] = value
    for part in range(norm.shape[0]):
        factor = rows_to_lanes(norm[part : part + 1, :], lanes)
        here = slice(part * lanes, (part + 1) * lanes)
        for column in range(0, width, lanes):
            piece = factor * value[here, column : column + lanes]
            scaled[here, column : column + lanes] = piece.astype(scaled.dtype)


def project(features, weight, source_norm, start, width):
    rows, depth = features.shape
    norm = source_norm.reshape(-1, 128)
    return pl.pallas_call(
        functools.partial(project_kernel, start),
        out_shape=[
            jax.ShapeDtypeStruct((rows, width), jnp.float32),
            jax.ShapeDtypeStruct((rows, width), jnp.bfloat16),
        ],
        in_specs=[HBM] * 3,
        out_specs=[VMEM] * 2,
        scratch_shapes=[
            pltpu.VMEM(features.shape, features.dtype),
            pltpu.VMEM((depth, width), weight.dtype),
            pltpu.VMEM(norm.shape, norm.dtype),
            pltpu.SemaphoreType.DMA((3,)),
        ],
        compiler_params=params(12),
        cost_estimate=cost(2 * rows * depth * width, 2 * depth * (rows + width)),
    )(*in_hbm(features, weight, norm))


def merge_kernel(
    own_tiles, per_owner, row, column, count, sources_hbm, targets_hbm, labels_hbm, tiles_hbm, out,
    total, tiles, sources, targets, labels, bases, seen, sems, tile_sems,
):
    small = [
        pltpu.make_async_copy(source, target, sems.at[k])
        for k, (source, target) in enumerate(
            [(sources_hbm, sources), (targets_hbm, targets), (labels_hbm, labels)]
        )
    ]
    parts = tile_sems.shape[0]
    each = tiles.shape[0] // parts
    large = [
        pltpu.make_async_copy(
            tiles_hbm.at[0, pl.ds(k * each, each)],
            tiles.at[pl.ds(k * each, each)],
            tile_sems.at[k],
        )
        for k in range(parts)
    ]
    for copy in small + large:
        copy.start()
    rows = total.shape[1]
    places, span = out.shape[0] // rows, out.shape[1] // rows
    spare = places * span
    for cell in range(spare + 1):
        seen[cell] = 0
    my_core, used = row[0] % 2, count[0]
    toggle = column[0] * own_tiles
    for copy in small:
        copy.wait()

    for slot in range(bases.shape[0]):
        owner, label = slot // per_owner, labels[0, slot]
        core, apart = owner % 2, lax.bitwise_xor(row[0], owner)
        x, y = lax.bitwise_and(apart, 2), lax.bitwise_and(lax.shift_right_logical(apart, 1), 2)
        first, second = (x, y) if core == 0 else (y, x)
        position = jnp.where(my_core == core, 4, 0) + second
        position += lax.shift_right_logical(jnp.where(second == 0, 2 - first, first), 1)
        base = (position * own_tiles + label) * span
        bases[slot] = jnp.where(label < own_tiles, base, spare)

    def add(slot):
        base = bases[targets[0, slot]]
        here = base + lax.bitwise_xor(sources[0, slot], toggle)
        cell = jnp.where((base < spare) & (slot < used), here, spare)
        before = jnp.where(seen[cell] > 0, total[cell], 0.0)
        seen[cell] = 1
        total[cell] = before + tiles[slot].astype(jnp.float32)

    for k, copy in enumerate(large):
        copy.wait()
        pl.loop(k * each, (k + 1) * each, unroll=4)(add)

    for place in range(places):
        for source in range(span):
            cell = place * span + source
            value = jnp.where(seen[cell] > 0, total[cell], 0.0)
            out[place * rows : (place + 1) * rows, source * rows : (source + 1) * rows] = (
                value.astype(out.dtype)
            )


def merge_tiles(own_tiles, owners, span, index_args, tile_weights):
    sources, targets, count, labels = index_args
    _, capacity, rows, _ = tile_weights.shape
    places = owners * own_tiles
    row = lax.axis_index("row").astype(jnp.int32).reshape(1)
    column = lax.axis_index("col").astype(jnp.int32).reshape(1)
    return pl.pallas_call(
        functools.partial(merge_kernel, own_tiles, labels.shape[1] // owners),
        out_shape=jax.ShapeDtypeStruct((places * rows, span * rows), jnp.bfloat16),
        in_specs=[SMEM] * 3 + [HBM] * 4,
        out_specs=VMEM,
        scratch_shapes=[
            pltpu.VMEM((places * span + 1, rows, rows), jnp.float32),
            pltpu.VMEM(tile_weights.shape[1:], tile_weights.dtype),
            pltpu.SMEM(sources.shape, jnp.int32),
            pltpu.SMEM(targets.shape, jnp.int32),
            pltpu.SMEM(labels.shape, jnp.int32),
            pltpu.SMEM((labels.shape[1],), jnp.int32),
            pltpu.SMEM((places * span + 1,), jnp.int32),
            pltpu.SemaphoreType.DMA((3,)),
            pltpu.SemaphoreType.DMA((4 if capacity % 4 == 0 else 1,)),
        ],
        compiler_params=params(24),
        cost_estimate=cost(8 * MIB, 12 * MIB),
    )(row, column, count, *in_hbm(sources, targets, labels, tile_weights))


def early_kernel(matrix, own, beside, across, out):
    rows = own.shape[0]
    value = jnp.dot(matrix[:, :rows], own[...], preferred_element_type=jnp.float32)
    value += jnp.dot(
        matrix[:, rows : 2 * rows], beside[...], preferred_element_type=jnp.float32
    )
    value += jnp.dot(matrix[:, 3 * rows :], across[...], preferred_element_type=jnp.float32)
    out[...] = value


def early_product(matrix, own, beside, across):
    total, depth = matrix.shape
    width = own.shape[1]
    return pl.pallas_call(
        early_kernel,
        out_shape=jax.ShapeDtypeStruct((total, width), jnp.float32),
        in_specs=[VMEM] * 4,
        out_specs=VMEM,
        compiler_params=params(16),
        cost_estimate=cost(total * depth * width, 1),
    )(matrix, own, beside, across)


def late_kernel(first, matrix, early, passed, out):
    rows = passed.shape[0]
    here = slice(first, first + out.shape[0])
    value = early[here, :] + jnp.dot(
        matrix[here, 2 * rows : 3 * rows], passed[...], preferred_element_type=jnp.float32
    )
    out[...] = value.astype(out.dtype)


def late_product(matrix, early, passed, first, count, dtype, weight):
    total, depth = matrix.shape
    width = passed.shape[1]
    return pl.pallas_call(
        functools.partial(late_kernel, first),
        out_shape=jax.ShapeDtypeStruct((count, width), dtype),
        in_specs=[VMEM] * 3,
        out_specs=VMEM,
        compiler_params=params(16),
        cost_estimate=cost(weight * total * depth * width, 1),
    )(matrix, early, passed)


def product_kernel(first, matrix, *refs):
    *blocks, out, gathered = refs
    rows = blocks[0].shape[0]
    for k, block in enumerate(blocks):
        gathered[k * rows : (k + 1) * rows, :] = block[...]
    value = jnp.dot(
        matrix[first : first + out.shape[0], :],
        gathered[...],
        preferred_element_type=jnp.float32,
    )
    out[...] = value.astype(out.dtype)


def product(matrix, blocks, first, count, dtype, weight):
    rows, width = blocks[0].shape
    total, depth = matrix.shape
    return pl.pallas_call(
        functools.partial(product_kernel, first),
        out_shape=jax.ShapeDtypeStruct((count, width), dtype),
        in_specs=[VMEM] * (1 + len(blocks)),
        out_specs=VMEM,
        scratch_shapes=[pltpu.VMEM((depth, width), blocks[0].dtype)],
        compiler_params=params(16),
        cost_estimate=cost(weight * total * depth * width, 1),
    )(matrix, *blocks)


def join_kernel(first, stay, came, *outs):
    start = 0
    for out in outs:
        rows = out.shape[0]
        value = stay[first + start : first + start + rows, :]
        out[...] = (value + came[start : start + rows, :].astype(jnp.float32)).astype(out.dtype)
        start += rows


def join(stay, came, first, rows, dtypes):
    width = stay.shape[1]
    return pl.pallas_call(
        functools.partial(join_kernel, first),
        out_shape=[jax.ShapeDtypeStruct((rows, width), dtype) for dtype in dtypes],
        in_specs=[VMEM] * 2,
        out_specs=[VMEM] * len(dtypes),
        compiler_params=params(12),
        cost_estimate=cost(1, 1),
    )(stay, came)


def activate(projected, norm, pieces, out):
    lanes = norm.shape[1]
    for part in range(norm.shape[0]):
        factor = rows_to_lanes(norm[part : part + 1, :], lanes)
        here = slice(part * lanes, (part + 1) * lanes)
        for column in range(0, out.shape[1], lanes):
            span = slice(column, column + lanes)
            value = projected[here, span]
            for piece in pieces:
                value += piece[here, span].astype(jnp.float32)
            out[here, span] = jnp.maximum(factor * value, 0.0).astype(out.dtype)


def first_kernel(projected, norm, *refs):
    *pieces, out = refs
    activate(projected, norm, pieces, out)


def last_kernel(ready, projected, norm, *refs):
    *pieces, out, rest, sems = refs
    width = ready.shape[1]
    early = pltpu.make_async_copy(ready, out.at[:, :width], sems.at[0])
    early.start()
    activate(projected, norm, pieces, rest)
    late = pltpu.make_async_copy(rest, out.at[:, width:], sems.at[1])
    late.start()
    early.wait()
    late.wait()


def finish(projected, target_norm, pieces):
    norm = target_norm.reshape(-1, 128)
    rows, width = projected[0].shape
    rest = projected[1].shape[1]
    ready = pl.pallas_call(
        first_kernel,
        out_shape=jax.ShapeDtypeStruct((rows, width), jnp.bfloat16),
        in_specs=[VMEM] * (2 + len(pieces[0])),
        out_specs=VMEM,
        compiler_params=params(12),
        cost_estimate=cost(6 * rows * width, 16 * rows * width),
    )(projected[0], norm, *pieces[0])
    return pl.pallas_call(
        last_kernel,
        out_shape=jax.ShapeDtypeStruct((rows, width + rest), jnp.bfloat16),
        in_specs=[VMEM] * (3 + len(pieces[1])),
        out_specs=HBM,
        scratch_shapes=[
            pltpu.VMEM((rows, rest), jnp.bfloat16),
            pltpu.SemaphoreType.DMA((2,)),
        ],
        compiler_params=params(12),
        cost_estimate=cost(6 * rows * rest, 16 * rows * rest),
    )(ready, projected[1], norm, *pieces[1])


def visit_kernel(own_tiles, per_owner, sources, targets, count, labels, tiles, blocks, out, total):
    spare, rows = total.shape[0] - 1, total.shape[1]
    total[...] = jnp.zeros_like(total)

    @pl.loop(0, count[0])
    def _(slot):
        target = targets[0, slot]
        label = labels[0, target]
        place = jnp.where(label < own_tiles, target // per_owner * own_tiles + label, spare)
        start = pl.multiple_of(sources[0, slot] * rows, rows)
        total[place] += jnp.dot(
            tiles[0, slot], blocks[pl.ds(start, rows), :], preferred_element_type=jnp.float32
        )

    @pl.loop(0, spare)
    def _(place):
        out[pl.ds(pl.multiple_of(place * rows, rows), rows), :] = total[place].astype(out.dtype)


def visit_tiles(own_tiles, owners, index_args, tile_weights, blocks):
    slots = index_args[-1].shape[1]
    rows = tile_weights.shape[-1]
    places = owners * own_tiles
    hidden = blocks.shape[1]
    return pl.pallas_call(
        functools.partial(visit_kernel, own_tiles, slots // owners),
        out_shape=jax.ShapeDtypeStruct((places * rows, hidden), jnp.bfloat16),
        in_specs=[SMEM] * 4 + [VMEM] * 2,
        out_specs=VMEM,
        scratch_shapes=[pltpu.VMEM((places + 1, rows, hidden), jnp.float32)],
        compiler_params=params(56),
    )(*index_args, tile_weights, blocks)


def swap(value, axis, apart):
    pairs = [(i, i ^ apart) for i in range(lax.axis_size(axis))]
    return lax.ppermute(value, axis, pairs)


def exchange(sent):
    owners = lax.axis_size("row")
    steps = [(2, 4), (4, 2), (6, 6)]
    return [
        lax.ppermute(value, "row", [(i, i ^ step[i % 2]) for i in range(owners)])
        for value, step in zip(sent, steps)
    ]


def per_device(
    features,
    weight,
    source_norm,
    target_norm,
    tile_weights,
    tile_source,
    tile_target,
    tile_count,
    mirror_tile,
):
    tile_rows = tile_weights.shape[-1]
    own_rows = features.shape[0]
    own_tiles = own_rows // tile_rows
    owners, columns = lax.axis_size("row"), lax.axis_size("col")
    span = own_tiles * columns
    index_args = (tile_source, tile_target, tile_count, mirror_tile)

    cells = owners * own_tiles * span * tile_rows * tile_rows
    if columns != 4 or owners != 8 or own_tiles & (own_tiles - 1) or cells > DENSE_ELEMENTS:
        projected = jnp.dot(features, weight, preferred_element_type=jnp.float32)
        scaled = (source_norm[:, None] * projected).astype(jnp.bfloat16)
        blocks = lax.all_gather(scaled, "col", axis=0, tiled=True)
        partial_value = visit_tiles(own_tiles, owners, index_args, tile_weights, blocks)
        outgoing = partial_value.reshape(owners, own_rows, -1)
        arrived = lax.all_to_all(outgoing, "row", split_axis=0, concat_axis=0, tiled=True)
        gathered = jnp.sum(arrived.astype(jnp.float32), axis=0) + projected
        return jnp.maximum(target_norm[:, None] * gathered, 0.0).astype(jnp.bfloat16)

    width = weight.shape[1] // CHUNKS
    projected, scaled = zip(
        *(project(features, weight, source_norm, k * width, width) for k in range(CHUNKS))
    )
    built = merge_tiles(own_tiles, owners, span, index_args, tile_weights)
    half = built.shape[0] // 2
    across = [swap(own, "col", 3) for own in scaled]
    beside = [swap(own, "col", 1) for own in scaled]
    onward, matrix = lax.optimization_barrier((across[0], built))
    passed = swap(onward, "col", 1)
    early = early_product(matrix, scaled[0], beside[0], across[0])
    away = [late_product(matrix, early, passed, 0, own_rows, jnp.bfloat16, WEIGHTS[0])]
    after, _ = lax.optimization_barrier((passed, away[0]))
    away.append(
        late_product(
            matrix, early, after, own_rows, half - own_rows, jnp.bfloat16, WEIGHTS[0]
        )
    )
    stay = late_product(matrix, early, passed, half, half, jnp.float32, WEIGHTS[1])
    came = [swap(value, "row", 1) for value in away]
    (lead,) = join(stay, came[0], 0, own_rows, [jnp.bfloat16])
    kept, *sent = join(stay, came[1], own_rows, own_rows, [jnp.float32] + [jnp.bfloat16] * 2)
    pieces = [[kept] + exchange([lead] + sent)]

    onward, _ = lax.optimization_barrier((across[1], early))
    blocks = scaled[1], beside[1], swap(onward, "col", 1), across[1]
    blocks, _ = lax.optimization_barrier((blocks, sent))
    away = product(matrix, blocks, 0, half, jnp.bfloat16, WEIGHTS[2])
    stay = product(matrix, blocks, half, half, jnp.float32, WEIGHTS[3])
    came = swap(away, "row", 1)
    lead, kept, *sent = join(
        stay, came, 0, own_rows, [jnp.bfloat16, jnp.float32] + [jnp.bfloat16] * 2
    )
    pieces.append([kept] + exchange([lead] + sent))
    return finish(projected, target_norm, pieces)


def solution(mesh):
    in_specs = (
        P(("row", "col"), None),
        P(),
        P(("row", "col")),
        P(("row", "col")),
        P(("row", "col"), None, None, None),
        P(("row", "col"), None),
        P(("row", "col"), None),
        P(("row", "col")),
        P(("row", "col"), None),
    )
    out_specs = P(("row", "col"), None)
    return jax.shard_map(
        per_device, mesh=mesh, in_specs=in_specs, out_specs=out_specs, check_vma=False
    )
```

```python
import functools

import jax
import jax.numpy as jnp
from jax import lax
from jax.experimental import pallas as pl
from jax.experimental.pallas import tpu as pltpu
from jax.sharding import PartitionSpec as P

DENSE_ELEMENTS = 4 * 1024 * 1024
CHUNKS = 2
WEIGHTS = (20, 20, 0, 20)
MIB = 1024 * 1024
SMEM = pl.BlockSpec(memory_space=pltpu.SMEM)
VMEM = pl.BlockSpec(memory_space=pltpu.VMEM)
HBM = pl.BlockSpec(memory_space=pltpu.HBM)


def params(mib):
    return pltpu.CompilerParams(vmem_limit_bytes=int(mib * MIB))


def cost(flops, moved):
    return pl.CostEstimate(flops=flops, bytes_accessed=moved, transcendentals=0)


def in_hbm(*values):
    return [pltpu.with_memory_space_constraint(value, pltpu.HBM) for value in values]


def rows_to_lanes(row, lanes):
    return jnp.broadcast_to(row, (lanes, row.shape[1])).T


def project_kernel(start, extra, features_hbm, weight_hbm, norm_hbm, *refs):
    extra_hbm, (projected, scaled), refs = refs[:extra], refs[extra : extra + 2], refs[extra + 2 :]
    staged, (features, weight, norm, sems) = refs[:extra], refs[extra:]
    width, lanes = scaled.shape[1], norm.shape[1]
    copies = [
        pltpu.make_async_copy(source, target, sems.at[k])
        for k, (source, target) in enumerate(
            [
                (weight_hbm.at[:, start : start + width], weight),
                (features_hbm, features),
                (norm_hbm, norm),
                *zip(extra_hbm, staged),
            ]
        )
    ]
    for copy in copies:
        copy.start()
    for copy in copies:
        copy.wait()
    value = jnp.dot(features[...], weight[...], preferred_element_type=jnp.float32)
    projected[...] = value
    for part in range(norm.shape[0]):
        factor = rows_to_lanes(norm[part : part + 1, :], lanes)
        here = slice(part * lanes, (part + 1) * lanes)
        for column in range(0, width, lanes):
            piece = factor * value[here, column : column + lanes]
            scaled[here, column : column + lanes] = piece.astype(scaled.dtype)


def project(features, weight, source_norm, start, width, *extra):
    rows, depth = features.shape
    norm = source_norm.reshape(-1, 128)
    return pl.pallas_call(
        functools.partial(project_kernel, start, len(extra)),
        out_shape=[
            jax.ShapeDtypeStruct((rows, width), jnp.float32),
            jax.ShapeDtypeStruct((rows, width), jnp.bfloat16),
        ]
        + [jax.ShapeDtypeStruct(value.shape, value.dtype) for value in extra],
        in_specs=[HBM] * (3 + len(extra)),
        out_specs=[VMEM] * (2 + len(extra)),
        scratch_shapes=[
            pltpu.VMEM(features.shape, features.dtype),
            pltpu.VMEM((depth, width), weight.dtype),
            pltpu.VMEM(norm.shape, norm.dtype),
            pltpu.SemaphoreType.DMA((3 + len(extra),)),
        ],
        compiler_params=params(12),
        cost_estimate=cost(2 * rows * depth * width, 2 * depth * (rows + width)),
    )(*in_hbm(features, weight, norm, *extra))


def merge_kernel(
    own_tiles, per_owner, row, column, count, sources_in, targets_in, labels_in, tiles_hbm, out,
    total, tiles, sources, targets, labels, bases, seen, sems, tile_sems,
):
    small = [
        pltpu.make_async_copy(source, target, sems.at[k])
        for k, (source, target) in enumerate(
            [(sources_in, sources), (targets_in, targets), (labels_in, labels)]
        )
    ]
    parts = tile_sems.shape[0]
    each = tiles.shape[0] // parts
    large = [
        pltpu.make_async_copy(
            tiles_hbm.at[0, pl.ds(k * each, each)],
            tiles.at[pl.ds(k * each, each)],
            tile_sems.at[k],
        )
        for k in range(parts)
    ]
    for copy in small + large:
        copy.start()
    rows = total.shape[1]
    places, span = out.shape[0] // rows, out.shape[1] // rows
    spare = places * span
    for cell in range(spare + 1):
        seen[cell] = 0
    my_core, used = row[0] % 2, count[0]
    toggle = column[0] * own_tiles
    for copy in small:
        copy.wait()

    for slot in range(bases.shape[0]):
        owner, label = slot // per_owner, labels[0, slot]
        core, apart = owner % 2, lax.bitwise_xor(row[0], owner)
        x, y = lax.bitwise_and(apart, 2), lax.bitwise_and(lax.shift_right_logical(apart, 1), 2)
        first, second = (x, y) if core == 0 else (y, x)
        position = jnp.where(my_core == core, 4, 0) + second
        position += lax.shift_right_logical(jnp.where(second == 0, 2 - first, first), 1)
        base = (position * own_tiles + label) * span
        bases[slot] = jnp.where(label < own_tiles, base, spare)

    def add(slot):
        base = bases[targets[0, slot]]
        here = base + lax.bitwise_xor(sources[0, slot], toggle)
        cell = jnp.where((base < spare) & (slot < used), here, spare)
        before = jnp.where(seen[cell] > 0, total[cell], 0.0)
        seen[cell] = 1
        total[cell] = before + tiles[slot].astype(jnp.float32)

    for k, copy in enumerate(large):
        copy.wait()
        pl.loop(k * each, (k + 1) * each, unroll=4)(add)

    for place in range(places):
        for source in range(span):
            cell = place * span + source
            value = jnp.where(seen[cell] > 0, total[cell], 0.0)
            out[place * rows : (place + 1) * rows, source * rows : (source + 1) * rows] = (
                value.astype(out.dtype)
            )


def merge_tiles(own_tiles, owners, span, index_args, tile_weights):
    sources, targets, count, labels = index_args
    _, capacity, rows, _ = tile_weights.shape
    places = owners * own_tiles
    row = lax.axis_index("row").astype(jnp.int32).reshape(1)
    column = lax.axis_index("col").astype(jnp.int32).reshape(1)
    return pl.pallas_call(
        functools.partial(merge_kernel, own_tiles, labels.shape[1] // owners),
        out_shape=jax.ShapeDtypeStruct((places * rows, span * rows), jnp.bfloat16),
        in_specs=[SMEM] * 3 + [VMEM] * 3 + [HBM],
        out_specs=VMEM,
        scratch_shapes=[
            pltpu.VMEM((places * span + 1, rows, rows), jnp.float32),
            pltpu.VMEM(tile_weights.shape[1:], tile_weights.dtype),
            pltpu.SMEM(sources.shape, jnp.int32),
            pltpu.SMEM(targets.shape, jnp.int32),
            pltpu.SMEM(labels.shape, jnp.int32),
            pltpu.SMEM((labels.shape[1],), jnp.int32),
            pltpu.SMEM((places * span + 1,), jnp.int32),
            pltpu.SemaphoreType.DMA((3,)),
            pltpu.SemaphoreType.DMA((4 if capacity % 4 == 0 else 1,)),
        ],
        compiler_params=params(24),
        cost_estimate=cost(8 * MIB, 12 * MIB),
    )(row, column, count, sources, targets, labels, *in_hbm(tile_weights))


def early_kernel(matrix, own, beside, across, out):
    rows = own.shape[0]
    value = jnp.dot(matrix[:, :rows], own[...], preferred_element_type=jnp.float32)
    value += jnp.dot(
        matrix[:, rows : 2 * rows], beside[...], preferred_element_type=jnp.float32
    )
    value += jnp.dot(matrix[:, 3 * rows :], across[...], preferred_element_type=jnp.float32)
    out[...] = value


def early_product(matrix, own, beside, across):
    total, depth = matrix.shape
    width = own.shape[1]
    return pl.pallas_call(
        early_kernel,
        out_shape=jax.ShapeDtypeStruct((total, width), jnp.float32),
        in_specs=[VMEM] * 4,
        out_specs=VMEM,
        compiler_params=params(16),
        cost_estimate=cost(total * depth * width, 1),
    )(matrix, own, beside, across)


def late_kernel(first, matrix, early, passed, out):
    rows = passed.shape[0]
    here = slice(first, first + out.shape[0])
    value = early[here, :] + jnp.dot(
        matrix[here, 2 * rows : 3 * rows], passed[...], preferred_element_type=jnp.float32
    )
    out[...] = value.astype(out.dtype)


def late_product(matrix, early, passed, first, count, dtype, weight):
    total, depth = matrix.shape
    width = passed.shape[1]
    return pl.pallas_call(
        functools.partial(late_kernel, first),
        out_shape=jax.ShapeDtypeStruct((count, width), dtype),
        in_specs=[VMEM] * 3,
        out_specs=VMEM,
        compiler_params=params(16),
        cost_estimate=cost(weight * total * depth * width, 1),
    )(matrix, early, passed)


def product_kernel(first, matrix, *refs):
    *blocks, out, gathered = refs
    rows = blocks[0].shape[0]
    for k, block in enumerate(blocks):
        gathered[k * rows : (k + 1) * rows, :] = block[...]
    value = jnp.dot(
        matrix[first : first + out.shape[0], :],
        gathered[...],
        preferred_element_type=jnp.float32,
    )
    out[...] = value.astype(out.dtype)


def product(matrix, blocks, first, count, dtype, weight):
    rows, width = blocks[0].shape
    total, depth = matrix.shape
    return pl.pallas_call(
        functools.partial(product_kernel, first),
        out_shape=jax.ShapeDtypeStruct((count, width), dtype),
        in_specs=[VMEM] * (1 + len(blocks)),
        out_specs=VMEM,
        scratch_shapes=[pltpu.VMEM((depth, width), blocks[0].dtype)],
        compiler_params=params(16),
        cost_estimate=cost(weight * total * depth * width, 1),
    )(matrix, *blocks)


def join_kernel(first, stay, came, *outs):
    start = 0
    for out in outs:
        rows = out.shape[0]
        value = stay[first + start : first + start + rows, :]
        out[...] = (value + came[start : start + rows, :].astype(jnp.float32)).astype(out.dtype)
        start += rows


def join(stay, came, first, rows, dtypes):
    width = stay.shape[1]
    return pl.pallas_call(
        functools.partial(join_kernel, first),
        out_shape=[jax.ShapeDtypeStruct((rows, width), dtype) for dtype in dtypes],
        in_specs=[VMEM] * 2,
        out_specs=[VMEM] * len(dtypes),
        compiler_params=params(12),
        cost_estimate=cost(1, 1),
    )(stay, came)


def activate(projected, norm, pieces, out):
    lanes = norm.shape[1]
    for part in range(norm.shape[0]):
        factor = rows_to_lanes(norm[part : part + 1, :], lanes)
        here = slice(part * lanes, (part + 1) * lanes)
        for column in range(0, out.shape[1], lanes):
            span = slice(column, column + lanes)
            value = projected[here, span]
            for piece in pieces:
                value += piece[here, span].astype(jnp.float32)
            out[here, span] = jnp.maximum(factor * value, 0.0).astype(out.dtype)


def first_kernel(projected, norm, *refs):
    *pieces, out = refs
    activate(projected, norm, pieces, out)


def last_kernel(ready, projected, norm, *refs):
    *pieces, out, rest, sems = refs
    width = ready.shape[1]
    early = pltpu.make_async_copy(ready, out.at[:, :width], sems.at[0])
    early.start()
    activate(projected, norm, pieces, rest)
    late = pltpu.make_async_copy(rest, out.at[:, width:], sems.at[1])
    late.start()
    early.wait()
    late.wait()


def finish(projected, target_norm, pieces):
    norm = target_norm.reshape(-1, 128)
    rows, width = projected[0].shape
    rest = projected[1].shape[1]
    ready = pl.pallas_call(
        first_kernel,
        out_shape=jax.ShapeDtypeStruct((rows, width), jnp.bfloat16),
        in_specs=[VMEM] * (2 + len(pieces[0])),
        out_specs=VMEM,
        compiler_params=params(12),
        cost_estimate=cost(6 * rows * width, 16 * rows * width),
    )(projected[0], norm, *pieces[0])
    return pl.pallas_call(
        last_kernel,
        out_shape=jax.ShapeDtypeStruct((rows, width + rest), jnp.bfloat16),
        in_specs=[VMEM] * (3 + len(pieces[1])),
        out_specs=HBM,
        scratch_shapes=[
            pltpu.VMEM((rows, rest), jnp.bfloat16),
            pltpu.SemaphoreType.DMA((2,)),
        ],
        compiler_params=params(12),
        cost_estimate=cost(6 * rows * rest, 16 * rows * rest),
    )(ready, projected[1], norm, *pieces[1])


def visit_kernel(own_tiles, per_owner, sources, targets, count, labels, tiles, blocks, out, total):
    spare, rows = total.shape[0] - 1, total.shape[1]
    total[...] = jnp.zeros_like(total)

    @pl.loop(0, count[0])
    def _(slot):
        target = targets[0, slot]
        label = labels[0, target]
        place = jnp.where(label < own_tiles, target // per_owner * own_tiles + label, spare)
        start = pl.multiple_of(sources[0, slot] * rows, rows)
        total[place] += jnp.dot(
            tiles[0, slot], blocks[pl.ds(start, rows), :], preferred_element_type=jnp.float32
        )

    @pl.loop(0, spare)
    def _(place):
        out[pl.ds(pl.multiple_of(place * rows, rows), rows), :] = total[place].astype(out.dtype)


def visit_tiles(own_tiles, owners, index_args, tile_weights, blocks):
    slots = index_args[-1].shape[1]
    rows = tile_weights.shape[-1]
    places = owners * own_tiles
    hidden = blocks.shape[1]
    return pl.pallas_call(
        functools.partial(visit_kernel, own_tiles, slots // owners),
        out_shape=jax.ShapeDtypeStruct((places * rows, hidden), jnp.bfloat16),
        in_specs=[SMEM] * 4 + [VMEM] * 2,
        out_specs=VMEM,
        scratch_shapes=[pltpu.VMEM((places + 1, rows, hidden), jnp.float32)],
        compiler_params=params(56),
    )(*index_args, tile_weights, blocks)


def swap(value, axis, apart):
    pairs = [(i, i ^ apart) for i in range(lax.axis_size(axis))]
    return lax.ppermute(value, axis, pairs)


def exchange(sent):
    owners = lax.axis_size("row")
    steps = [(2, 4), (4, 2), (6, 6)]
    return [
        lax.ppermute(value, "row", [(i, i ^ step[i % 2]) for i in range(owners)])
        for value, step in zip(sent, steps)
    ]


def per_device(
    features,
    weight,
    source_norm,
    target_norm,
    tile_weights,
    tile_source,
    tile_target,
    tile_count,
    mirror_tile,
):
    tile_rows = tile_weights.shape[-1]
    own_rows = features.shape[0]
    own_tiles = own_rows // tile_rows
    owners, columns = lax.axis_size("row"), lax.axis_size("col")
    span = own_tiles * columns
    index_args = (tile_source, tile_target, tile_count, mirror_tile)

    cells = owners * own_tiles * span * tile_rows * tile_rows
    if columns != 4 or owners != 8 or own_tiles & (own_tiles - 1) or cells > DENSE_ELEMENTS:
        projected = jnp.dot(features, weight, preferred_element_type=jnp.float32)
        scaled = (source_norm[:, None] * projected).astype(jnp.bfloat16)
        blocks = lax.all_gather(scaled, "col", axis=0, tiled=True)
        partial_value = visit_tiles(own_tiles, owners, index_args, tile_weights, blocks)
        outgoing = partial_value.reshape(owners, own_rows, -1)
        arrived = lax.all_to_all(outgoing, "row", split_axis=0, concat_axis=0, tiled=True)
        gathered = jnp.sum(arrived.astype(jnp.float32), axis=0) + projected
        return jnp.maximum(target_norm[:, None] * gathered, 0.0).astype(jnp.bfloat16)

    width = weight.shape[1] // CHUNKS
    first = project(features, weight, source_norm, 0, width)
    second = project(
        features, weight, source_norm, width, width, tile_source, tile_target, mirror_tile
    )
    projected, scaled = zip(first, second[:2])
    sources, targets, labels = second[2:]
    index_args = sources, targets, tile_count, labels
    built = merge_tiles(own_tiles, owners, span, index_args, tile_weights)
    half = built.shape[0] // 2
    across = [swap(own, "col", 3) for own in scaled]
    beside = [swap(own, "col", 1) for own in scaled]
    onward, matrix = lax.optimization_barrier((across[0], built))
    passed = swap(onward, "col", 1)
    early = early_product(matrix, scaled[0], beside[0], across[0])
    away = [late_product(matrix, early, passed, 0, own_rows, jnp.bfloat16, WEIGHTS[0])]
    after, _ = lax.optimization_barrier((passed, away[0]))
    away.append(
        late_product(
            matrix, early, after, own_rows, half - own_rows, jnp.bfloat16, WEIGHTS[0]
        )
    )
    stay = late_product(matrix, early, passed, half, half, jnp.float32, WEIGHTS[1])
    came = [swap(value, "row", 1) for value in away]
    (lead,) = join(stay, came[0], 0, own_rows, [jnp.bfloat16])
    kept, *sent = join(stay, came[1], own_rows, own_rows, [jnp.float32] + [jnp.bfloat16] * 2)
    pieces = [[kept] + exchange([lead] + sent)]

    onward, _ = lax.optimization_barrier((across[1], early))
    blocks = scaled[1], beside[1], swap(onward, "col", 1), across[1]
    blocks, _ = lax.optimization_barrier((blocks, sent))
    away = product(matrix, blocks, 0, half, jnp.bfloat16, WEIGHTS[2])
    stay = product(matrix, blocks, half, half, jnp.float32, WEIGHTS[3])
    came = swap(away, "row", 1)
    lead, kept, *sent = join(
        stay, came, 0, own_rows, [jnp.bfloat16, jnp.float32] + [jnp.bfloat16] * 2
    )
    pieces.append([kept] + exchange([lead] + sent))
    return finish(projected, target_norm, pieces)


def solution(mesh):
    in_specs = (
        P(("row", "col"), None),
        P(),
        P(("row", "col")),
        P(("row", "col")),
        P(("row", "col"), None, None, None),
        P(("row", "col"), None),
        P(("row", "col"), None),
        P(("row", "col")),
        P(("row", "col"), None),
    )
    out_specs = P(("row", "col"), None)
    return jax.shard_map(
        per_device, mesh=mesh, in_specs=in_specs, out_specs=out_specs, check_vma=False
    )
```

```python
import functools

import jax
import jax.numpy as jnp
from jax import lax
from jax.experimental import pallas as pl
from jax.experimental.pallas import tpu as pltpu
from jax.sharding import PartitionSpec as P

DENSE_ELEMENTS = 4 * 1024 * 1024
CHUNKS = 2
WEIGHTS = (20, 20, 0, 20)
MIB = 1024 * 1024
SMEM = pl.BlockSpec(memory_space=pltpu.SMEM)
VMEM = pl.BlockSpec(memory_space=pltpu.VMEM)
HBM = pl.BlockSpec(memory_space=pltpu.HBM)


def params(mib):
    return pltpu.CompilerParams(vmem_limit_bytes=int(mib * MIB))


def cost(flops, moved):
    return pl.CostEstimate(flops=flops, bytes_accessed=moved, transcendentals=0)


def in_hbm(*values):
    return [pltpu.with_memory_space_constraint(value, pltpu.HBM) for value in values]


def rows_to_lanes(row, lanes):
    return jnp.broadcast_to(row, (lanes, row.shape[1])).T


def project_kernel(start, extra, features_hbm, weight_hbm, norm_hbm, *refs):
    extra_hbm, (projected, scaled), refs = refs[:extra], refs[extra : extra + 2], refs[extra + 2 :]
    staged, (features, weight, norm, sems) = refs[:extra], refs[extra:]
    width, lanes = scaled.shape[1], norm.shape[1]
    copies = [
        pltpu.make_async_copy(source, target, sems.at[k])
        for k, (source, target) in enumerate(
            [
                (weight_hbm.at[:, start : start + width], weight),
                (features_hbm, features),
                (norm_hbm, norm),
                *zip(extra_hbm, staged),
            ]
        )
    ]
    for copy in copies:
        copy.start()
    for copy in copies:
        copy.wait()
    value = jnp.dot(features[...], weight[...], preferred_element_type=jnp.float32)
    projected[...] = value
    for part in range(norm.shape[0]):
        factor = rows_to_lanes(norm[part : part + 1, :], lanes)
        here = slice(part * lanes, (part + 1) * lanes)
        for column in range(0, width, lanes):
            piece = factor * value[here, column : column + lanes]
            scaled[here, column : column + lanes] = piece.astype(scaled.dtype)


def project(features, weight, source_norm, start, width, *extra):
    rows, depth = features.shape
    norm = source_norm.reshape(-1, 128)
    return pl.pallas_call(
        functools.partial(project_kernel, start, len(extra)),
        out_shape=[
            jax.ShapeDtypeStruct((rows, width), jnp.float32),
            jax.ShapeDtypeStruct((rows, width), jnp.bfloat16),
        ]
        + [jax.ShapeDtypeStruct(value.shape, value.dtype) for value in extra],
        in_specs=[HBM] * (3 + len(extra)),
        out_specs=[VMEM] * (2 + len(extra)),
        scratch_shapes=[
            pltpu.VMEM(features.shape, features.dtype),
            pltpu.VMEM((depth, width), weight.dtype),
            pltpu.VMEM(norm.shape, norm.dtype),
            pltpu.SemaphoreType.DMA((3 + len(extra),)),
        ],
        compiler_params=params(12),
        cost_estimate=cost(2 * rows * depth * width, 2 * depth * (rows + width)),
    )(*in_hbm(features, weight, norm, *extra))


def merge_kernel(
    own_tiles, per_owner, row, column, count, sources_in, targets_in, labels_in, tiles_hbm, out,
    total, tiles, sources, targets, labels, bases, seen, sems, tile_sems,
):
    small = [
        pltpu.make_async_copy(source, target, sems.at[k])
        for k, (source, target) in enumerate(
            [(sources_in, sources), (targets_in, targets), (labels_in, labels)]
        )
    ]
    parts = tile_sems.shape[0]
    each = tiles.shape[0] // parts
    large = [
        pltpu.make_async_copy(
            tiles_hbm.at[0, pl.ds(k * each, each)],
            tiles.at[pl.ds(k * each, each)],
            tile_sems.at[k],
        )
        for k in range(parts)
    ]
    for copy in small + large:
        copy.start()
    rows = total.shape[1]
    places, span = out.shape[0] // rows, out.shape[1] // rows
    spare = places * span
    for cell in range(spare + 1):
        seen[cell] = 0
    my_core, used = row[0] % 2, count[0]
    toggle = column[0] * own_tiles
    for copy in small:
        copy.wait()

    for slot in range(bases.shape[0]):
        owner, label = slot // per_owner, labels[0, slot]
        core, apart = owner % 2, lax.bitwise_xor(row[0], owner)
        x, y = lax.bitwise_and(apart, 2), lax.bitwise_and(lax.shift_right_logical(apart, 1), 2)
        first, second = (x, y) if core == 0 else (y, x)
        position = jnp.where(my_core == core, 4, 0) + second
        position += lax.shift_right_logical(jnp.where(second == 0, 2 - first, first), 1)
        base = (position * own_tiles + label) * span
        bases[slot] = jnp.where(label < own_tiles, base, spare)

    def add(slot):
        base = bases[targets[0, slot]]
        here = base + lax.bitwise_xor(sources[0, slot], toggle)
        cell = jnp.where((base < spare) & (slot < used), here, spare)
        before = jnp.where(seen[cell] > 0, total[cell], 0.0)
        seen[cell] = 1
        total[cell] = before + tiles[slot].astype(jnp.float32)

    for k, copy in enumerate(large):
        copy.wait()
        pl.loop(k * each, (k + 1) * each, unroll=min(each, 16))(add)

    for place in range(places):
        for source in range(span):
            cell = place * span + source
            value = jnp.where(seen[cell] > 0, total[cell], 0.0)
            out[place * rows : (place + 1) * rows, source * rows : (source + 1) * rows] = (
                value.astype(out.dtype)
            )


def merge_tiles(own_tiles, owners, span, index_args, tile_weights):
    sources, targets, count, labels = index_args
    _, capacity, rows, _ = tile_weights.shape
    places = owners * own_tiles
    row = lax.axis_index("row").astype(jnp.int32).reshape(1)
    column = lax.axis_index("col").astype(jnp.int32).reshape(1)
    return pl.pallas_call(
        functools.partial(merge_kernel, own_tiles, labels.shape[1] // owners),
        out_shape=jax.ShapeDtypeStruct((places * rows, span * rows), jnp.bfloat16),
        in_specs=[SMEM] * 3 + [VMEM] * 3 + [HBM],
        out_specs=VMEM,
        scratch_shapes=[
            pltpu.VMEM((places * span + 1, rows, rows), jnp.float32),
            pltpu.VMEM(tile_weights.shape[1:], tile_weights.dtype),
            pltpu.SMEM(sources.shape, jnp.int32),
            pltpu.SMEM(targets.shape, jnp.int32),
            pltpu.SMEM(labels.shape, jnp.int32),
            pltpu.SMEM((labels.shape[1],), jnp.int32),
            pltpu.SMEM((places * span + 1,), jnp.int32),
            pltpu.SemaphoreType.DMA((3,)),
            pltpu.SemaphoreType.DMA((4 if capacity % 4 == 0 else 1,)),
        ],
        compiler_params=params(24),
        cost_estimate=cost(8 * MIB, 12 * MIB),
    )(row, column, count, sources, targets, labels, *in_hbm(tile_weights))


def early_kernel(matrix, own, beside, across, out):
    rows = own.shape[0]
    value = jnp.dot(matrix[:, :rows], own[...], preferred_element_type=jnp.float32)
    value += jnp.dot(
        matrix[:, rows : 2 * rows], beside[...], preferred_element_type=jnp.float32
    )
    value += jnp.dot(matrix[:, 3 * rows :], across[...], preferred_element_type=jnp.float32)
    out[...] = value


def early_product(matrix, own, beside, across):
    total, depth = matrix.shape
    width = own.shape[1]
    return pl.pallas_call(
        early_kernel,
        out_shape=jax.ShapeDtypeStruct((total, width), jnp.float32),
        in_specs=[VMEM] * 4,
        out_specs=VMEM,
        compiler_params=params(16),
        cost_estimate=cost(total * depth * width, 1),
    )(matrix, own, beside, across)


def late_kernel(first, matrix, early, passed, out):
    rows = passed.shape[0]
    here = slice(first, first + out.shape[0])
    value = early[here, :] + jnp.dot(
        matrix[here, 2 * rows : 3 * rows], passed[...], preferred_element_type=jnp.float32
    )
    out[...] = value.astype(out.dtype)


def late_product(matrix, early, passed, first, count, dtype, weight):
    total, depth = matrix.shape
    width = passed.shape[1]
    return pl.pallas_call(
        functools.partial(late_kernel, first),
        out_shape=jax.ShapeDtypeStruct((count, width), dtype),
        in_specs=[VMEM] * 3,
        out_specs=VMEM,
        compiler_params=params(16),
        cost_estimate=cost(weight * total * depth * width, 1),
    )(matrix, early, passed)


def product_kernel(first, matrix, *refs):
    *blocks, out, gathered = refs
    rows = blocks[0].shape[0]
    for k, block in enumerate(blocks):
        gathered[k * rows : (k + 1) * rows, :] = block[...]
    value = jnp.dot(
        matrix[first : first + out.shape[0], :],
        gathered[...],
        preferred_element_type=jnp.float32,
    )
    out[...] = value.astype(out.dtype)


def product(matrix, blocks, first, count, dtype, weight):
    rows, width = blocks[0].shape
    total, depth = matrix.shape
    return pl.pallas_call(
        functools.partial(product_kernel, first),
        out_shape=jax.ShapeDtypeStruct((count, width), dtype),
        in_specs=[VMEM] * (1 + len(blocks)),
        out_specs=VMEM,
        scratch_shapes=[pltpu.VMEM((depth, width), blocks[0].dtype)],
        compiler_params=params(16),
        cost_estimate=cost(weight * total * depth * width, 1),
    )(matrix, *blocks)


def join_kernel(first, stay, came, *outs):
    start = 0
    for out in outs:
        rows = out.shape[0]
        value = stay[first + start : first + start + rows, :]
        out[...] = (value + came[start : start + rows, :].astype(jnp.float32)).astype(out.dtype)
        start += rows


def join(stay, came, first, rows, dtypes):
    width = stay.shape[1]
    return pl.pallas_call(
        functools.partial(join_kernel, first),
        out_shape=[jax.ShapeDtypeStruct((rows, width), dtype) for dtype in dtypes],
        in_specs=[VMEM] * 2,
        out_specs=[VMEM] * len(dtypes),
        compiler_params=params(12),
        cost_estimate=cost(1, 1),
    )(stay, came)


def activate(projected, norm, pieces, out):
    lanes = norm.shape[1]
    for part in range(norm.shape[0]):
        factor = rows_to_lanes(norm[part : part + 1, :], lanes)
        here = slice(part * lanes, (part + 1) * lanes)
        for column in range(0, out.shape[1], lanes):
            span = slice(column, column + lanes)
            value = projected[here, span]
            for piece in pieces:
                value += piece[here, span].astype(jnp.float32)
            out[here, span] = jnp.maximum(factor * value, 0.0).astype(out.dtype)


def first_kernel(projected, norm, *refs):
    *pieces, out = refs
    activate(projected, norm, pieces, out)


def last_kernel(ready, projected, norm, *refs):
    *pieces, out, rest, sems = refs
    width = ready.shape[1]
    early = pltpu.make_async_copy(ready, out.at[:, :width], sems.at[0])
    early.start()
    activate(projected, norm, pieces, rest)
    late = pltpu.make_async_copy(rest, out.at[:, width:], sems.at[1])
    late.start()
    early.wait()
    late.wait()


def finish(projected, target_norm, pieces):
    norm = target_norm.reshape(-1, 128)
    rows, width = projected[0].shape
    rest = projected[1].shape[1]
    ready = pl.pallas_call(
        first_kernel,
        out_shape=jax.ShapeDtypeStruct((rows, width), jnp.bfloat16),
        in_specs=[VMEM] * (2 + len(pieces[0])),
        out_specs=VMEM,
        compiler_params=params(12),
        cost_estimate=cost(6 * rows * width, 16 * rows * width),
    )(projected[0], norm, *pieces[0])
    return pl.pallas_call(
        last_kernel,
        out_shape=jax.ShapeDtypeStruct((rows, width + rest), jnp.bfloat16),
        in_specs=[VMEM] * (3 + len(pieces[1])),
        out_specs=HBM,
        scratch_shapes=[
            pltpu.VMEM((rows, rest), jnp.bfloat16),
            pltpu.SemaphoreType.DMA((2,)),
        ],
        compiler_params=params(12),
        cost_estimate=cost(6 * rows * rest, 16 * rows * rest),
    )(ready, projected[1], norm, *pieces[1])


def visit_kernel(own_tiles, per_owner, sources, targets, count, labels, tiles, blocks, out, total):
    spare, rows = total.shape[0] - 1, total.shape[1]
    total[...] = jnp.zeros_like(total)

    @pl.loop(0, count[0])
    def _(slot):
        target = targets[0, slot]
        label = labels[0, target]
        place = jnp.where(label < own_tiles, target // per_owner * own_tiles + label, spare)
        start = pl.multiple_of(sources[0, slot] * rows, rows)
        total[place] += jnp.dot(
            tiles[0, slot], blocks[pl.ds(start, rows), :], preferred_element_type=jnp.float32
        )

    @pl.loop(0, spare)
    def _(place):
        out[pl.ds(pl.multiple_of(place * rows, rows), rows), :] = total[place].astype(out.dtype)


def visit_tiles(own_tiles, owners, index_args, tile_weights, blocks):
    slots = index_args[-1].shape[1]
    rows = tile_weights.shape[-1]
    places = owners * own_tiles
    hidden = blocks.shape[1]
    return pl.pallas_call(
        functools.partial(visit_kernel, own_tiles, slots // owners),
        out_shape=jax.ShapeDtypeStruct((places * rows, hidden), jnp.bfloat16),
        in_specs=[SMEM] * 4 + [VMEM] * 2,
        out_specs=VMEM,
        scratch_shapes=[pltpu.VMEM((places + 1, rows, hidden), jnp.float32)],
        compiler_params=params(56),
    )(*index_args, tile_weights, blocks)


def swap(value, axis, apart):
    pairs = [(i, i ^ apart) for i in range(lax.axis_size(axis))]
    return lax.ppermute(value, axis, pairs)


def exchange(sent):
    owners = lax.axis_size("row")
    steps = [(2, 4), (4, 2), (6, 6)]
    return [
        lax.ppermute(value, "row", [(i, i ^ step[i % 2]) for i in range(owners)])
        for value, step in zip(sent, steps)
    ]


def per_device(
    features,
    weight,
    source_norm,
    target_norm,
    tile_weights,
    tile_source,
    tile_target,
    tile_count,
    mirror_tile,
):
    tile_rows = tile_weights.shape[-1]
    own_rows = features.shape[0]
    own_tiles = own_rows // tile_rows
    owners, columns = lax.axis_size("row"), lax.axis_size("col")
    span = own_tiles * columns
    index_args = (tile_source, tile_target, tile_count, mirror_tile)

    cells = owners * own_tiles * span * tile_rows * tile_rows
    if columns != 4 or owners != 8 or own_tiles & (own_tiles - 1) or cells > DENSE_ELEMENTS:
        projected = jnp.dot(features, weight, preferred_element_type=jnp.float32)
        scaled = (source_norm[:, None] * projected).astype(jnp.bfloat16)
        blocks = lax.all_gather(scaled, "col", axis=0, tiled=True)
        partial_value = visit_tiles(own_tiles, owners, index_args, tile_weights, blocks)
        outgoing = partial_value.reshape(owners, own_rows, -1)
        arrived = lax.all_to_all(outgoing, "row", split_axis=0, concat_axis=0, tiled=True)
        gathered = jnp.sum(arrived.astype(jnp.float32), axis=0) + projected
        return jnp.maximum(target_norm[:, None] * gathered, 0.0).astype(jnp.bfloat16)

    width = weight.shape[1] // CHUNKS
    first = project(features, weight, source_norm, 0, width)
    second = project(
        features, weight, source_norm, width, width, tile_source, tile_target, mirror_tile
    )
    projected, scaled = zip(first, second[:2])
    sources, targets, labels = second[2:]
    index_args = sources, targets, tile_count, labels
    built = merge_tiles(own_tiles, owners, span, index_args, tile_weights)
    half = built.shape[0] // 2
    across = [swap(own, "col", 3) for own in scaled]
    beside = [swap(own, "col", 1) for own in scaled]
    onward, matrix = lax.optimization_barrier((across[0], built))
    passed = swap(onward, "col", 1)
    early = early_product(matrix, scaled[0], beside[0], across[0])
    away = [late_product(matrix, early, passed, 0, own_rows, jnp.bfloat16, WEIGHTS[0])]
    after, _ = lax.optimization_barrier((passed, away[0]))
    away.append(
        late_product(
            matrix, early, after, own_rows, half - own_rows, jnp.bfloat16, WEIGHTS[0]
        )
    )
    stay = late_product(matrix, early, passed, half, half, jnp.float32, WEIGHTS[1])
    came = [swap(value, "row", 1) for value in away]
    (lead,) = join(stay, came[0], 0, own_rows, [jnp.bfloat16])
    kept, *sent = join(stay, came[1], own_rows, own_rows, [jnp.float32] + [jnp.bfloat16] * 2)
    pieces = [[kept] + exchange([lead] + sent)]

    onward, _ = lax.optimization_barrier((across[1], early))
    blocks = scaled[1], beside[1], swap(onward, "col", 1), across[1]
    blocks, _ = lax.optimization_barrier((blocks, sent))
    away = product(matrix, blocks, 0, half, jnp.bfloat16, WEIGHTS[2])
    stay = product(matrix, blocks, half, half, jnp.float32, WEIGHTS[3])
    came = swap(away, "row", 1)
    lead, kept, *sent = join(
        stay, came, 0, own_rows, [jnp.bfloat16, jnp.float32] + [jnp.bfloat16] * 2
    )
    pieces.append([kept] + exchange([lead] + sent))
    return finish(projected, target_norm, pieces)


def solution(mesh):
    in_specs = (
        P(("row", "col"), None),
        P(),
        P(("row", "col")),
        P(("row", "col")),
        P(("row", "col"), None, None, None),
        P(("row", "col"), None),
        P(("row", "col"), None),
        P(("row", "col")),
        P(("row", "col"), None),
    )
    out_specs = P(("row", "col"), None)
    return jax.shard_map(
        per_device, mesh=mesh, in_specs=in_specs, out_specs=out_specs, check_vma=False
    )
```
